32 devices in a mesh: dp: 4 (over x, core), fsdp: 8 (over z, y).
Axes of the slice: x: 2, y: 2, z: 4, core: 2. Of those that a mesh axis runs over, the one named last changes fastest.
Arguments:
- tokens: bfloat16 [64, 512, 768], P(('dp', 'fsdp')), may hold values from -6 to 6
- cotangent: bfloat16 [64, 512, 768], P(('dp', 'fsdp')), may hold values from -6 to 6
- segment_ids: int32 [64, 512], P(('dp', 'fsdp')), may hold values from 0 to 3, as said below
- pad_mask: int32 [64, 512], P(('dp', 'fsdp')), may hold values from 0 to 1, as said below
- row_counts: int32 [32], P(('dp', 'fsdp')), may hold values from 1 to 2, as said below
- query_weight: bfloat16 [768, 768], P(('dp', 'fsdp')), may hold values from -0.21875 to 0.21875
- query_bias: bfloat16 [768], P(('dp', 'fsdp')), may hold values from -3 to 3
- key_weight: bfloat16 [768, 768], P(('dp', 'fsdp')), may hold values from -0.21875 to 0.21875
- value_weight: bfloat16 [768, 768], P(('dp', 'fsdp')), may hold values from -0.21875 to 0.21875
- value_bias: bfloat16 [768], P(('dp', 'fsdp')), may hold values from -3 to 3
- out_weight: bfloat16 [768, 768], P(('dp', 'fsdp')), may hold values from -1.75 to 1.75
- out_bias: bfloat16 [768], P(('dp', 'fsdp')), may hold values from -3 to 3
- first_gain: bfloat16 [768], P(('dp', 'fsdp')), may hold values from 0.25 to 1.75
- first_shift: bfloat16 [768], P(('dp', 'fsdp')), may hold values from -3 to 3
- up_weight: bfloat16 [3072, 768], P(('dp', 'fsdp')), may hold values from -0.21875 to 0.21875
- up_bias: bfloat16 [3072], P(('dp', 'fsdp')), may hold values from -3 to 3
- down_weight: bfloat16 [768, 3072], P(('dp', 'fsdp')), may hold values from -0.109375 to 0.109375
- down_bias: bfloat16 [768], P(('dp', 'fsdp')), may hold values from -3 to 3
- second_gain: bfloat16 [768], P(('dp', 'fsdp')), may hold values from 0.25 to 1.75
- second_shift: bfloat16 [768], P(('dp', 'fsdp')), may hold values from -3 to 3
Outputs:
- outputs: bfloat16 [64, 512, 768], P(('dp', 'fsdp'))
- tokens_grad: float32 [64, 512, 768], P(('dp', 'fsdp'))
- query_weight_grad: float32 [768, 768], P(('dp', 'fsdp'))
- query_bias_grad: float32 [768], P(('dp', 'fsdp'))
- key_weight_grad: float32 [768, 768], P(('dp', 'fsdp'))
- value_weight_grad: float32 [768, 768], P(('dp', 'fsdp'))
- value_bias_grad: float32 [768], P(('dp', 'fsdp'))
- out_weight_grad: float32 [768, 768], P(('dp', 'fsdp'))
- out_bias_grad: float32 [768], P(('dp', 'fsdp'))
- first_gain_grad: float32 [768], P(('dp', 'fsdp'))
- first_shift_grad: float32 [768], P(('dp', 'fsdp'))
- up_weight_grad: float32 [3072, 768], P(('dp', 'fsdp'))
- up_bias_grad: float32 [3072], P(('dp', 'fsdp'))
- down_weight_grad: float32 [768, 3072], P(('dp', 'fsdp'))
- down_bias_grad: float32 [768], P(('dp', 'fsdp'))
- second_gain_grad: float32 [768], P(('dp', 'fsdp'))
- second_shift_grad: float32 [768], P(('dp', 'fsdp'))
The draws below stay inside these ranges and needn't reach their ends.
Inputs may be any that keep to these rules, and one draw needn't show every extreme that they name: `segment_ids`: each row holds one bucket: segment number = position // length with length 512, 256 or 128 for the whole row. `pad_mask`: within every sequence of segment_ids, the ones form a leading run of at least half its length. A device uses its first row_counts row slots; some device uses all 2.
All inputs are finite; a program needn't handle non-finite values.
Results may differ from the reference program's by a relative error of at most 0.024.
Values may be sent and summed in bfloat16 or wider, within the bound.
No kernel may reach another device: no remote copies, remote signals or barrier semaphores. Data moves between devices by JAX's collectives and lax.ppermute only.
A program may use at most 192 MiB of HBM per device.

```python
import math
import jax
import jax.numpy as jnp
from jax import lax

D = 768
HEADS = 12
HEAD = 64
FF = 3072
ROW_LEN = 512
CAP = 2
LAYERS = 2
SHARDS = 32
ROWS = 64


def row_lengths(key):
    bucket = jax.random.randint(key, (ROWS, 1), 0, 3)
    return jnp.where(bucket == 0, ROW_LEN, jnp.where(bucket == 1, ROW_LEN // 2, ROW_LEN // 4)).astype(jnp.int32)


def draw_segment_ids(key, part):
    lengths = row_lengths(key)
    position = jnp.arange(ROW_LEN, dtype=jnp.int32)[None, :]
    return (position // lengths).astype(jnp.int32)


def draw_pad_mask(key, part):
    lengths = row_lengths(key)
    key = jax.random.fold_in(key, 5)
    position = jnp.arange(ROW_LEN, dtype=jnp.int32)[None, :]
    sequence = (position // lengths).astype(jnp.int32)
    lowest = (lengths + 1) // 2
    spans = lengths - lowest + 1
    raw_draw = jax.random.randint(key, (ROWS, 4), 0, 65536)
    picked = jnp.take_along_axis(raw_draw, sequence, axis=1)
    live_len = lowest + picked % spans
    return (position % lengths < live_len).astype(jnp.int32)


def draw_row_counts(key, part):
    key = jax.random.fold_in(key, 7)
    first, second = jax.random.split(key)
    counts = jax.random.randint(first, (SHARDS,), 1, CAP + 1)
    fullest = jax.random.randint(second, (), 0, SHARDS)
    return jnp.where(jnp.arange(SHARDS) == fullest, CAP, counts).astype(jnp.int32)


def with_spikes(values, key, source, target, shards_of, factor):
    def block_of(dim):
        return (jnp.arange(values.shape[dim]) // (values.shape[dim] // shards_of)).reshape((-1,) + (1,) * (values.ndim - 1 - dim))

    first = jax.random.permutation(key, shards_of)[block_of(target)]
    second = (block_of(target) + shards_of // 2) % shards_of
    return jnp.where((block_of(source) == first) | (block_of(source) == second), factor * values, values)


def steps_of(stream_key, extent, shards, least, top_value):
    gain = 1.0
    for dim, shards_of in shards:
        heights = jax.random.uniform(jax.random.fold_in(jax.random.fold_in(stream_key, 6), dim), (shards_of,), jnp.float32, least / len(shards), top_value / len(shards))
        gain = gain * jnp.repeat(jnp.exp(heights), extent[dim] // shards_of).reshape((-1,) + (1,) * (len(extent) - 1 - dim))
    return gain


def noise(key, dims, spread, bound, cuts=(), held_as=jnp.bfloat16):
    entries = jax.random.normal(key, dims, jnp.float32) * spread
    if len(cuts) > 0:
        entries = steps_of(key, dims, cuts, -0.22, 0.18) * entries
    return jnp.clip(entries, min=-bound, max=bound).astype(held_as)


def heavy_noise(own_key, shape, spread, limit, shards, heavy, held_as=jnp.bfloat16):
    values = spread * jax.random.normal(own_key, shape, jnp.float32)
    if shards:
        values = values * steps_of(own_key, shape, shards, -0.22, 0.18)
    return jnp.clip(with_spikes(values, jax.random.fold_in(own_key, 3), *heavy), -limit, limit).astype(held_as)


def setup_inputs(seed: int = 0) -> dict:
    key_list = jax.random.split(jax.random.key(seed), 21)
    tokens = noise(key_list[0], (ROWS, ROW_LEN, D), 1.0, 6.0, ((0, 32),))
    cotangent = heavy_noise(key_list[1], (ROWS, ROW_LEN, D), 1.0, 6.0, ((0, 32),), (0, 2, 32, 2.75))
    segment_ids = draw_segment_ids(jax.random.fold_in(key_list[20], 71), 0)
    pad_mask = draw_pad_mask(jax.random.fold_in(key_list[20], 71), 0)
    row_counts = draw_row_counts(jax.random.fold_in(key_list[20], 71), 0)
    query_weight = noise(key_list[5], (D, D), D ** -0.5, 0.21875, ((0, 32),))
    query_bias = noise(key_list[6], (D,), 0.5, 3.0, ((0, 32),))
    key_weight = noise(key_list[7], (D, D), D ** -0.5, 0.21875, ((0, 32),))
    value_weight = noise(key_list[8], (D, D), D ** -0.5, 0.21875, ((0, 32),))
    value_bias = noise(key_list[9], (D,), 0.5, 3.0, ((0, 32),))
    out_weight = noise(key_list[10], (D, D), (D // 64) ** -0.5, 1.75, ((0, 32),))
    out_bias = noise(key_list[11], (D,), 0.5, 3.0, ((0, 32),))
    first_gain = jnp.clip(1.0 + 0.15 * jax.random.normal(key_list[12], (D,), jnp.float32), 0.25, 1.75).astype(jnp.bfloat16)
    first_shift = noise(key_list[13], (D,), 0.5, 3.0, ((0, 32),))
    up_weight = noise(key_list[14], (FF, D), D ** -0.5, 0.21875, ((0, 32),))
    up_bias = noise(key_list[15], (FF,), 0.5, 3.0, ((0, 32),))
    down_weight = noise(key_list[16], (D, FF), FF ** -0.5, 0.109375, ((0, 32),))
    down_bias = noise(key_list[17], (D,), 0.5, 3.0, ((0, 32),))
    second_gain = jnp.clip(1.0 + 0.15 * jax.random.normal(key_list[18], (D,), jnp.float32), 0.25, 1.75).astype(jnp.bfloat16)
    second_shift = noise(key_list[19], (D,), 0.5, 3.0, ((0, 32),))
    return dict(tokens=tokens, cotangent=cotangent, segment_ids=segment_ids, pad_mask=pad_mask, row_counts=row_counts, query_weight=query_weight, query_bias=query_bias, key_weight=key_weight, value_weight=value_weight, value_bias=value_bias, out_weight=out_weight, out_bias=out_bias, first_gain=first_gain, first_shift=first_shift, up_weight=up_weight, up_bias=up_bias, down_weight=down_weight, down_bias=down_bias, second_gain=second_gain, second_shift=second_shift)


@jax.custom_vjp
def low(v):
    return lax.optimization_barrier(v.astype(jnp.bfloat16)).astype(jnp.float32)

@jax.custom_vjp
def low_back(v):
    return v

def low_keep(v):
    return (low(v), None)

def low_pass(kept, grad):
    return (grad,)

def back_keep(v):
    return (v, None)

def back_low(kept, grad):
    return (low(grad),)
low.defvjp(low_keep, low_pass)
low_back.defvjp(back_keep, back_low)
norm_eps = 1e-06
masked_score = -1000000000.0

def project(inputs, weight):
    return jnp.dot(inputs, weight.T, precision=lax.Precision.HIGHEST)

def layer_norm(inputs, norm_gain, norm_shift):
    average = lax.optimization_barrier(jnp.mean(inputs, axis=-1, keepdims=True))
    centered = inputs - average
    variance = lax.optimization_barrier(jnp.mean(centered * centered, axis=-1, keepdims=True))
    return centered * lax.rsqrt(variance + norm_eps) * norm_gain + norm_shift

def attend(blocks):
    queries, key_rows, value_rows, segments, alive = blocks
    length = segments.shape[-1]
    position = jnp.arange(length, dtype=jnp.int32)
    diagonal = position[:, None] == position[None, :]
    allowed = (segments[:, :, None] == segments[:, None, :]) & ((alive[:, None, :] > 0) | diagonal[None])
    scores = jnp.einsum('glhe,gmhe->ghlm', queries, key_rows, precision=lax.Precision.HIGHEST)
    scores = low_back(scores * HEAD ** (-0.5))
    scores = jnp.where(allowed[:, None], scores, masked_score)
    highest = lax.optimization_barrier(jnp.max(scores, axis=-1, keepdims=True))
    weights = jnp.exp(scores - highest)
    probs = low(weights / lax.optimization_barrier(jnp.sum(weights, axis=-1, keepdims=True)))
    context = jnp.einsum('ghlm,gmhe->glhe', probs, value_rows, precision=lax.Precision.HIGHEST)
    return low_back(low(context))

def application(hidden, params, segments, alive):
    query_weight, query_bias, key_weight, value_weight, value_bias, out_weight, out_bias, first_gain, first_shift, up_weight, up_bias, down_weight, down_bias, second_gain, second_shift = params
    inputs = low(hidden)
    queries = low_back(low(project(inputs, query_weight) + query_bias))
    key_rows = low_back(low(project(inputs, key_weight)))
    value_rows = low_back(low(project(inputs, value_weight) + value_bias))
    group = math.gcd(ROWS, max(1, 4096 // ROW_LEN))
    shape = (ROWS // group, group, ROW_LEN, HEADS, HEAD)
    flat_shape = (ROWS // group, group, ROW_LEN)
    context = lax.map(jax.checkpoint(attend), (queries.reshape(shape), key_rows.reshape(shape), value_rows.reshape(shape), segments.reshape(flat_shape), alive.reshape(flat_shape)))
    context = context.reshape(ROWS * ROW_LEN, D)
    attn_out = low_back(project(context, out_weight) + out_bias)
    normed = layer_norm(hidden + attn_out, first_gain, first_shift)
    upward = low_back(project(low(normed), up_weight) + up_bias)
    activated = low(jax.nn.gelu(upward, approximate=True))
    branch = low_back(project(activated, down_weight) + down_bias)
    return layer_norm(normed + branch, second_gain, second_shift)

def reference(tokens, cotangent, segment_ids, pad_mask, row_counts, query_weight, query_bias, key_weight, value_weight, value_bias, out_weight, out_bias, first_gain, first_shift, up_weight, up_bias, down_weight, down_bias, second_gain, second_shift):
    slots = jnp.arange(ROWS, dtype=jnp.int32) % CAP
    owners = jnp.repeat(row_counts, CAP)
    present = (slots < owners).astype(jnp.int32)
    alive = pad_mask * present[:, None]
    alive_flat = alive.reshape(ROWS * ROW_LEN, 1).astype(jnp.float32)
    params = tuple((weight.astype(jnp.float32) for weight in (query_weight, query_bias, key_weight, value_weight, value_bias, out_weight, out_bias, first_gain, first_shift, up_weight, up_bias, down_weight, down_bias, second_gain, second_shift)))

    def forward(hidden, weights):
        flat = hidden.reshape(ROWS * ROW_LEN, D)
        for layer in range(LAYERS):
            flat = application(flat, weights, segment_ids, alive)
        return (flat * alive_flat).reshape(ROWS, ROW_LEN, D)
    result, pullback = jax.vjp(forward, tokens.astype(jnp.float32), params)
    tokens_grad, grads = pullback(cotangent.astype(jnp.float32))
    return (result.astype(jnp.bfloat16), tokens_grad, grads[0], grads[1], grads[2], grads[3], grads[4], grads[5], grads[6], grads[7], grads[8], grads[9], grads[10], grads[11], grads[12], grads[13], grads[14])
```

```python
from functools import partial
import math

import jax
import jax.numpy as jnp
from jax import lax
from jax.experimental import pallas as pl
from jax.experimental.pallas import tpu as pltpu
from jax.sharding import PartitionSpec as P

HEAD = 64
LAYERS = 2
QUAD = 4 * HEAD
TILE = 256
norm_eps = 1e-06
masked_score = -1000000000.0
VMEM = 60 * 1024 * 1024
bf16 = jnp.bfloat16
f32 = jnp.float32

QB, VB, OB, G1, S1, DB, G2, S2 = range(8)


def dot_nt(left, right):
    return lax.dot_general(left, right, (((1,), (1,)), ((), ())), preferred_element_type=f32)


def dot_nn(left, right):
    return lax.dot_general(left, right, (((1,), (0,)), ((), ())), preferred_element_type=f32)


def normalize(v):
    mean = jnp.mean(v, axis=-1, keepdims=True)
    centered = v - mean
    rstd = lax.rsqrt(jnp.mean(centered * centered, axis=-1, keepdims=True) + norm_eps)
    return centered * rstd, rstd


def normalize_back(grad, gain, unit, rstd):
    scaled = grad * gain
    first = jnp.mean(scaled, axis=-1, keepdims=True)
    second = jnp.mean(scaled * unit, axis=-1, keepdims=True)
    return rstd * (scaled - first - unit * second)


def partial_sum(v):
    return jnp.sum(v.reshape(v.shape[0] // 8, 8, v.shape[1]), axis=0)


def piece_copies(core, pieces, place, sems, which=None):
    copies = []
    for index, piece in enumerate(pieces):
        source = piece if which is None else piece.at[which]
        _, rows, half = source.shape
        sibling, side = index // 2, index % 2
        for x in range(2):
            slot = 2 * x + (core if sibling == 0 else 1 - core)
            start = pl.multiple_of(slot * rows, rows)
            copies.append(
                pltpu.make_async_copy(
                    source.at[x],
                    place.at[pl.ds(start, rows), pl.ds(side * half, half)],
                    sems.at[index * 2 + x],
                )
            )
    return copies


def start_all(copies):
    for copy in copies:
        copy.start()


def wait_all(copies):
    for copy in copies:
        copy.wait()


def params():
    return pltpu.CompilerParams(vmem_limit_bytes=VMEM)


ANY = pl.BlockSpec(memory_space=pl.ANY)
SMEM = pl.BlockSpec(memory_space=pltpu.SMEM)


def whole(shape):
    return pl.BlockSpec(shape, lambda *_: (0,) * len(shape))


def mask_into(mask, seg_col, alive_col, seg_row):
    length = mask.shape[0]
    key = lax.broadcasted_iota(jnp.int32, (length, length), 0)
    query = lax.broadcasted_iota(jnp.int32, (length, length), 1)
    same = seg_col[:, 0:1] == seg_row[0]
    allowed = same & ((alive_col[:, 0:1] > 0) | (key == query))
    mask[...] = jnp.where(allowed, 0.0, masked_score)


def attend_forward_kernel(
    core_ref, x, seg_col, alive_col, seg_row, vecs, own_a, own_b, sib_a, sib_b,
    q_out, k_out, v_out, ctx_out, lse_out, weights, mask, sems,
):
    row, quad = pl.program_id(0), pl.program_id(1)
    core = core_ref[0]
    first = (row == 0) & (quad == 0)
    copies = [
        piece_copies(core, (own_a, own_b, sib_a, sib_b), weights.at[w], sems.at[w], w)
        for w in range(3)
    ]

    @pl.when(first)
    def _():
        for group in copies:
            start_all(group)

    @pl.when(quad == 0)
    def _():
        mask_into(mask, seg_col, alive_col, seg_row)

    @pl.when(first)
    def _():
        for group in copies:
            wait_all(group)

    inputs = x[...]
    heads = pl.ds(pl.multiple_of(quad * QUAD, QUAD), QUAD)
    queries = (dot_nt(inputs, weights[0, heads, :]) + vecs[QB : QB + 1, :]).astype(bf16)
    keys = dot_nt(inputs, weights[1, heads, :]).astype(bf16)
    values = (dot_nt(inputs, weights[2, heads, :]) + vecs[VB : VB + 1, :]).astype(bf16)
    q_out[...] = queries
    k_out[...] = keys
    v_out[...] = values
    scaled = queries * bf16(HEAD**-0.5)
    length = inputs.shape[0]
    lane = lax.broadcasted_iota(jnp.int32, (length, 2 * HEAD), 1)
    for pair in range(2):
        cols = slice(pair * 2 * HEAD, (pair + 1) * 2 * HEAD)
        kp, qp = keys[:, cols], scaled[:, cols]
        vt = values[:, cols].T
        parts = []
        for h in range(2):
            km = jnp.where((lane >= HEAD) if h else (lane < HEAD), kp, bf16(0))
            scores = dot_nt(km, qp) + mask[...]
            highest = jnp.max(scores, axis=0, keepdims=True)
            weight = jnp.exp(scores - highest)
            total = jnp.sum(weight, axis=0, keepdims=True)
            parts.append(dot_nn(vt[h * HEAD : (h + 1) * HEAD], weight.astype(bf16)) / total)
            lse_out[0, 0, pl.ds(2 * pair + h, 1), :] = highest + jnp.log(total)
        ctx_out[:, cols] = jnp.concatenate(parts, axis=0).T.astype(bf16)


def attend_forward(core, x, seg_col, alive_col, seg_row, vecs, qkv):
    count, width = x.shape
    rows, _, length = seg_row.shape
    quads = width // QUAD
    full = pl.BlockSpec((length, width), lambda r, j: (r, 0))
    col = pl.BlockSpec((length, 128), lambda r, j: (r, 0))
    block = pl.BlockSpec((length, QUAD), lambda r, j: (r, j))
    low = jax.ShapeDtypeStruct((count, width), bf16)
    return pl.pallas_call(
        attend_forward_kernel,
        grid=(rows, quads),
        in_specs=[SMEM, full, col, col, pl.BlockSpec((1, 1, length), lambda r, j: (r, 0, 0)),
                  pl.BlockSpec((8, QUAD), lambda r, j: (0, j)), ANY, ANY, ANY, ANY],
        out_specs=[block] * 4 + [pl.BlockSpec((1, 1, 8, length), lambda r, j: (r, j, 0, 0))],
        out_shape=[low] * 4 + [jax.ShapeDtypeStruct((rows, quads, 8, length), f32)],
        scratch_shapes=[
            pltpu.VMEM((3, width, width), bf16),
            pltpu.VMEM((length, length), f32),
            pltpu.SemaphoreType.DMA((3, 8)),
        ],
        compiler_params=params(),
        cost_estimate=pl.CostEstimate(
            flops=2 * count * width * width * 3 + 4 * 4 * count * length * width,
            bytes_accessed=count * width * 10 + 3 * width * width * 2, transcendentals=0),
        name="attend_forward",
    )(core, x, seg_col, alive_col, seg_row, vecs, *qkv)


GELU_A = math.sqrt(2.0 / math.pi)
GELU_B = 0.044715


def gelu_both(u):
    square = u * u
    t = jnp.tanh(u * (GELU_A + (GELU_A * GELU_B) * square))
    half = 0.5 + 0.5 * t
    slope = half + (u * (1.0 - t * t)) * (0.5 * GELU_A + (1.5 * GELU_A * GELU_B) * square)
    return u * half, slope


def widen_kernel(
    top, core_ref, ctx, resid, vecs, up_bias, oo_a, oo_b, os_a, os_b, uo_a, uo_b, us_a, us_b,
    mixed_out, low_out, act_out, slope_out, out_weight, up_weight, sems,
):
    core = core_ref[0]
    first = pl.program_id(0) == 0
    out_copies = piece_copies(core, (oo_a, oo_b, os_a, os_b), out_weight, sems.at[0])
    up_copies = piece_copies(core, (uo_a, uo_b, us_a, us_b), up_weight, sems.at[1])

    @pl.when(first)
    def _():
        start_all(out_copies)
        start_all(up_copies)
        wait_all(out_copies)

    if top:
        hidden = normalize(resid[...])[0] * vecs[G2 : G2 + 1, :] + vecs[S2 : S2 + 1, :]
    else:
        hidden = resid[...].astype(f32)
    mixed = hidden + dot_nt(ctx[...], out_weight[...]) + vecs[OB : OB + 1, :]
    mixed_out[...] = mixed
    normed = normalize(mixed)[0] * vecs[G1 : G1 + 1, :] + vecs[S1 : S1 + 1, :]
    low = normed.astype(bf16)
    low_out[...] = low

    @pl.when(first)
    def _():
        wait_all(up_copies)

    width = low.shape[1]
    for chunk in range(up_weight.shape[0] // width):
        cols = slice(chunk * width, (chunk + 1) * width)
        upward = dot_nt(low, up_weight[cols, :]) + up_bias[0:1, cols]
        act, slope = gelu_both(upward)
        act_out[:, cols] = act.astype(bf16)
        slope_out[:, cols] = slope.astype(bf16)


def widen(top, core, ctx, resid, vecs, up_bias, out_weight, up_weight):
    count, width = ctx.shape
    wide = up_bias.shape[1]
    tile = pl.BlockSpec((TILE, width), lambda i: (i, 0))
    broad = pl.BlockSpec((TILE, wide), lambda i: (i, 0))
    return pl.pallas_call(
        partial(widen_kernel, top),
        grid=(count // TILE,),
        in_specs=[SMEM, tile, tile, whole((8, width)), whole((8, wide))] + [ANY] * 8,
        out_specs=[tile, tile, broad, broad],
        out_shape=[
            jax.ShapeDtypeStruct((count, width), f32),
            jax.ShapeDtypeStruct((count, width), bf16),
            jax.ShapeDtypeStruct((count, wide), bf16),
            jax.ShapeDtypeStruct((count, wide), bf16),
        ],
        scratch_shapes=[
            pltpu.VMEM((width, width), bf16),
            pltpu.VMEM((wide, width), bf16),
            pltpu.SemaphoreType.DMA((2, 8)),
        ],
        compiler_params=params(),
        cost_estimate=pl.CostEstimate(
            flops=2 * count * width * (width + wide),
            bytes_accessed=count * (width * 12 + wide * 4), transcendentals=0),
        name="widen",
    )(core, ctx, resid, vecs, up_bias, *out_weight, *up_weight)


def narrow_kernel(core_ref, act, mixed, vecs, do_a, do_b, ds_a, ds_b, combined_out, low_out, down_weight, sems):
    core = core_ref[0]
    copies = piece_copies(core, (do_a, do_b, ds_a, ds_b), down_weight, sems)

    @pl.when(pl.program_id(0) == 0)
    def _():
        start_all(copies)
        wait_all(copies)

    normed = normalize(mixed[...])[0] * vecs[G1 : G1 + 1, :] + vecs[S1 : S1 + 1, :]
    combined = normed + dot_nt(act[...], down_weight[...]) + vecs[DB : DB + 1, :]
    combined_out[...] = combined
    hidden = normalize(combined)[0] * vecs[G2 : G2 + 1, :] + vecs[S2 : S2 + 1, :]
    low_out[...] = hidden.astype(bf16)


def narrow(core, act, mixed, vecs, down_weight):
    count, width = mixed.shape
    wide = act.shape[1]
    tile = pl.BlockSpec((TILE, width), lambda i: (i, 0))
    broad = pl.BlockSpec((TILE, wide), lambda i: (i, 0))
    return pl.pallas_call(
        narrow_kernel,
        grid=(count // TILE,),
        in_specs=[SMEM, broad, tile, whole((8, width))] + [ANY] * 4,
        out_specs=[tile, tile],
        out_shape=[jax.ShapeDtypeStruct((count, width), f32), jax.ShapeDtypeStruct((count, width), bf16)],
        scratch_shapes=[pltpu.VMEM((width, wide), bf16), pltpu.SemaphoreType.DMA((8,))],
        compiler_params=params(),
        cost_estimate=pl.CostEstimate(
            flops=2 * count * width * wide, bytes_accessed=count * (width * 10 + wide * 2), transcendentals=0),
        name="narrow",
    )(core, act, mixed, vecs, *down_weight)


def add_rows(out, first, values):
    @pl.when(first)
    def _():
        out[...] = jnp.zeros_like(out)

    for index, value in enumerate(values):
        out[index] += partial_sum(value)


def narrow_top_kernel(
    core_ref, act, mixed, vecs, cot, alive_col, do_a, do_b, ds_a, ds_b,
    outputs, gc_out, gb_out, sums, down_weight, sems,
):
    core = core_ref[0]
    first = pl.program_id(0) == 0
    copies = piece_copies(core, (do_a, do_b, ds_a, ds_b), down_weight, sems)

    @pl.when(first)
    def _():
        start_all(copies)
        wait_all(copies)

    normed = normalize(mixed[...])[0] * vecs[G1 : G1 + 1, :] + vecs[S1 : S1 + 1, :]
    combined = normed + dot_nt(act[...], down_weight[...]) + vecs[DB : DB + 1, :]
    unit, rstd = normalize(combined)
    gain = vecs[G2 : G2 + 1, :]
    alive = alive_col[:, 0:1].astype(f32)
    outputs[...] = ((unit * gain + vecs[S2 : S2 + 1, :]) * alive).astype(bf16)
    grad = cot[...].astype(f32) * alive
    grad_combined = normalize_back(grad, gain, unit, rstd)
    branch = grad_combined.astype(bf16)
    gc_out[...] = grad_combined
    gb_out[...] = branch
    add_rows(sums, first, (grad * unit, grad, branch.astype(f32)))


def narrow_top(core, act, mixed, vecs, cot, alive_col, down_weight):
    count, width = mixed.shape
    wide = act.shape[1]
    tile = pl.BlockSpec((TILE, width), lambda i: (i, 0))
    broad = pl.BlockSpec((TILE, wide), lambda i: (i, 0))
    return pl.pallas_call(
        narrow_top_kernel,
        grid=(count // TILE,),
        in_specs=[SMEM, broad, tile, whole((8, width)), tile, pl.BlockSpec((TILE, 128), lambda i: (i, 0))] + [ANY] * 4,
        out_specs=[tile, tile, tile, whole((3, 8, width))],
        out_shape=[
            jax.ShapeDtypeStruct((count, width), bf16),
            jax.ShapeDtypeStruct((count, width), f32),
            jax.ShapeDtypeStruct((count, width), bf16),
            jax.ShapeDtypeStruct((3, 8, width), f32),
        ],
        scratch_shapes=[pltpu.VMEM((width, wide), bf16), pltpu.SemaphoreType.DMA((8,))],
        compiler_params=params(),
        cost_estimate=pl.CostEstimate(
            flops=2 * count * width * wide, bytes_accessed=count * (width * 14 + wide * 2), transcendentals=0),
        name="narrow_top",
    )(core, act, mixed, vecs, cot, alive_col, *down_weight)


def feed_back_kernel(
    core_ref, gb, gc, slope, mixed, vecs, do_a, do_b, ds_a, ds_b, uo_a, uo_b, us_a, us_b, oo_a, oo_b, os_a, os_b,
    gu_out, gm_out, ga_out, gctx_out, sums, up_sums, down_weight, up_weight, out_weight, sems,
):
    core = core_ref[0]
    first = pl.program_id(0) == 0
    down_copies = piece_copies(core, (do_a, do_b, ds_a, ds_b), down_weight, sems.at[0])
    up_copies = piece_copies(core, (uo_a, uo_b, us_a, us_b), up_weight, sems.at[1])
    out_copies = piece_copies(core, (oo_a, oo_b, os_a, os_b), out_weight, sems.at[2])

    @pl.when(first)
    def _():
        start_all(down_copies)
        start_all(up_copies)
        start_all(out_copies)
        up_sums[...] = jnp.zeros_like(up_sums)
        wait_all(down_copies)
        wait_all(up_copies)

    branch = gb[...]
    grad_normed = gc[...]
    width = branch.shape[1]
    for chunk in range(up_weight.shape[0] // width):
        cols = slice(chunk * width, (chunk + 1) * width)
        grad_up = (dot_nn(branch, down_weight[:, cols]) * slope[:, cols].astype(f32)).astype(bf16)
        gu_out[:, cols] = grad_up
        up_sums[:, cols] += partial_sum(grad_up.astype(f32))
        grad_normed = grad_normed + dot_nn(grad_up, up_weight[cols, :])
    unit, rstd = normalize(mixed[...])
    grad_mixed = normalize_back(grad_normed, vecs[G1 : G1 + 1, :], unit, rstd)
    gm_out[...] = grad_mixed
    attn = grad_mixed.astype(bf16)
    ga_out[...] = attn
    add_rows(sums, first, (grad_normed * unit, grad_normed, attn.astype(f32)))

    @pl.when(first)
    def _():
        wait_all(out_copies)

    gctx_out[...] = dot_nn(attn, out_weight[...]).astype(bf16)


def feed_back(core, gb, gc, slope, mixed, vecs, down_weight, up_weight, out_weight):
    count, width = mixed.shape
    wide = slope.shape[1]
    tile = pl.BlockSpec((TILE, width), lambda i: (i, 0))
    broad = pl.BlockSpec((TILE, wide), lambda i: (i, 0))
    return pl.pallas_call(
        feed_back_kernel,
        grid=(count // TILE,),
        in_specs=[SMEM, tile, tile, broad, tile, whole((8, width))] + [ANY] * 12,
        out_specs=[broad, tile, tile, tile, whole((3, 8, width)), whole((8, wide))],
        out_shape=[
            jax.ShapeDtypeStruct((count, wide), bf16),
            jax.ShapeDtypeStruct((count, width), f32),
            jax.ShapeDtypeStruct((count, width), bf16),
            jax.ShapeDtypeStruct((count, width), bf16),
            jax.ShapeDtypeStruct((3, 8, width), f32),
            jax.ShapeDtypeStruct((8, wide), f32),
        ],
        scratch_shapes=[
            pltpu.VMEM((width, wide), bf16),
            pltpu.VMEM((wide, width), bf16),
            pltpu.VMEM((width, width), bf16),
            pltpu.SemaphoreType.DMA((3, 8)),
        ],
        compiler_params=params(),
        cost_estimate=pl.CostEstimate(
            flops=2 * count * width * (width + 2 * wide),
            bytes_accessed=count * (width * 20 + wide * 4), transcendentals=0),
        name="feed_back",
    )(core, gb, gc, slope, mixed, vecs, *down_weight, *up_weight, *out_weight)


def attend_back_kernel(
    q, k, v, gctx, lse, seg_col, alive_col, seg_row, grads, sums, mask,
):
    @pl.when(pl.program_id(1) == 0)
    def _():
        mask_into(mask, seg_col, alive_col, seg_row)

    length = q.shape[0]
    lane = lax.broadcasted_iota(jnp.int32, (length, 2 * HEAD), 1)
    scaling = HEAD**-0.5
    for pair in range(2):
        cols = slice(pair * 2 * HEAD, (pair + 1) * 2 * HEAD)
        kp, vp, go = k[:, cols], v[:, cols], gctx[:, cols]
        qp = q[:, cols] * bf16(scaling)
        kt = kp.T
        dq_parts = []
        dk = dv = None
        for h in range(2):
            here = (lane >= HEAD) if h else (lane < HEAD)
            zero = bf16(0)
            qm, gm = jnp.where(here, qp, zero), jnp.where(here, go, zero)
            scores = dot_nt(kp, qm) + mask[...]
            probs = jnp.exp(scores - lse[0, 0, pl.ds(2 * pair + h, 1), :])
            weighted = probs * dot_nt(vp, gm)
            inner = jnp.sum(weighted, axis=0, keepdims=True)
            grad_scores = (weighted - probs * inner).astype(bf16)
            dv_h = dot_nn(probs.astype(bf16), gm)
            dk_h = dot_nn(grad_scores, qm)
            dv = dv_h if dv is None else dv + dv_h
            dk = dk_h if dk is None else dk + dk_h
            dq_parts.append(dot_nn(kt[h * HEAD : (h + 1) * HEAD], grad_scores))
        dq = (jnp.concatenate(dq_parts, axis=0).T * scaling).astype(bf16)
        dv = dv.astype(bf16)
        grads[0, :, cols] = dq
        grads[1, :, cols] = dk.astype(bf16)
        grads[2, :, cols] = dv
        sums[0, 0, :, cols] = partial_sum(dq.astype(f32))
        sums[0, 1, :, cols] = partial_sum(dv.astype(f32))


def attend_back(q, k, v, gctx, lse, seg_col, alive_col, seg_row):
    count, width = q.shape
    rows, _, length = seg_row.shape
    col = pl.BlockSpec((length, 128), lambda r, j: (r, 0))
    block = pl.BlockSpec((length, QUAD), lambda r, j: (r, j))
    return pl.pallas_call(
        attend_back_kernel,
        grid=(rows, width // QUAD),
        in_specs=[block] * 4 + [pl.BlockSpec((1, 1, 8, length), lambda r, j: (r, j, 0, 0)), col, col,
                                pl.BlockSpec((1, 1, length), lambda r, j: (r, 0, 0))],
        out_specs=[pl.BlockSpec((3, length, QUAD), lambda r, j: (0, r, j)),
                   pl.BlockSpec((1, 2, 8, QUAD), lambda r, j: (r, 0, 0, j))],
        out_shape=[jax.ShapeDtypeStruct((3, count, width), bf16), jax.ShapeDtypeStruct((rows, 2, 8, width), f32)],
        scratch_shapes=[pltpu.VMEM((length, length), f32)],
        compiler_params=params(),
        cost_estimate=pl.CostEstimate(
            flops=4 * 10 * count * length * width, bytes_accessed=count * width * 16, transcendentals=0),
        name="attend_back",
    )(q, k, v, gctx, lse, seg_col, alive_col, seg_row)


def input_back_kernel(below, core_ref, grads, gm, *rest):
    if below:
        combined, vecs, own_a, own_b, sib_a, sib_b, gc_out, gb_out, sums, weights, sems = rest
    else:
        own_a, own_b, sib_a, sib_b, grad_out, weights, sems = rest
    core = core_ref[0]
    first = pl.program_id(0) == 0
    copies = [
        piece_copies(core, (own_a, own_b, sib_a, sib_b), weights.at[w], sems.at[w], w)
        for w in range(3)
    ]

    @pl.when(first)
    def _():
        for group in copies:
            start_all(group)
        for group in copies:
            wait_all(group)

    grad = gm[...]
    for w in range(3):
        grad = grad + dot_nn(grads[w], weights[w])
    if below:
        unit, rstd = normalize(combined[...])
        grad_combined = normalize_back(grad, vecs[G2 : G2 + 1, :], unit, rstd)
        branch = grad_combined.astype(bf16)
        gc_out[...] = grad_combined
        gb_out[...] = branch
        add_rows(sums, first, (grad * unit, grad, branch.astype(f32)))
    else:
        grad_out[...] = grad


def input_back(core, grads, gm, qkv, combined=None, vecs=None):
    count, width = gm.shape
    below = combined is not None
    tile = pl.BlockSpec((TILE, width), lambda i: (i, 0))
    high = jax.ShapeDtypeStruct((count, width), f32)
    extra, extra_specs = ((combined, vecs), [tile, whole((8, width))]) if below else ((), [])
    out_specs, out_shape = [tile], [high]
    if below:
        out_specs += [tile, whole((3, 8, width))]
        out_shape += [jax.ShapeDtypeStruct((count, width), bf16), jax.ShapeDtypeStruct((3, 8, width), f32)]
    return pl.pallas_call(
        partial(input_back_kernel, below),
        grid=(count // TILE,),
        in_specs=[SMEM, pl.BlockSpec((3, TILE, width), lambda i: (0, i, 0)), tile] + extra_specs + [ANY] * 4,
        out_specs=out_specs,
        out_shape=out_shape,
        scratch_shapes=[pltpu.VMEM((3, width, width), bf16), pltpu.SemaphoreType.DMA((3, 8))],
        compiler_params=params(),
        cost_estimate=pl.CostEstimate(
            flops=2 * count * width * width * 3, bytes_accessed=count * width * 14, transcendentals=0),
        name="input_back",
    )(core, grads, gm, *extra, *qkv)


def weight_grad_kernel(layers, place_ref, *refs):
    grads, inputs = refs[:layers], refs[layers : 2 * layers]
    keep, send, turned = refs[2 * layers :]
    core, flip = place_ref[0], place_ref[1]
    rows = turned.shape[0] // 4
    span = grads[0].shape[-2]

    @pl.when(pl.program_id(1) == 0)
    def _():
        for layer in range(layers):
            flat = grads[layer][0].T
            for block in range(4):
                x, c = block // 2, block % 2
                slot = 2 * ((x + flip) % 2) + (c + core) % 2
                turned[pl.ds(pl.multiple_of(slot * rows, rows), rows), layer * span : (layer + 1) * span] = (
                    flat[block * rows : (block + 1) * rows]
                )

    total = None
    for layer in range(layers):
        term = dot_nn(turned[:, layer * span : (layer + 1) * span], inputs[layer][...])
        total = term if total is None else total + term
    total = total.astype(bf16)
    halves = keep.shape[1]
    wide = keep.shape[-1]
    for half in range(halves):
        for x in range(2):
            for c, out in ((0, keep), (1, send)):
                start = (2 * x + c) * rows
                out[0, half, x] = total[start : start + rows, half * wide : (half + 1) * wide]


def weight_grad(place, grads, inputs):
    layers = len(grads)
    count_w, span, n = grads[0].shape
    depth = inputs[0].shape[1]
    chunk = min(depth, n)
    chunks = depth // chunk
    halves = 2 if chunks == 1 else 1
    wide = chunk // halves
    per_half = depth // 2 // wide
    rows = n // 4
    if chunks == 1:
        out_spec = pl.BlockSpec((1, 2, 2, rows, wide), lambda w, j: (w, 0, 0, 0, 0))
    else:
        out_spec = pl.BlockSpec((1, 1, 2, rows, wide), lambda w, j: (w, j // per_half, 0, 0, j % per_half))
    out = jax.ShapeDtypeStruct((count_w, 2, 2, rows, depth // 2), bf16)
    return pl.pallas_call(
        partial(weight_grad_kernel, layers),
        grid=(count_w, chunks),
        in_specs=[SMEM] + [pl.BlockSpec((1, span, n), lambda w, j: (w, 0, 0))] * layers
        + [pl.BlockSpec((span, chunk), lambda w, j: (0, j))] * layers,
        out_specs=[out_spec, out_spec],
        out_shape=[out, out],
        scratch_shapes=[pltpu.VMEM((n, layers * span), bf16)],
        compiler_params=params(),
        cost_estimate=pl.CostEstimate(
            flops=2 * layers * span * n * depth * count_w,
            bytes_accessed=2 * layers * span * (n * count_w + depth) + 2 * n * depth * count_w, transcendentals=0),
        name="weight_grad",
    )(place, *grads, *inputs)


def tall_grad_kernel(layers, place_ref, *refs):
    grads, inputs = refs[:layers], refs[layers : 2 * layers]
    keep, send = refs[2 * layers :]
    total = None
    for layer in range(layers):
        term = dot_nn(grads[layer][...].T, inputs[layer][...])
        total = term if total is None else total + term
    total = total.astype(bf16)
    wide = keep.shape[-1]

    for c, out in ((0, keep), (1, send)):
        @pl.when(pl.program_id(1) == c)
        def _():
            for half in range(2):
                out[half, 0] = total[:, half * wide : (half + 1) * wide]


def tall_grad(place, grads, inputs):
    layers = len(grads)
    span, n = grads[0].shape
    depth = inputs[0].shape[1]
    rows = n // 4

    def column(x, c, place):
        return 0, 2 * ((x + place[1]) % 2) + (c + place[0]) % 2

    out_spec = pl.BlockSpec((2, 1, rows, depth // 2), lambda x, c, place: (0, x, 0, 0))
    out = jax.ShapeDtypeStruct((2, 2, rows, depth // 2), bf16)
    return pl.pallas_call(
        partial(tall_grad_kernel, layers),
        grid_spec=pltpu.PrefetchScalarGridSpec(
            num_scalar_prefetch=1,
            grid=(2, 2),
            in_specs=[pl.BlockSpec((span, rows), column)] * layers
            + [pl.BlockSpec((span, depth), lambda x, c, place: (0, 0))] * layers,
            out_specs=[out_spec, out_spec],
        ),
        out_shape=[out, out],
        compiler_params=params(),
        cost_estimate=pl.CostEstimate(
            flops=2 * layers * span * n * depth,
            bytes_accessed=2 * layers * span * (n + depth) + 2 * n * depth, transcendentals=0),
        name="tall_grad",
    )(place, *grads, *inputs)


AXES = ("dp", "fsdp")


def halves(v):
    middle = v.shape[-1] // 2
    return v[..., :middle], v[..., middle:]


def pack_vectors(parts):
    return jnp.concatenate(parts, axis=-1)


class Plain:
    def __init__(self, mesh):
        self.devices = math.prod(mesh.shape.values())

    def place(self):
        return jnp.zeros((2,), jnp.int32)

    def gather(self, shards, vector):
        def pieces(full):
            blocks = full.reshape(full.shape[:-2] + (2, 2, full.shape[-2] // 4, full.shape[-1]))
            own, sibling = blocks[..., 0, :, :], blocks[..., 1, :, :]
            return (*halves(own), *halves(sibling))

        def full(shard):
            return lax.all_gather(shard, AXES, axis=0, tiled=True)

        query, key, value, out, up, down = shards
        qkv = jnp.stack([full(query), full(key), full(value)])
        return (pieces(qkv), pieces(full(out)), pieces(full(up)), pieces(full(down))), full(vector[None])

    def scatter(self, keep, send):
        count, sides, xs, rows, half = keep.shape
        both = jnp.stack([keep, send], axis=3).astype(f32)
        full = jnp.moveaxis(both, 1, 4).reshape(count, xs * 2 * rows, sides * half)
        return lax.psum_scatter(full, AXES, scatter_dimension=1, tiled=True)

    def scatter_vector(self, vector):
        return lax.psum_scatter(vector, AXES, scatter_dimension=0, tiled=True)[0]


class Grid:
    def __init__(self, mesh):
        pass

    def where(self):
        dp, fsdp = lax.axis_index("dp"), lax.axis_index("fsdp")
        return dp // 2, dp % 2, fsdp // 2, fsdp % 2

    def place(self):
        x, core, _, _ = self.where()
        return jnp.stack([core, x]).astype(jnp.int32)

    def swap(self, value, x=0, core=0, z=0, y=0):
        flip = ((x * 2 + core) * 4 + z) * 2 + y
        return lax.ppermute(value, AXES, [(i, i ^ flip) for i in range(32)])

    def ordered(self, mine, other, side, axis=0):
        return jnp.stack([jnp.where(side == 0, mine, other), jnp.where(side == 0, other, mine)], axis=axis)

    def spread(self, payload):
        x, _, z, y = self.where()
        parts = [payload] + [self.swap(payload, z=k) for k in range(1, 4)]
        odd, high = z % 2, z // 2
        parts = [jnp.where(odd == 0, parts[k], parts[k ^ 1]) for k in range(4)]
        parts = jnp.stack([jnp.where(high == 0, parts[k], parts[k ^ 2]) for k in range(4)])
        left, right = halves(parts)
        left_x = self.ordered(left, self.swap(left, x=1), x)
        right_y = self.ordered(right, self.swap(right, y=1), y, axis=1)
        left_xy = self.ordered(left_x, self.swap(left_x, y=1), y, axis=2)
        right_xy = self.ordered(right_y, self.swap(right_y, x=1), x)
        return left_xy, right_xy, parts

    def pieces(self, left, right, start, rows):
        def section(v):
            v = v[:, :, :, start : start + rows]
            return v.reshape(2, 8 * rows, v.shape[-1])

        return section(left), section(right)

    def with_sibling(self, left, right):
        return left, right, self.swap(left, core=1), self.swap(right, core=1)

    def gather(self, shards, vector):
        query, key, value, out, up, down = shards
        _, core, _, _ = self.where()
        small, width = query.shape
        tail = jnp.zeros((8, width), bf16).at[0, : vector.shape[0]].set(vector)
        left, right, token = self.spread(jnp.concatenate([query, key, value, tail], axis=0))
        stack = [self.pieces(left, right, w * small, small) for w in range(3)]
        qkv = self.with_sibling(jnp.stack([s[0] for s in stack]), jnp.stack([s[1] for s in stack]))
        mine = left[:, :, :, 3 * small, : vector.shape[0]].reshape(2, 8, -1)
        vectors = self.ordered(mine, self.swap(mine, core=1), core, axis=1).reshape(32, -1)
        second = jnp.concatenate([out, up], axis=0)
        second, token = lax.optimization_barrier((second, token))
        left, right, token = self.spread(second)
        out_w = self.with_sibling(*self.pieces(left, right, 0, out.shape[0]))
        up_w = self.with_sibling(*self.pieces(left, right, out.shape[0], up.shape[0]))
        down, token = lax.optimization_barrier((down, token))
        left, right, _ = self.spread(down)
        down_w = self.with_sibling(*self.pieces(left, right, 0, down.shape[0]))
        return (qkv, out_w, up_w, down_w), vectors

    def scatter(self, keep, send):
        _, _, z, y = self.where()
        count, _, _, rows, half = keep.shape
        mine = rows // 8

        def add(a, b):
            return (a.astype(f32) + b.astype(f32)).astype(bf16)

        def pick(v, index, axis):
            return lax.dynamic_index_in_dim(v, index, axis, keepdims=False)

        total = add(keep, self.swap(send, core=1)).reshape(count, 2, 2, 4, 2, mine, half)
        left, right = total[:, 0], total[:, 1]
        left = add(left[:, 0], self.swap(left[:, 1], x=1))
        right = add(pick(right, y, 3), self.swap(pick(right, 1 - y, 3), y=1))
        left = add(pick(left, y, 2), self.swap(pick(left, 1 - y, 2), y=1))
        right = add(right[:, 0], self.swap(right[:, 1], x=1))
        both = jnp.concatenate([left, right], axis=-1)
        result = pick(both, z, 1).astype(f32)
        for k in range(1, 4):
            result = result + self.swap(pick(both, z ^ k, 1), z=k).astype(f32)
        return result

    def scatter_vector(self, vector):
        x, core, z, y = self.where()

        def pick(v, index, axis):
            return lax.dynamic_index_in_dim(v, index, axis, keepdims=False)

        total = vector.reshape(2, 2, 4, 2, -1)
        total = pick(total, core, 1) + self.swap(pick(total, 1 - core, 1), core=1)
        total = pick(total, x, 0) + self.swap(pick(total, 1 - x, 0), x=1)
        total = pick(total, y, 1) + self.swap(pick(total, 1 - y, 1), y=1)
        result = pick(total, z, 0)
        for k in range(1, 4):
            result = result + self.swap(pick(total, z ^ k, 0), z=k)
        return result


def column_info(values, count):
    return jnp.broadcast_to(values.reshape(count, 1), (count, 128))


def body(
    exchange,
    tokens,
    cotangent,
    segment_ids,
    pad_mask,
    row_counts,
    query_weight,
    query_bias,
    key_weight,
    value_weight,
    value_bias,
    out_weight,
    out_bias,
    first_gain,
    first_shift,
    up_weight,
    up_bias,
    down_weight,
    down_bias,
    second_gain,
    second_shift,
):
    rows_here, row_len, width = tokens.shape
    count = rows_here * row_len
    present = (jnp.arange(rows_here, dtype=jnp.int32) < row_counts[0]).astype(jnp.int32)
    alive = pad_mask * present[:, None]
    alive_col = column_info(alive, count)
    seg_col = column_info(segment_ids, count)
    seg_row = segment_ids.reshape(rows_here, 1, row_len)
    place = exchange.place()

    mine = jnp.concatenate(
        [query_bias, value_bias, out_bias, first_gain, first_shift, down_bias, second_gain, second_shift, up_bias]
    )
    (qkv, out_w, up_w, down_w), vectors = exchange.gather(
        (query_weight, key_weight, value_weight, out_weight, up_weight, down_weight), mine
    )
    devices = vectors.shape[0]
    small = query_bias.shape[0]
    vectors = vectors.astype(f32)
    vecs = vectors[:, : 8 * small].reshape(devices, 8, small).transpose(1, 0, 2).reshape(8, width)
    wide = up_bias.shape[0] * devices
    up_vec = jnp.broadcast_to(vectors[:, 8 * small :].reshape(1, wide), (8, wide))

    flat = tokens.reshape(count, width)
    saved = []
    inputs, resid = flat, flat
    for layer in range(LAYERS):
        top = layer == LAYERS - 1
        queries, keys, values, context, lse = attend_forward(
            place, inputs, seg_col, alive_col, seg_row, vecs, qkv
        )
        mixed, low, act, slope = widen(layer > 0, place, context, resid, vecs, up_vec, out_w, up_w)
        kept = dict(inputs=inputs, q=queries, k=keys, v=values, ctx=context, lse=lse, mixed=mixed, low=low, act=act, slope=slope)
        if top:
            outputs, gc, gb, norm_sums = narrow_top(
                place, act, mixed, vecs, cotangent.reshape(count, width), alive_col, down_w
            )
        else:
            resid, inputs = narrow(place, act, mixed, vecs, down_w)
            kept["combined"] = resid
        saved.append(kept)

    terms = [[] for _ in range(4)]
    second_sums, first_sums, up_sums, bias_sums = 0, 0, 0, 0
    results = {}
    for layer in reversed(range(LAYERS)):
        kept = saved[layer]
        last = layer == 0
        second_sums = second_sums + norm_sums
        terms[0].append((gb, kept["act"]))
        if last:
            results["down"] = exchange.scatter(*weight_grad(place, [g[None] for g, _ in terms[0]], [v for _, v in terms[0]]))
        gu, gm, ga, gctx, sums, wide_sums = feed_back(
            place, gb, gc, kept["slope"], kept["mixed"], vecs, down_w, up_w, out_w
        )
        first_sums, up_sums = first_sums + sums, up_sums + wide_sums
        terms[1].append((gu, kept["low"]))
        terms[2].append((ga, kept["ctx"]))
        if last:
            keep, send = tall_grad(place, [g for g, _ in terms[1]], [v for _, v in terms[1]])
            results["up"] = exchange.scatter(keep[None], send[None])
            results["out"] = exchange.scatter(*weight_grad(place, [g[None] for g, _ in terms[2]], [v for _, v in terms[2]]))
        grads, sums = attend_back(
            kept["q"], kept["k"], kept["v"], gctx, kept["lse"], seg_col, alive_col, seg_row
        )
        bias_sums = bias_sums + jnp.sum(sums, axis=0)
        terms[3].append((grads, kept["inputs"]))
        if last:
            results["qkv"] = exchange.scatter(*weight_grad(place, [g for g, _ in terms[3]], [v for _, v in terms[3]]))
            (tokens_grad,) = input_back(place, grads, gm, qkv)
        else:
            gc, gb, norm_sums = input_back(place, grads, gm, qkv, saved[layer - 1]["combined"], vecs)

    bias_sums = jnp.sum(bias_sums, axis=1)
    first_sums = jnp.sum(first_sums, axis=1)
    second_sums = jnp.sum(second_sums, axis=1)
    up_sums = jnp.sum(up_sums, axis=0)
    stacked = jnp.stack(
        [bias_sums[0], bias_sums[1], first_sums[2], first_sums[0], first_sums[1], second_sums[2], second_sums[0], second_sums[1]]
    )
    vector = jnp.concatenate(
        [
            stacked.reshape(8, devices, small).transpose(1, 0, 2).reshape(devices, 8 * small),
            up_sums.reshape(devices, wide // devices),
        ],
        axis=1,
    )
    vector = exchange.scatter_vector(vector)
    piece = [vector[i * small : (i + 1) * small] for i in range(8)]
    query_grad, key_grad, value_grad = results["qkv"]
    return (
        outputs.reshape(rows_here, row_len, width),
        tokens_grad.reshape(rows_here, row_len, width),
        query_grad,
        piece[QB],
        key_grad,
        value_grad,
        piece[VB],
        results["out"][0],
        piece[OB],
        piece[G1],
        piece[S1],
        results["up"][0],
        vector[8 * small :],
        results["down"][0],
        piece[DB],
        piece[G2],
        piece[S2],
    )


def solution(mesh):
    rows = P(AXES, None, None)
    flat = P(AXES, None)
    line = P(AXES)
    matrices = (flat, line, flat, flat, line, flat, line, line, line, flat, line, flat, line, line, line)
    exchange = Grid(mesh) if dict(mesh.shape) == {"dp": 4, "fsdp": 8} else Plain(mesh)
    return jax.shard_map(
        partial(body, exchange),
        mesh=mesh,
        in_specs=(rows, rows, flat, flat, line) + matrices,
        out_specs=(rows, rows) + matrices,
        check_vma=False,
    )
```

```python
from functools import partial
import math

import jax
import jax.numpy as jnp
from jax import lax
from jax.experimental import pallas as pl
from jax.experimental.pallas import tpu as pltpu
from jax.sharding import PartitionSpec as P

HEAD = 64
LAYERS = 2
QUAD = 4 * HEAD
TILE = 256
SUB = 256
norm_eps = 1e-06
masked_score = -1000000000.0
VMEM = 60 * 1024 * 1024
bf16 = jnp.bfloat16
f32 = jnp.float32

QB, VB, OB, G1, S1, DB, G2, S2 = range(8)


def dot_nt(left, right):
    return lax.dot_general(left, right, (((1,), (1,)), ((), ())), preferred_element_type=f32)


def dot_nn(left, right):
    return lax.dot_general(left, right, (((1,), (0,)), ((), ())), preferred_element_type=f32)


def normalize(v):
    mean = jnp.mean(v, axis=-1, keepdims=True)
    centered = v - mean
    rstd = lax.rsqrt(jnp.mean(centered * centered, axis=-1, keepdims=True) + norm_eps)
    return centered * rstd, rstd


def normalize_back(grad, gain, unit, rstd):
    scaled = grad * gain
    first = jnp.mean(scaled, axis=-1, keepdims=True)
    second = jnp.mean(scaled * unit, axis=-1, keepdims=True)
    return rstd * (scaled - first - unit * second)


def partial_sum(v):
    return jnp.sum(v.reshape(v.shape[0] // 8, 8, v.shape[1]), axis=0)


def piece_copies(core, pieces, place, sems, which=None):
    copies = []
    for sibling, piece in enumerate(pieces):
        source = piece if which is None else piece.at[which]
        sides, _, rows, half = source.shape
        for side in range(sides):
            for x in range(2):
                slot = 2 * x + (1 - core if sibling else core)
                start = pl.multiple_of(slot * rows, rows)
                copies.append(
                    pltpu.make_async_copy(
                        source.at[side, x],
                        place.at[pl.ds(start, rows), pl.ds(side * half, half)],
                        sems.at[4 * sibling + 2 * side + x],
                    )
                )
    return copies


def start_all(copies):
    for copy in copies:
        copy.start()


def wait_all(copies):
    for copy in copies:
        copy.wait()


def params():
    return pltpu.CompilerParams(vmem_limit_bytes=VMEM)


ANY = pl.BlockSpec(memory_space=pl.ANY)
SMEM = pl.BlockSpec(memory_space=pltpu.SMEM)


def whole(shape):
    return pl.BlockSpec(shape, lambda *_: (0,) * len(shape))


def mask_into(mask, seg_col, alive_col, seg_row):
    length = mask.shape[0]
    key = lax.broadcasted_iota(jnp.int32, (length, length), 0)
    query = lax.broadcasted_iota(jnp.int32, (length, length), 1)
    same = seg_col[:, 0:1] == seg_row[0]
    allowed = same & ((alive_col[:, 0:1] > 0) | (key == query))
    mask[...] = jnp.where(allowed, 0.0, masked_score)


def attend_forward_kernel(
    core_ref, x, seg_col, alive_col, seg_row, vecs, own, sib, *rest
):
    q_out, k_out, v_out, ctx_out, lse_out, weights, mask, sems = rest[-8:]
    row, quad = pl.program_id(0), pl.program_id(1)
    core = core_ref[0]
    first = (row == 0) & (quad == 0)
    copies = [
        piece_copies(core, (own, sib), weights.at[w], sems.at[w], w)
        for w in range(3)
    ]

    @pl.when(first)
    def _():
        for group in copies:
            start_all(group)

    @pl.when(quad == 0)
    def _():
        mask_into(mask, seg_col, alive_col, seg_row)

    @pl.when(first)
    def _():
        for group in copies:
            wait_all(group)

    inputs = x[...]
    heads = pl.ds(pl.multiple_of(quad * QUAD, QUAD), QUAD)
    queries = (dot_nt(inputs, weights[0, heads, :]) + vecs[QB : QB + 1, :]).astype(bf16)
    keys = dot_nt(inputs, weights[1, heads, :]).astype(bf16)
    values = (dot_nt(inputs, weights[2, heads, :]) + vecs[VB : VB + 1, :]).astype(bf16)
    q_out[...] = queries
    k_out[...] = keys
    v_out[...] = values
    scaled = queries * bf16(HEAD**-0.5)
    length = inputs.shape[0]
    lane = lax.broadcasted_iota(jnp.int32, (length, 2 * HEAD), 1)
    for pair in range(2):
        cols = slice(pair * 2 * HEAD, (pair + 1) * 2 * HEAD)
        kp, qp = keys[:, cols], scaled[:, cols]
        vt = values[:, cols].T
        parts = []
        for h in range(2):
            km = jnp.where((lane >= HEAD) if h else (lane < HEAD), kp, bf16(0))
            scores = dot_nt(km, qp) + mask[...]
            highest = jnp.max(scores, axis=0, keepdims=True)
            weight = jnp.exp(scores - highest)
            total = jnp.sum(weight, axis=0, keepdims=True)
            parts.append(dot_nn(vt[h * HEAD : (h + 1) * HEAD], weight.astype(bf16)) / total)
            lse_out[0, 0, pl.ds(2 * pair + h, 1), :] = highest + jnp.log(total)
        ctx_out[:, cols] = jnp.concatenate(parts, axis=0).T.astype(bf16)


def attend_forward(core, x, seg_col, alive_col, seg_row, vecs, qkv, start=0, stop=None, before=()):
    count, width = x.shape
    rows, _, length = seg_row.shape
    stop = rows if stop is None else stop
    quads = width // QUAD
    full = pl.BlockSpec((length, width), lambda r, j: (r + start, 0))
    col = pl.BlockSpec((length, 128), lambda r, j: (r + start, 0))
    block = pl.BlockSpec((length, QUAD), lambda r, j: (r + start, j))
    low = jax.ShapeDtypeStruct((count, width), bf16)
    share = (stop - start) / rows
    return pl.pallas_call(
        attend_forward_kernel,
        grid=(stop - start, quads),
        in_specs=[SMEM, full, col, col, pl.BlockSpec((1, 1, length), lambda r, j: (r + start, 0, 0)),
                  pl.BlockSpec((8, QUAD), lambda r, j: (0, j)), ANY, ANY] + [ANY] * len(before),
        out_specs=[block] * 4 + [pl.BlockSpec((1, 1, 8, length), lambda r, j: (r + start, j, 0, 0))],
        out_shape=[low] * 4 + [jax.ShapeDtypeStruct((rows, quads, 8, length), f32)],
        scratch_shapes=[
            pltpu.VMEM((3, width, width), bf16),
            pltpu.VMEM((length, length), f32),
            pltpu.SemaphoreType.DMA((3, 8)),
        ],
        input_output_aliases={8 + i: i for i in range(len(before))},
        compiler_params=params(),
        cost_estimate=pl.CostEstimate(
            flops=int(share * (2 * count * width * width * 3 + 4 * 4 * count * length * width)),
            bytes_accessed=int(share * count * width * 10) + 3 * width * width * 2, transcendentals=0),
        name="attend_forward",
    )(core, x, seg_col, alive_col, seg_row, vecs, *qkv, *before)


GELU_A = math.sqrt(2.0 / math.pi)
GELU_B = 0.044715


def gelu_both(u):
    square = u * u
    t = jnp.tanh(u * (GELU_A + (GELU_A * GELU_B) * square))
    half = 0.5 + 0.5 * t
    slope = half + (u * (1.0 - t * t)) * (0.5 * GELU_A + (1.5 * GELU_A * GELU_B) * square)
    return u * half, slope


def widen_kernel(
    core_ref, ctx, resid, vecs, up_bias, o_own, o_sib, u_own, u_sib,
    mixed_out, low_out, act_out, slope_out, out_weight, up_weight, sems,
):
    core = core_ref[0]
    first = pl.program_id(0) == 0
    out_copies = piece_copies(core, (o_own, o_sib), out_weight, sems.at[0])
    up_copies = piece_copies(core, (u_own, u_sib), up_weight, sems.at[1])

    @pl.when(first)
    def _():
        start_all(out_copies)
        start_all(up_copies)
        wait_all(out_copies)

    mixed = resid[...].astype(f32) + dot_nt(ctx[...], out_weight[...]) + vecs[OB : OB + 1, :]
    mixed_out[...] = mixed
    normed = normalize(mixed)[0] * vecs[G1 : G1 + 1, :] + vecs[S1 : S1 + 1, :]
    low = normed.astype(bf16)
    low_out[...] = low

    @pl.when(first)
    def _():
        wait_all(up_copies)

    width = low.shape[1]
    for chunk in range(up_weight.shape[0] // width):
        cols = slice(chunk * width, (chunk + 1) * width)
        upward = dot_nt(low, up_weight[cols, :]) + up_bias[0:1, cols]
        act, slope = gelu_both(upward)
        act_out[:, cols] = act.astype(bf16)
        slope_out[:, cols] = slope.astype(bf16)


def widen(core, ctx, resid, vecs, up_bias, out_weight, up_weight):
    count, width = ctx.shape
    wide = up_bias.shape[1]
    tile = pl.BlockSpec((TILE, width), lambda i: (i, 0))
    broad = pl.BlockSpec((TILE, wide), lambda i: (i, 0))
    return pl.pallas_call(
        widen_kernel,
        grid=(count // TILE,),
        in_specs=[SMEM, tile, tile, whole((8, width)), whole((8, wide))] + [ANY] * 4,
        out_specs=[tile, tile, broad, broad],
        out_shape=[
            jax.ShapeDtypeStruct((count, width), f32),
            jax.ShapeDtypeStruct((count, width), bf16),
            jax.ShapeDtypeStruct((count, wide), bf16),
            jax.ShapeDtypeStruct((count, wide), bf16),
        ],
        scratch_shapes=[
            pltpu.VMEM((width, width), bf16),
            pltpu.VMEM((wide, width), bf16),
            pltpu.SemaphoreType.DMA((2, 8)),
        ],
        compiler_params=params(),
        cost_estimate=pl.CostEstimate(
            flops=2 * count * width * (width + wide),
            bytes_accessed=count * (width * 12 + wide * 4), transcendentals=0),
        name="widen",
    )(core, ctx, resid, vecs, up_bias, *out_weight, *up_weight)


def narrow_kernel(core_ref, act, mixed, vecs, d_own, d_sib, combined_out, low_out, down_weight, sems):
    core = core_ref[0]
    copies = piece_copies(core, (d_own, d_sib), down_weight, sems)

    @pl.when(pl.program_id(0) == 0)
    def _():
        start_all(copies)
        wait_all(copies)

    normed = normalize(mixed[...])[0] * vecs[G1 : G1 + 1, :] + vecs[S1 : S1 + 1, :]
    combined = normed + dot_nt(act[...], down_weight[...]) + vecs[DB : DB + 1, :]
    combined_out[...] = combined
    hidden = normalize(combined)[0] * vecs[G2 : G2 + 1, :] + vecs[S2 : S2 + 1, :]
    low_out[...] = hidden.astype(bf16)


def narrow(core, act, mixed, vecs, down_weight):
    count, width = mixed.shape
    wide = act.shape[1]
    tile = pl.BlockSpec((TILE, width), lambda i: (i, 0))
    broad = pl.BlockSpec((TILE, wide), lambda i: (i, 0))
    return pl.pallas_call(
        narrow_kernel,
        grid=(count // TILE,),
        in_specs=[SMEM, broad, tile, whole((8, width))] + [ANY] * 2,
        out_specs=[tile, tile],
        out_shape=[jax.ShapeDtypeStruct((count, width), f32), jax.ShapeDtypeStruct((count, width), bf16)],
        scratch_shapes=[pltpu.VMEM((width, wide), bf16), pltpu.SemaphoreType.DMA((8,))],
        compiler_params=params(),
        cost_estimate=pl.CostEstimate(
            flops=2 * count * width * wide, bytes_accessed=count * (width * 10 + wide * 2), transcendentals=0),
        name="narrow",
    )(core, act, mixed, vecs, *down_weight)


def add_rows(out, first, values):
    @pl.when(first)
    def _():
        out[...] = jnp.zeros_like(out)

    for index, value in enumerate(values):
        out[index] += partial_sum(value)


def top_kernel(
    core_ref, ctx, resid, cot, alive_col, vecs, up_bias,
    o_own, o_sib, u_own, u_sib, d_own, d_sib,
    outputs, low_out, act_out, gb_out, gu_out, ga_out, gm_out, gctx_out, sums, up_sums,
    out_weight, up_weight, down_weight, slopes, sems,
):
    core = core_ref[0]
    first = pl.program_id(0) == 0
    out_copies = piece_copies(core, (o_own, o_sib), out_weight, sems.at[0])
    up_copies = piece_copies(core, (u_own, u_sib), up_weight, sems.at[1])
    down_copies = piece_copies(core, (d_own, d_sib), down_weight, sems.at[2])

    @pl.when(first)
    def _():
        start_all(out_copies)
        start_all(up_copies)
        start_all(down_copies)
        sums[...] = jnp.zeros_like(sums)
        up_sums[...] = jnp.zeros_like(up_sums)
        wait_all(out_copies)
        wait_all(up_copies)
        wait_all(down_copies)

    width = ctx.shape[1]
    chunks = [slice(c * width, (c + 1) * width) for c in range(up_weight.shape[0] // width)]
    for part in range(ctx.shape[0] // SUB):
        rows = slice(part * SUB, (part + 1) * SUB)
        hidden = normalize(resid[rows, :])[0] * vecs[G2 : G2 + 1, :] + vecs[S2 : S2 + 1, :]
        mixed = hidden + dot_nt(ctx[rows, :], out_weight[...]) + vecs[OB : OB + 1, :]
        first_unit, first_rstd = normalize(mixed)
        combined = first_unit * vecs[G1 : G1 + 1, :] + vecs[S1 : S1 + 1, :]
        low = combined.astype(bf16)
        low_out[rows, :] = low
        for cols in chunks:
            act, slope = gelu_both(dot_nt(low, up_weight[cols, :]) + up_bias[0:1, cols])
            act = act.astype(bf16)
            act_out[rows, cols] = act
            slopes[rows, cols] = slope.astype(bf16)
            combined = combined + dot_nt(act, down_weight[:, cols])
        unit, rstd = normalize(combined + vecs[DB : DB + 1, :])
        gain = vecs[G2 : G2 + 1, :]
        alive = alive_col[rows, 0:1].astype(f32)
        outputs[rows, :] = ((unit * gain + vecs[S2 : S2 + 1, :]) * alive).astype(bf16)
        grad = cot[rows, :].astype(f32) * alive
        sums[0] += partial_sum(grad * unit)
        sums[1] += partial_sum(grad)
        grad = normalize_back(grad, gain, unit, rstd)
        feed_back_rows(
            rows, chunks, grad, slopes, first_unit, first_rstd, vecs, down_weight, up_weight, out_weight,
            gb_out, gu_out, ga_out, gm_out, gctx_out, sums, up_sums,
        )


def feed_back_rows(
    rows, chunks, grad, slopes, unit, rstd, vecs, down_weight, up_weight, out_weight,
    gb_out, gu_out, ga_out, gm_out, gctx_out, sums, up_sums,
):
    branch = grad.astype(bf16)
    gb_out[rows, :] = branch
    sums[2] += partial_sum(branch.astype(f32))
    for cols in chunks:
        grad_up = (dot_nn(branch, down_weight[:, cols]) * slopes[rows, cols].astype(f32)).astype(bf16)
        gu_out[rows, cols] = grad_up
        up_sums[:, cols] += partial_sum(grad_up.astype(f32))
        grad = grad + dot_nn(grad_up, up_weight[cols, :])
    sums[3] += partial_sum(grad * unit)
    sums[4] += partial_sum(grad)
    grad = normalize_back(grad, vecs[G1 : G1 + 1, :], unit, rstd)
    gm_out[rows, :] = grad
    attn = grad.astype(bf16)
    ga_out[rows, :] = attn
    sums[5] += partial_sum(attn.astype(f32))
    gctx_out[rows, :] = dot_nn(attn, out_weight[...]).astype(bf16)


def top(core, ctx, resid, cot, alive_col, vecs, up_bias, out_weight, up_weight, down_weight):
    count, width = ctx.shape
    wide = up_bias.shape[1]
    tile = pl.BlockSpec((TILE, width), lambda i: (i, 0))
    broad = pl.BlockSpec((TILE, wide), lambda i: (i, 0))
    low = jax.ShapeDtypeStruct((count, width), bf16)
    low_wide = jax.ShapeDtypeStruct((count, wide), bf16)
    return pl.pallas_call(
        top_kernel,
        grid=(count // TILE,),
        in_specs=[SMEM, tile, tile, tile, pl.BlockSpec((TILE, 128), lambda i: (i, 0)), whole((8, width)),
                  whole((8, wide))] + [ANY] * 6,
        out_specs=[tile, tile, broad, tile, broad, tile, tile, tile, whole((6, 8, width)), whole((8, wide))],
        out_shape=[low, low, low_wide, low, low_wide, low, jax.ShapeDtypeStruct((count, width), f32), low,
                   jax.ShapeDtypeStruct((6, 8, width), f32), jax.ShapeDtypeStruct((8, wide), f32)],
        scratch_shapes=[
            pltpu.VMEM((width, width), bf16),
            pltpu.VMEM((wide, width), bf16),
            pltpu.VMEM((width, wide), bf16),
            pltpu.VMEM((TILE, wide), bf16),
            pltpu.SemaphoreType.DMA((3, 8)),
        ],
        compiler_params=params(),
        cost_estimate=pl.CostEstimate(
            flops=4 * count * width * (width + 2 * wide),
            bytes_accessed=count * (width * 22 + wide * 4), transcendentals=0),
        name="top",
    )(core, ctx, resid, cot, alive_col, vecs, up_bias, *out_weight, *up_weight, *down_weight)


def lower_kernel(
    core_ref, grads, gm, combined, slope, mixed, vecs, d_own, d_sib, u_own, u_sib,
    o_own, o_sib, q_own, q_sib,
    gb_out, gu_out, ga_out, gm_out, gctx_out, sums, up_sums, down_weight, up_weight, out_weight, weights, sems,
):
    core = core_ref[0]
    first = pl.program_id(0) == 0
    down_copies = piece_copies(core, (d_own, d_sib), down_weight, sems.at[0])
    up_copies = piece_copies(core, (u_own, u_sib), up_weight, sems.at[1])
    out_copies = piece_copies(core, (o_own, o_sib), out_weight, sems.at[2])
    copies = [
        piece_copies(core, (q_own, q_sib), weights.at[w], sems.at[3 + w], w) for w in range(3)
    ]

    @pl.when(first)
    def _():
        for group in copies:
            start_all(group)
        start_all(down_copies)
        start_all(up_copies)
        start_all(out_copies)
        sums[...] = jnp.zeros_like(sums)
        up_sums[...] = jnp.zeros_like(up_sums)
        for group in copies:
            wait_all(group)
        wait_all(down_copies)
        wait_all(up_copies)
        wait_all(out_copies)

    width = gm.shape[1]
    chunks = [slice(c * width, (c + 1) * width) for c in range(up_weight.shape[0] // width)]
    for part in range(gm.shape[0] // SUB):
        rows = slice(part * SUB, (part + 1) * SUB)
        grad = gm[rows, :]
        for w in range(3):
            grad = grad + dot_nn(grads[w, rows, :], weights[w])
        unit, rstd = normalize(combined[rows, :])
        sums[0] += partial_sum(grad * unit)
        sums[1] += partial_sum(grad)
        grad = normalize_back(grad, vecs[G2 : G2 + 1, :], unit, rstd)
        first_unit, first_rstd = normalize(mixed[rows, :])
        feed_back_rows(
            rows, chunks, grad, slope, first_unit, first_rstd, vecs, down_weight, up_weight, out_weight,
            gb_out, gu_out, ga_out, gm_out, gctx_out, sums, up_sums,
        )


def lower(core, grads, gm, combined, slope, mixed, vecs, down_weight, up_weight, out_weight, qkv):
    count, width = mixed.shape
    wide = slope.shape[1]
    tile = pl.BlockSpec((TILE, width), lambda i: (i, 0))
    broad = pl.BlockSpec((TILE, wide), lambda i: (i, 0))
    low = jax.ShapeDtypeStruct((count, width), bf16)
    return pl.pallas_call(
        lower_kernel,
        grid=(count // TILE,),
        in_specs=[SMEM, pl.BlockSpec((3, TILE, width), lambda i: (0, i, 0)), tile, tile, broad, tile,
                  whole((8, width))] + [ANY] * 8,
        out_specs=[tile, broad, tile, tile, tile, whole((6, 8, width)), whole((8, wide))],
        out_shape=[low, jax.ShapeDtypeStruct((count, wide), bf16), low, jax.ShapeDtypeStruct((count, width), f32), low,
                   jax.ShapeDtypeStruct((6, 8, width), f32), jax.ShapeDtypeStruct((8, wide), f32)],
        scratch_shapes=[
            pltpu.VMEM((width, wide), bf16),
            pltpu.VMEM((wide, width), bf16),
            pltpu.VMEM((width, width), bf16),
            pltpu.VMEM((3, width, width), bf16),
            pltpu.SemaphoreType.DMA((6, 8)),
        ],
        compiler_params=params(),
        cost_estimate=pl.CostEstimate(
            flops=2 * count * width * (4 * width + 2 * wide),
            bytes_accessed=count * (width * 30 + wide * 4), transcendentals=0),
        name="lower",
    )(core, grads, gm, combined, slope, mixed, vecs, *down_weight, *up_weight, *out_weight, *qkv)


def attend_back_kernel(
    q, k, v, gctx, lse, seg_col, alive_col, seg_row, *rest
):
    grads, sums, mask = rest[-3:]

    @pl.when(pl.program_id(1) == 0)
    def _():
        mask_into(mask, seg_col, alive_col, seg_row)

    length = q.shape[0]
    lane = lax.broadcasted_iota(jnp.int32, (length, 2 * HEAD), 1)
    scaling = HEAD**-0.5
    for pair in range(2):
        cols = slice(pair * 2 * HEAD, (pair + 1) * 2 * HEAD)
        kp, vp, go = k[:, cols], v[:, cols], gctx[:, cols]
        qp = q[:, cols] * bf16(scaling)
        kt = kp.T
        dq_parts = []
        dk = dv = None
        for h in range(2):
            here = (lane >= HEAD) if h else (lane < HEAD)
            zero = bf16(0)
            qm, gm = jnp.where(here, qp, zero), jnp.where(here, go, zero)
            scores = dot_nt(kp, qm) + mask[...]
            probs = jnp.exp(scores - lse[0, 0, pl.ds(2 * pair + h, 1), :])
            weighted = probs * dot_nt(vp, gm)
            inner = jnp.sum(weighted, axis=0, keepdims=True)
            grad_scores = (weighted - probs * inner).astype(bf16)
            dv_h = dot_nn(probs.astype(bf16), gm)
            dk_h = dot_nn(grad_scores, qm)
            dv = dv_h if dv is None else dv + dv_h
            dk = dk_h if dk is None else dk + dk_h
            dq_parts.append(dot_nn(kt[h * HEAD : (h + 1) * HEAD], grad_scores))
        dq = (jnp.concatenate(dq_parts, axis=0).T * scaling).astype(bf16)
        dv = dv.astype(bf16)
        grads[0, :, cols] = dq
        grads[1, :, cols] = dk.astype(bf16)
        grads[2, :, cols] = dv
        sums[0, 0, :, cols] = partial_sum(dq.astype(f32))
        sums[0, 1, :, cols] = partial_sum(dv.astype(f32))


def attend_back(q, k, v, gctx, lse, seg_col, alive_col, seg_row, start=0, stop=None, before=()):
    count, width = q.shape
    rows, _, length = seg_row.shape
    stop = rows if stop is None else stop
    col = pl.BlockSpec((length, 128), lambda r, j: (r + start, 0))
    block = pl.BlockSpec((length, QUAD), lambda r, j: (r + start, j))
    share = (stop - start) / rows
    return pl.pallas_call(
        attend_back_kernel,
        grid=(stop - start, width // QUAD),
        in_specs=[block] * 4 + [pl.BlockSpec((1, 1, 8, length), lambda r, j: (r + start, j, 0, 0)), col, col,
                                pl.BlockSpec((1, 1, length), lambda r, j: (r + start, 0, 0))] + [ANY] * len(before),
        out_specs=[pl.BlockSpec((3, length, QUAD), lambda r, j: (0, r + start, j)),
                   pl.BlockSpec((1, 2, 8, QUAD), lambda r, j: (r + start, 0, 0, j))],
        out_shape=[jax.ShapeDtypeStruct((3, count, width), bf16), jax.ShapeDtypeStruct((rows, 2, 8, width), f32)],
        scratch_shapes=[pltpu.VMEM((length, length), f32)],
        input_output_aliases={8 + i: i for i in range(len(before))},
        compiler_params=params(),
        cost_estimate=pl.CostEstimate(
            flops=int(share * 4 * 10 * count * length * width),
            bytes_accessed=int(share * count * width * 16), transcendentals=0),
        name="attend_back",
    )(q, k, v, gctx, lse, seg_col, alive_col, seg_row, *before)


def input_back_kernel(core_ref, grads, gm, own, sib, grad_out, weights, sems):
    core = core_ref[0]
    copies = [
        piece_copies(core, (own, sib), weights.at[w], sems.at[w], w)
        for w in range(3)
    ]

    @pl.when(pl.program_id(0) == 0)
    def _():
        for group in copies:
            start_all(group)
        for group in copies:
            wait_all(group)

    grad = gm[...]
    for w in range(3):
        grad = grad + dot_nn(grads[w], weights[w])
    grad_out[...] = grad


def input_back(core, grads, gm, qkv):
    count, width = gm.shape
    tile = pl.BlockSpec((TILE, width), lambda i: (i, 0))
    return pl.pallas_call(
        input_back_kernel,
        grid=(count // TILE,),
        in_specs=[SMEM, pl.BlockSpec((3, TILE, width), lambda i: (0, i, 0)), tile] + [ANY] * 2,
        out_specs=tile,
        out_shape=jax.ShapeDtypeStruct((count, width), f32),
        scratch_shapes=[pltpu.VMEM((3, width, width), bf16), pltpu.SemaphoreType.DMA((3, 8))],
        compiler_params=params(),
        cost_estimate=pl.CostEstimate(
            flops=2 * count * width * width * 3, bytes_accessed=count * width * 14, transcendentals=0),
        name="input_back",
    )(core, grads, gm, *qkv)


def weight_grad_kernel(layers, place_ref, *refs):
    grads, inputs = refs[:layers], refs[layers : 2 * layers]
    keep, send, turned = refs[2 * layers :]
    core, flip = place_ref[0], place_ref[1]
    rows = turned.shape[0] // 4
    span = grads[0].shape[-2]

    @pl.when(pl.program_id(1) == 0)
    def _():
        for layer in range(layers):
            flat = grads[layer][0].T
            for block in range(4):
                x, c = block // 2, block % 2
                slot = 2 * ((x + flip) % 2) + (c + core) % 2
                turned[pl.ds(pl.multiple_of(slot * rows, rows), rows), layer * span : (layer + 1) * span] = (
                    flat[block * rows : (block + 1) * rows]
                )

    total = None
    for layer in range(layers):
        term = dot_nn(turned[:, layer * span : (layer + 1) * span], inputs[layer][...])
        total = term if total is None else total + term
    total = total.astype(bf16)
    halves = keep.shape[1]
    wide = keep.shape[-1]
    for half in range(halves):
        for x in range(2):
            for c, out in ((0, keep), (1, send)):
                start = (2 * x + c) * rows
                out[0, half, x] = total[start : start + rows, half * wide : (half + 1) * wide]


def weight_grad(place, grads, inputs):
    layers = len(grads)
    count_w, span, n = grads[0].shape
    depth = inputs[0].shape[1]
    chunk = min(depth, n)
    chunks = depth // chunk
    halves = 2 if chunks == 1 else 1
    wide = chunk // halves
    per_half = depth // 2 // wide
    rows = n // 4
    if chunks == 1:
        out_spec = pl.BlockSpec((1, 2, 2, rows, wide), lambda w, j: (w, 0, 0, 0, 0))
    else:
        out_spec = pl.BlockSpec((1, 1, 2, rows, wide), lambda w, j: (w, j // per_half, 0, 0, j % per_half))
    out = jax.ShapeDtypeStruct((count_w, 2, 2, rows, depth // 2), bf16)
    return pl.pallas_call(
        partial(weight_grad_kernel, layers),
        grid=(count_w, chunks),
        in_specs=[SMEM] + [pl.BlockSpec((1, span, n), lambda w, j: (w, 0, 0))] * layers
        + [pl.BlockSpec((span, chunk), lambda w, j: (0, j))] * layers,
        out_specs=[out_spec, out_spec],
        out_shape=[out, out],
        scratch_shapes=[pltpu.VMEM((n, layers * span), bf16)],
        compiler_params=params(),
        cost_estimate=pl.CostEstimate(
            flops=2 * layers * span * n * depth * count_w,
            bytes_accessed=2 * layers * span * (n * count_w + depth) + 2 * n * depth * count_w, transcendentals=0),
        name="weight_grad",
    )(place, *grads, *inputs)


def joint_grad_kernel(layers, small, tall, place_ref, *refs):
    grads, inputs = refs[:layers], refs[layers : 2 * layers]
    bias_sums, norm_sums, up_sums = (refs[(2 + i) * layers : (3 + i) * layers] for i in range(3))
    keep, send, turned, totals, short = refs[5 * layers :]
    core, flip = place_ref[0], place_ref[1]
    which = pl.program_id(0)
    sides, _, blocks, _, half = keep.shape
    width = turned.shape[0]
    rows = width // 4
    span = inputs[0].shape[0]

    def slot(block):
        return 2 * ((block // 2 + flip) % 2) + (block % 2 + core) % 2

    for layer in range(layers):
        flat = grads[layer][0].T
        for block in range(4):
            turned[pl.ds(pl.multiple_of(slot(block) * rows, rows), rows), layer * span : (layer + 1) * span] = (
                flat[block * rows : (block + 1) * rows]
            )
    total = None
    for layer in range(layers):
        term = dot_nn(turned[:, layer * span : (layer + 1) * span], inputs[layer][...])
        total = term if total is None else total + term
    totals[which] = total

    @pl.when(which == 0)
    def _():
        bias = sum(jnp.sum(ref[...], axis=(0, 2)) for ref in bias_sums)
        norm = sum(jnp.sum(ref[...], axis=1) for ref in norm_sums)
        up = sum(jnp.sum(ref[...], axis=0, keepdims=True) for ref in up_sums)
        rest = [norm[n : n + 1] for n in (5, 3, 4, 2, 0, 1)]
        lines = jnp.concatenate([bias[0:1], bias[1:2], *rest], axis=0)
        short[...] = jnp.zeros_like(short)
        quarter = up.shape[1] // 4
        for block in range(4):
            place = slot(block)
            here = pltpu.roll(lines, lax.rem(width - place * rows, width), 1)
            above = jnp.where(place == 0, up[:, :quarter], 0.0)
            for index in range(1, 4):
                above = above + jnp.where(place == index, up[:, index * quarter : (index + 1) * quarter], 0.0)
            above = jnp.broadcast_to(above, (8, quarter))
            for zy in range(blocks):
                first = pltpu.roll(here, (width - zy * small) % width, 1)[:, :128]
                second = pltpu.roll(above, (quarter - zy * tall) % quarter, 1)[:, :128]
                short[block, zy, :, 0:128] = first
                short[block, zy, :, 128:256] = second

    @pl.when(which == pl.num_programs(0) - 1)
    def _():
        for block in range(4):
            out = (keep, send)[block % 2]
            for zy in range(blocks):
                start = block * rows + zy * small
                for side in range(sides):
                    cols = slice(side * half, (side + 1) * half)
                    parts = [totals[w, start : start + small, cols] for w in range(totals.shape[0])]
                    out[side, block // 2, zy] = jnp.concatenate([*parts, short[block, zy, :, cols]], axis=0).astype(bf16)


def joint_grad(place, grads, inputs, bias_sums, norm_sums, up_sums, small, tall):
    layers = len(grads)
    count, span, n = grads[0].shape
    depth = inputs[0].shape[1]
    blocks = n // 4 // small
    lines = count * small + 8
    out = jax.ShapeDtypeStruct((2, 2, blocks, lines, depth // 2), bf16)
    sums = [*bias_sums, *norm_sums, *up_sums]
    return pl.pallas_call(
        partial(joint_grad_kernel, layers, small, tall),
        grid=(count,),
        in_specs=[SMEM] + [pl.BlockSpec((1, span, n), lambda w: (w, 0, 0))] * layers + [whole((span, depth))] * layers
        + [whole(v.shape) for v in sums],
        out_specs=[whole(out.shape)] * 2,
        out_shape=[out, out],
        scratch_shapes=[
            pltpu.VMEM((n, layers * span), bf16),
            pltpu.VMEM((count, n, depth), f32),
            pltpu.VMEM((4, blocks, 8, depth), f32),
        ],
        compiler_params=params(),
        cost_estimate=pl.CostEstimate(
            flops=2 * layers * span * n * depth * count,
            bytes_accessed=2 * layers * span * (n * count + depth) + 2 * n * depth * count, transcendentals=0),
        name="joint_grad",
    )(place, *grads, *inputs, *sums)


def tall_grad_kernel(layers, place_ref, *refs):
    tall, tall_in, flat, flat_in = (refs[i * layers : (i + 1) * layers] for i in range(4))
    keep, send, turned, flat_total = refs[4 * layers :]
    step = pl.program_id(0)
    core, flip = place_ref[0], place_ref[1]
    sides, _, blocks, rows, half = keep.shape
    flat_rows = flat_total.shape[0] // 4
    small = flat_rows // blocks
    large = rows - small

    def product(left, right):
        total = None
        for layer in range(layers):
            term = dot_nn(left[layer][...].T, right[layer][...])
            total = term if total is None else total + term
        return total

    @pl.when(step == 0)
    def _():
        total = product(flat, flat_in)
        for block in range(4):
            slot = 2 * ((block // 2 + flip) % 2) + (block % 2 + core) % 2
            flat_total[pl.ds(pl.multiple_of(slot * flat_rows, flat_rows), flat_rows), :] = (
                total[block * flat_rows : (block + 1) * flat_rows]
            )

    @pl.when(step > 0)
    def _():
        turned[...] = product(tall, tall_in).astype(bf16)
        slot = step - 1
        for c, out in ((0, keep), (1, send)):
            @pl.when(slot % 2 == c)
            def _():
                for side in range(sides):
                    cols = slice(side * half, (side + 1) * half)
                    for block in range(blocks):
                        out[side, 0, block, :large, :] = turned[block * large : (block + 1) * large, cols]
                        start = pl.multiple_of(slot * flat_rows + block * small, 8)
                        out[side, 0, block, large:, :] = flat_total[pl.ds(start, small), cols].astype(bf16)


def tall_grad(place, tall, tall_in, flat, flat_in):
    layers = len(tall)
    span, n = tall[0].shape
    depth = tall_in[0].shape[1]
    flat_n = flat[0].shape[1]
    rows = n // 4

    def column(s, place):
        slot = jnp.maximum(s - 1, 0)
        return 0, 2 * ((slot // 2 + place[1]) % 2) + (slot % 2 + place[0]) % 2

    def fixed(shape):
        return pl.BlockSpec(shape, lambda s, place: (0, 0))

    blocks = 8
    share = (n + flat_n) // 4 // blocks
    out_spec = pl.BlockSpec(
        (2, 1, blocks, share, depth // 2), lambda s, place: (0, jnp.maximum(s - 1, 0) // 2, 0, 0, 0)
    )
    out = jax.ShapeDtypeStruct((2, 2, blocks, share, depth // 2), bf16)
    return pl.pallas_call(
        partial(tall_grad_kernel, layers),
        grid_spec=pltpu.PrefetchScalarGridSpec(
            num_scalar_prefetch=1,
            grid=(5,),
            in_specs=[pl.BlockSpec((span, rows), column)] * layers + [fixed((span, depth))] * layers
            + [fixed((span, flat_n))] * layers + [fixed((span, depth))] * layers,
            out_specs=[out_spec, out_spec],
            scratch_shapes=[pltpu.VMEM((rows, depth), bf16), pltpu.VMEM((flat_n, depth), f32)],
        ),
        out_shape=[out, out],
        compiler_params=params(),
        cost_estimate=pl.CostEstimate(
            flops=2 * layers * span * (n + flat_n) * depth,
            bytes_accessed=2 * layers * span * (n + flat_n + 2 * depth) + 2 * (n + flat_n) * depth, transcendentals=0),
        name="tall_grad",
    )(place, *tall, *tall_in, *flat, *flat_in)


def pack_kernel(weights, *refs):
    parts, out, rows = refs[:-2], refs[-2], refs[-1]
    rows[...] = jnp.zeros_like(rows)
    start = 0
    for part in parts[:weights]:
        rows[start : start + part.shape[0], :] = part[...].astype(f32)
        start += part.shape[0]
    for index, part in enumerate(parts[weights:-1]):
        rows[start + index : start + index + 1, : part.shape[1]] = part[...].astype(f32)
    rows[start : start + 1, 128 : 128 + parts[-1].shape[1]] = parts[-1][...].astype(f32)
    out[...] = rows[...].astype(bf16)


def pack(vectors, weights=()):
    parts = [*weights, *(vector[None] for vector in vectors)]
    shape = (sum(weight.shape[0] for weight in weights) + 8, weights[0].shape[1] if weights else 256)
    return pl.pallas_call(
        partial(pack_kernel, len(weights)),
        in_specs=[whole(part.shape) for part in parts],
        out_specs=whole(shape),
        out_shape=jax.ShapeDtypeStruct(shape, bf16),
        scratch_shapes=[pltpu.VMEM(shape, f32)],
        name="pack",
    )(*parts)


AXES = ("dp", "fsdp")


def halves(v):
    middle = v.shape[-1] // 2
    return v[..., :middle], v[..., middle:]


def tie(value, after):
    return value if after is None else lax.optimization_barrier((value, after))[0]


class Chain:
    def __init__(self, stages):
        self.stages, self.result, self.landed = stages, None, None
        self.step()

    def step(self, after=None):
        if self.stages is None:
            return self.landed
        try:
            self.landed = self.stages.send(after) if self.landed is not None else next(self.stages)
        except StopIteration as end:
            self.result = end.value
            self.stages = None
        return self.landed

    def finish(self, after=None):
        while self.stages is not None:
            self.step(after)
        return self.result


class Plain:
    def __init__(self, mesh):
        self.devices = math.prod(mesh.shape.values())

    def place(self):
        return jnp.zeros((2,), jnp.int32)

    def spread(self, shards, vectors=None):
        def pieces(full):
            blocks = full.reshape(full.shape[:-2] + (2, 2, full.shape[-2] // 4, full.shape[-1]))
            return tuple(jnp.stack(halves(blocks[..., core, :, :]), axis=-4) for core in range(2))

        full = [lax.all_gather(shard, AXES, axis=0, tiled=True) for shard in shards]
        yield full[0]
        if vectors is None:
            return [pieces(weight) for weight in full]
        return pieces(jnp.stack(full)), lax.all_gather(pack(vectors), AXES, axis=0, tiled=False)

    def reduce(self, keep, send):
        count, sides, xs, rows, half = keep.shape
        both = jnp.stack([keep, send], axis=3).astype(f32)
        full = jnp.moveaxis(both, 1, 4).reshape(count, xs * 2 * rows, sides * half)
        full = lax.psum_scatter(full, AXES, scatter_dimension=1, tiled=True)
        yield full
        return full

    def reduce_joined(self, keep, send, tall, flat):
        large = keep.shape[3] * tall // (tall + flat)
        results = []
        for rows in (slice(0, large), slice(large, None)):
            sides, xs, half = keep.shape[0], keep.shape[1], keep.shape[-1]
            parts = [v[:, :, :, rows].reshape(1, sides, xs, -1, half) for v in (keep, send)]
            results.append(Chain(self.reduce(*parts)).finish())
        yield results[0]
        return jnp.concatenate(results, axis=1)

    def joint_grad(self, place, grads, inputs, bias_sums, norm_sums, up_sums, small, tall):
        bias = sum(jnp.sum(v, axis=(0, 2)) for v in bias_sums)
        norm = sum(jnp.sum(v, axis=1) for v in norm_sums)
        up = sum(jnp.sum(v, axis=0) for v in up_sums)
        lines = jnp.stack([bias[0], bias[1], norm[5], norm[3], norm[4], norm[2], norm[0], norm[1]])
        lines = lines.reshape(8, self.devices, small).transpose(1, 0, 2)
        return (*weight_grad(place, grads, inputs), lines, up.reshape(self.devices, tall))

    def reduce_joint(self, keep, send, lines, up):
        full = Chain(self.reduce(keep, send)).finish()
        lines = lax.psum_scatter(lines, AXES, scatter_dimension=0, tiled=True)[0]
        up = lax.psum_scatter(up, AXES, scatter_dimension=0, tiled=True)
        rows = full.reshape(-1, full.shape[-1])
        yield rows
        short = jnp.zeros((8, full.shape[-1]), f32).at[:, : lines.shape[1]].set(lines).at[:1, 128 : 128 + up.shape[1]].set(up)
        return jnp.concatenate([rows, short], axis=0)


class Grid:
    def __init__(self, mesh):
        pass

    def where(self):
        dp, fsdp = lax.axis_index("dp"), lax.axis_index("fsdp")
        return dp // 2, dp % 2, fsdp // 2, fsdp % 2

    def place(self):
        x, core, _, _ = self.where()
        return jnp.stack([core, x]).astype(jnp.int32)

    def swap(self, value, x=0, core=0, z=0, y=0):
        flip = ((x * 2 + core) * 4 + z) * 2 + y
        return lax.ppermute(value, AXES, [(i, i ^ flip) for i in range(32)])

    def ordered(self, mine, other, side, axis=0):
        return jnp.stack([jnp.where(side == 0, mine, other), jnp.where(side == 0, other, mine)], axis=axis)

    def ordered_z(self, parts, z):
        odd, high = z % 2, z // 2
        parts = [jnp.where(odd == 0, parts[k], parts[k ^ 1]) for k in range(4)]
        return jnp.stack([jnp.where(high == 0, parts[k], parts[k ^ 2]) for k in range(4)])

    def spread(self, shards, vectors=None):
        x, core, z, y = self.where()
        if vectors is not None:
            payload = pack(vectors, shards)
        else:
            payload = jnp.concatenate(shards, axis=0) if len(shards) > 1 else shards[0]
        parts = [payload] + [self.swap(payload, z=k) for k in range(1, 4)]
        parts = tie(parts, (yield parts[1:]))
        left, right = halves(self.ordered_z(parts, z))
        got = self.swap(left, x=1), self.swap(right, y=1)
        got = tie(got, (yield got))
        left = self.ordered(left, got[0], x)
        right = self.ordered(right, got[1], y, axis=1)
        got = self.swap(left, y=1), self.swap(right, x=1)
        got = tie(got, (yield got))
        left = self.ordered(left, got[0], y, axis=2)
        right = self.ordered(right, got[1], x)
        own, start = [], 0
        for shard in shards:
            rows = shard.shape[0]
            own.append(jnp.stack([v[:, :, :, start : start + rows].reshape(2, 8 * rows, -1) for v in (left, right)]))
            start += rows
        if vectors is not None:
            own = [jnp.stack(own), left[:, :, :, start:, :256]]
        other = [self.swap(mine, core=1) for mine in own]
        other = tie(other, (yield other))
        if vectors is None:
            return list(zip(own, other))
        vectors = self.ordered(own[1], other[1], core, axis=1)
        return (own[0], other[0]), vectors.reshape(32, 8, 256)

    def reduce(self, keep, send):
        _, _, z, y = self.where()
        count, _, _, rows, half = keep.shape
        mine = rows // 8

        def add(a, b):
            return (a.astype(f32) + b.astype(f32)).astype(bf16)

        def pick(v, index, axis):
            return lax.dynamic_index_in_dim(v, index, axis, keepdims=False)

        got = self.swap(send, core=1)
        got = tie(got, (yield got))
        total = add(keep, got).reshape(count, 2, 2, 4, 2, mine, half)
        left, right = total[:, 0], total[:, 1]
        got = self.swap(left[:, 1], x=1), self.swap(pick(right, 1 - y, 3), y=1)
        got = tie(got, (yield got))
        left, right = add(left[:, 0], got[0]), add(pick(right, y, 3), got[1])
        got = self.swap(pick(left, 1 - y, 2), y=1), self.swap(right[:, 1], x=1)
        got = tie(got, (yield got))
        left, right = add(pick(left, y, 2), got[0]), add(right[:, 0], got[1])
        both = jnp.concatenate([left, right], axis=-1)
        got = [self.swap(pick(both, z ^ k, 1), z=k) for k in range(1, 4)]
        got = tie(got, (yield got))
        result = pick(both, z, 1).astype(f32)
        for part in got:
            result = result + part.astype(f32)
        return result

    def reduce_joined(self, keep, send, tall, flat):
        shape = (1, 2, 2, -1, keep.shape[-1])
        return self.reduce(keep.reshape(shape), send.reshape(shape))

    def joint_grad(self, *operands):
        return joint_grad(*operands)

    def reduce_joint(self, keep, send):
        shape = (1, 2, 2, -1, keep.shape[-1])
        result = yield from self.reduce(keep.reshape(shape), send.reshape(shape))
        return result[0]


def column_info(values, count):
    return jnp.broadcast_to(values.reshape(count, 1), (count, 128))


def body(
    exchange,
    tokens,
    cotangent,
    segment_ids,
    pad_mask,
    row_counts,
    query_weight,
    query_bias,
    key_weight,
    value_weight,
    value_bias,
    out_weight,
    out_bias,
    first_gain,
    first_shift,
    up_weight,
    up_bias,
    down_weight,
    down_bias,
    second_gain,
    second_shift,
):
    rows_here, row_len, width = tokens.shape
    count = rows_here * row_len
    small, tall = query_bias.shape[0], up_bias.shape[0]
    place = exchange.place()

    first = Chain(
        exchange.spread(
            [query_weight, key_weight, value_weight],
            [query_bias, value_bias, out_bias, first_gain, first_shift, down_bias, second_gain, second_shift, up_bias],
        )
    )
    z_landed = first.landed
    first.step()
    second = Chain(exchange.spread(tie([out_weight, up_weight], z_landed)))
    first.step()
    xy_landed = first.landed
    first.step()
    second.step(xy_landed)
    qkv, vectors = first.finish()
    vectors = vectors.astype(f32)
    devices = vectors.shape[0]
    wide = tall * devices
    vecs = vectors[:, :, :small].transpose(1, 0, 2).reshape(8, width)
    up_vec = jnp.broadcast_to(vectors[:, 0, 128 : 128 + tall].reshape(1, wide), (8, wide))

    present = (jnp.arange(rows_here, dtype=jnp.int32) < row_counts[0]).astype(jnp.int32)
    alive = pad_mask * present[:, None]
    alive_col = column_info(alive, count)
    seg_col = column_info(segment_ids, count)
    seg_row = segment_ids.reshape(rows_here, 1, row_len)
    info = (seg_col, alive_col, seg_row)
    flat = tokens.reshape(count, width)

    landed = second.landed
    second.step()
    third = Chain(exchange.spread([tie(down_weight, landed)]))
    lower_kept = attend_forward(place, tie(flat, landed), *info, vecs, qkv, 0, 1)
    third.step(lower_kept[3])
    lower_kept = attend_forward(place, flat, *info, vecs, qkv, 1, rows_here, lower_kept)
    second.step(lower_kept[3])
    third.step(lower_kept[3])
    out_w, up_w = second.finish()
    mixed, lower_low, lower_act, slope = widen(place, lower_kept[3], flat, vecs, up_vec, out_w, up_w)
    third.step(lower_low)
    (down_w,) = third.finish()
    combined, inputs = narrow(place, lower_act, mixed, vecs, down_w)

    upper_kept = attend_forward(place, inputs, *info, vecs, qkv)
    outputs, upper_low, upper_act, upper_gb, upper_gu, upper_ga, gm, gctx, sums, up_sums = top(
        place, upper_kept[3], combined, cotangent.reshape(count, width), alive_col, vecs, up_vec, out_w, up_w, down_w
    )
    upper_grads, bias_sums = attend_back(*upper_kept[:3], gctx, upper_kept[4], *info)
    lower_gb, lower_gu, lower_ga, gm, gctx, more_sums, more_up_sums = lower(
        place, upper_grads, gm, combined, slope, mixed, vecs, down_w, up_w, out_w, qkv
    )

    keep, send = weight_grad(place, [upper_gb[None], lower_gb[None]], [upper_act, lower_act])
    down_sum = Chain(exchange.reduce(keep, send))
    keep, send = tall_grad(
        place, [upper_gu, tie(lower_gu, keep)], [upper_low, lower_low], [upper_ga, lower_ga], [upper_kept[3], lower_kept[3]]
    )
    up_sum = Chain(exchange.reduce_joined(keep, send, tall, small))
    landed = down_sum.landed
    down_sum.step()
    part = attend_back(*lower_kept[:3], tie(gctx, (keep, landed)), lower_kept[4], *info, 0, 1)
    landed = (down_sum.landed, up_sum.landed)
    down_sum.step()
    up_sum.step()
    lower_grads, more_bias_sums = attend_back(
        *lower_kept[:3], tie(gctx, landed), lower_kept[4], *info, 1, rows_here, part
    )
    landed = (down_sum.landed, up_sum.landed)
    down_sum.step()
    up_sum.step()
    joint = exchange.joint_grad(
        place, [upper_grads, tie(lower_grads, landed)], [inputs, flat],
        [bias_sums, more_bias_sums], [sums, more_sums], [up_sums, more_up_sums], small, tall,
    )
    qkv_sum = Chain(exchange.reduce_joint(*joint))
    landed = (down_sum.landed, up_sum.landed)
    up_sum.step()
    tokens_grad = input_back(place, tie(lower_grads, (joint[0], landed)), gm, qkv)
    qkv_sum.step(tokens_grad)
    up_out = up_sum.finish()[0]
    joint = qkv_sum.finish()
    query_grad, key_grad, value_grad = (joint[i * small : (i + 1) * small] for i in range(3))
    lines = joint[3 * small :]
    piece = [lines[i, :small] for i in range(8)]
    return (
        outputs.reshape(rows_here, row_len, width),
        tokens_grad.reshape(rows_here, row_len, width),
        query_grad,
        piece[QB],
        key_grad,
        value_grad,
        piece[VB],
        up_out[tall:],
        piece[OB],
        piece[G1],
        piece[S1],
        up_out[:tall],
        lines[0, 128 : 128 + tall],
        down_sum.finish()[0],
        piece[DB],
        piece[G2],
        piece[S2],
    )


def solution(mesh):
    rows = P(AXES, None, None)
    flat = P(AXES, None)
    line = P(AXES)
    matrices = (flat, line, flat, flat, line, flat, line, line, line, flat, line, flat, line, line, line)
    exchange = Grid(mesh) if dict(mesh.shape) == {"dp": 4, "fsdp": 8} else Plain(mesh)
    return jax.shard_map(
        partial(body, exchange),
        mesh=mesh,
        in_specs=(rows, rows, flat, flat, line) + matrices,
        out_specs=(rows, rows) + matrices,
        check_vma=False,
    )
```

```python
from functools import partial
import math

import jax
import jax.numpy as jnp
from jax import lax
from jax.experimental import pallas as pl
from jax.experimental.pallas import tpu as pltpu
from jax.sharding import PartitionSpec as P

HEAD = 64
LAYERS = 2
QUAD = 4 * HEAD
TILE = 256
SUB = 256
norm_eps = 1e-06
masked_score = -1000000000.0
VMEM = 60 * 1024 * 1024
bf16 = jnp.bfloat16
f32 = jnp.float32

QB, VB, OB, G1, S1, DB, G2, S2 = range(8)


def dot_nt(left, right):
    return lax.dot_general(left, right, (((1,), (1,)), ((), ())), preferred_element_type=f32)


def dot_nn(left, right):
    return lax.dot_general(left, right, (((1,), (0,)), ((), ())), preferred_element_type=f32)


def dot_tn(left, right):
    return lax.dot_general(left, right, (((0,), (0,)), ((), ())), preferred_element_type=f32)


def normalize(v):
    mean = jnp.mean(v, axis=-1, keepdims=True)
    centered = v - mean
    rstd = lax.rsqrt(jnp.mean(centered * centered, axis=-1, keepdims=True) + norm_eps)
    return centered * rstd, rstd


def normalize_back(grad, gain, unit, rstd):
    scaled = grad * gain
    first = jnp.mean(scaled, axis=-1, keepdims=True)
    second = jnp.mean(scaled * unit, axis=-1, keepdims=True)
    return rstd * (scaled - first - unit * second)


def partial_sum(v):
    return jnp.sum(v.reshape(v.shape[0] // 8, 8, v.shape[1]), axis=0)


def piece_copies(core, pieces, place, sems, which=None):
    copies = []
    for sibling, piece in enumerate(pieces):
        source = piece if which is None else piece.at[which]
        if len(source.shape) == 2:
            rows = source.shape[0] // 2
            part = slice(sibling * rows, (sibling + 1) * rows)
            copies.append(pltpu.make_async_copy(source.at[part, :], place.at[part, :], sems.at[4 * sibling]))
            continue
        sides, _, rows, half = source.shape
        for side in range(sides):
            for x in range(2):
                slot = 2 * x + (1 - core if sibling else core)
                start = pl.multiple_of(slot * rows, rows)
                copies.append(
                    pltpu.make_async_copy(
                        source.at[side, x],
                        place.at[pl.ds(start, rows), pl.ds(side * half, half)],
                        sems.at[4 * sibling + 2 * side + x],
                    )
                )
    return copies


def start_all(copies):
    for copy in copies:
        copy.start()


def wait_all(copies):
    for copy in copies:
        copy.wait()


def params():
    return pltpu.CompilerParams(vmem_limit_bytes=VMEM)


ANY = pl.BlockSpec(memory_space=pl.ANY)
SMEM = pl.BlockSpec(memory_space=pltpu.SMEM)


def whole(shape):
    return pl.BlockSpec(shape, lambda *_: (0,) * len(shape))


def mask_into(mask, seg_col, alive_col, seg_row):
    length = mask.shape[0]
    key = lax.broadcasted_iota(jnp.int32, (length, length), 0)
    query = lax.broadcasted_iota(jnp.int32, (length, length), 1)
    same = seg_col[:, 0:1] == seg_row[0]
    allowed = same & ((alive_col[:, 0:1] > 0) | (key == query))
    mask[...] = jnp.where(allowed, 0.0, masked_score)


def attend_forward_kernel(
    core_ref, x, seg_col, alive_col, seg_row, vecs, own, sib, *rest
):
    q_out, k_out, v_out, ctx_out, lse_out, weights, mask, sems = rest[-8:]
    row, quad = pl.program_id(0), pl.program_id(1)
    core = core_ref[0]
    first = (row == 0) & (quad == 0)
    copies = [
        piece_copies(core, (own, sib), weights.at[w], sems.at[w], w)
        for w in range(3)
    ]

    @pl.when(first)
    def _():
        for group in copies:
            start_all(group)

    @pl.when(quad == 0)
    def _():
        mask_into(mask, seg_col, alive_col, seg_row)

    @pl.when(first)
    def _():
        for group in copies:
            wait_all(group)

    inputs = x[...]
    heads = pl.ds(pl.multiple_of(quad * QUAD, QUAD), QUAD)
    queries = (dot_nt(inputs, weights[0, heads, :]) + vecs[QB : QB + 1, :]).astype(bf16)
    keys = dot_nt(inputs, weights[1, heads, :]).astype(bf16)
    values = (dot_nt(inputs, weights[2, heads, :]) + vecs[VB : VB + 1, :]).astype(bf16)
    q_out[...] = queries
    k_out[...] = keys
    v_out[...] = values
    scaled = queries * bf16(HEAD**-0.5)
    length = inputs.shape[0]
    lane = lax.broadcasted_iota(jnp.int32, (length, 2 * HEAD), 1)
    for pair in range(2):
        cols = slice(pair * 2 * HEAD, (pair + 1) * 2 * HEAD)
        kp, qp = keys[:, cols], scaled[:, cols]
        vt = values[:, cols].T
        parts = []
        for h in range(2):
            km = jnp.where((lane >= HEAD) if h else (lane < HEAD), kp, bf16(0))
            scores = dot_nt(km, qp) + mask[...]
            highest = jnp.max(scores, axis=0, keepdims=True)
            weight = jnp.exp(scores - highest)
            total = jnp.sum(weight, axis=0, keepdims=True)
            parts.append(dot_nn(vt[h * HEAD : (h + 1) * HEAD], weight.astype(bf16)) / total)
            lse_out[0, 0, pl.ds(2 * pair + h, 1), :] = highest + jnp.log(total)
        ctx_out[:, cols] = jnp.concatenate(parts, axis=0).T.astype(bf16)


def attend_forward(core, x, seg_col, alive_col, seg_row, vecs, qkv, start=0, stop=None, before=()):
    count, width = x.shape
    rows, _, length = seg_row.shape
    stop = rows if stop is None else stop
    quads = width // QUAD
    full = pl.BlockSpec((length, width), lambda r, j: (r + start, 0))
    col = pl.BlockSpec((length, 128), lambda r, j: (r + start, 0))
    block = pl.BlockSpec((length, QUAD), lambda r, j: (r + start, j))
    low = jax.ShapeDtypeStruct((count, width), bf16)
    share = (stop - start) / rows
    return pl.pallas_call(
        attend_forward_kernel,
        grid=(stop - start, quads),
        in_specs=[SMEM, full, col, col, pl.BlockSpec((1, 1, length), lambda r, j: (r + start, 0, 0)),
                  pl.BlockSpec((8, QUAD), lambda r, j: (0, j)), ANY, ANY] + [ANY] * len(before),
        out_specs=[block] * 4 + [pl.BlockSpec((1, 1, 8, length), lambda r, j: (r + start, j, 0, 0))],
        out_shape=[low] * 4 + [jax.ShapeDtypeStruct((rows, quads, 8, length), f32)],
        scratch_shapes=[
            pltpu.VMEM((3, width, width), bf16),
            pltpu.VMEM((length, length), f32),
            pltpu.SemaphoreType.DMA((3, 8)),
        ],
        input_output_aliases={8 + i: i for i in range(len(before))},
        compiler_params=params(),
        cost_estimate=pl.CostEstimate(
            flops=int(share * (2 * count * width * width * 3 + 4 * 4 * count * length * width)),
            bytes_accessed=int(share * count * width * 10) + 3 * width * width * 2, transcendentals=0),
        name="attend_forward",
    )(core, x, seg_col, alive_col, seg_row, vecs, *qkv, *before)


GELU_A = math.sqrt(2.0 / math.pi)
GELU_B = 0.044715


def gelu_both(u):
    square = u * u
    t = jnp.tanh(u * (GELU_A + (GELU_A * GELU_B) * square))
    half = 0.5 + 0.5 * t
    slope = half + (u * (1.0 - t * t)) * (0.5 * GELU_A + (1.5 * GELU_A * GELU_B) * square)
    return u * half, slope


def widen_kernel(
    core_ref, ctx, resid, vecs, up_bias, o_own, o_sib, u_own, u_sib,
    mixed_out, low_out, act_out, slope_out, out_weight, up_weight, sems,
):
    core = core_ref[0]
    first = pl.program_id(0) == 0
    out_copies = piece_copies(core, (o_own, o_sib), out_weight, sems.at[0])
    up_copies = piece_copies(core, (u_own, u_sib), up_weight, sems.at[1])

    @pl.when(first)
    def _():
        start_all(out_copies)
        start_all(up_copies)
        wait_all(out_copies)

    mixed = resid[...].astype(f32) + dot_nt(ctx[...], out_weight[...]) + vecs[OB : OB + 1, :]
    mixed_out[...] = mixed
    normed = normalize(mixed)[0] * vecs[G1 : G1 + 1, :] + vecs[S1 : S1 + 1, :]
    low = normed.astype(bf16)
    low_out[...] = low

    @pl.when(first)
    def _():
        wait_all(up_copies)

    width = low.shape[1]
    for chunk in range(up_weight.shape[0] // width):
        cols = slice(chunk * width, (chunk + 1) * width)
        upward = dot_nt(low, up_weight[cols, :]) + up_bias[0:1, cols]
        act, slope = gelu_both(upward)
        act_out[:, cols] = act.astype(bf16)
        slope_out[:, cols] = slope.astype(bf16)


def widen(core, ctx, resid, vecs, up_bias, out_weight, up_weight):
    count, width = ctx.shape
    wide = up_bias.shape[1]
    tile = pl.BlockSpec((TILE, width), lambda i: (i, 0))
    broad = pl.BlockSpec((TILE, wide), lambda i: (i, 0))
    return pl.pallas_call(
        widen_kernel,
        grid=(count // TILE,),
        in_specs=[SMEM, tile, tile, whole((8, width)), whole((8, wide))] + [ANY] * 4,
        out_specs=[tile, tile, broad, broad],
        out_shape=[
            jax.ShapeDtypeStruct((count, width), f32),
            jax.ShapeDtypeStruct((count, width), bf16),
            jax.ShapeDtypeStruct((count, wide), bf16),
            jax.ShapeDtypeStruct((count, wide), bf16),
        ],
        scratch_shapes=[
            pltpu.VMEM((width, width), bf16),
            pltpu.VMEM((wide, width), bf16),
            pltpu.SemaphoreType.DMA((2, 8)),
        ],
        compiler_params=params(),
        cost_estimate=pl.CostEstimate(
            flops=2 * count * width * (width + wide),
            bytes_accessed=count * (width * 12 + wide * 4), transcendentals=0),
        name="widen",
    )(core, ctx, resid, vecs, up_bias, *out_weight, *up_weight)


def narrow_kernel(core_ref, act, mixed, vecs, d_own, d_sib, combined_out, low_out, down_weight, sems):
    core = core_ref[0]
    copies = piece_copies(core, (d_own, d_sib), down_weight, sems)

    @pl.when(pl.program_id(0) == 0)
    def _():
        start_all(copies)
        wait_all(copies)

    normed = normalize(mixed[...])[0] * vecs[G1 : G1 + 1, :] + vecs[S1 : S1 + 1, :]
    combined = normed + dot_nt(act[...], down_weight[...]) + vecs[DB : DB + 1, :]
    combined_out[...] = combined
    hidden = normalize(combined)[0] * vecs[G2 : G2 + 1, :] + vecs[S2 : S2 + 1, :]
    low_out[...] = hidden.astype(bf16)


def narrow(core, act, mixed, vecs, down_weight):
    count, width = mixed.shape
    wide = act.shape[1]
    tile = pl.BlockSpec((TILE, width), lambda i: (i, 0))
    broad = pl.BlockSpec((TILE, wide), lambda i: (i, 0))
    return pl.pallas_call(
        narrow_kernel,
        grid=(count // TILE,),
        in_specs=[SMEM, broad, tile, whole((8, width))] + [ANY] * 2,
        out_specs=[tile, tile],
        out_shape=[jax.ShapeDtypeStruct((count, width), f32), jax.ShapeDtypeStruct((count, width), bf16)],
        scratch_shapes=[pltpu.VMEM((width, wide), bf16), pltpu.SemaphoreType.DMA((8,))],
        compiler_params=params(),
        cost_estimate=pl.CostEstimate(
            flops=2 * count * width * wide, bytes_accessed=count * (width * 10 + wide * 2), transcendentals=0),
        name="narrow",
    )(core, act, mixed, vecs, *down_weight)


def add_rows(out, first, values):
    @pl.when(first)
    def _():
        out[...] = jnp.zeros_like(out)

    for index, value in enumerate(values):
        out[index] += partial_sum(value)


def top_kernel(
    core_ref, ctx, resid, cot, alive_col, vecs, up_bias,
    o_own, o_sib, u_own, u_sib, d_own, d_sib,
    outputs, low_out, act_out, gb_out, gu_out, ga_out, gm_out, gctx_out, sums, up_sums,
    out_weight, up_weight, down_weight, slopes, sems,
):
    core = core_ref[0]
    first = pl.program_id(0) == 0
    out_copies = piece_copies(core, (o_own, o_sib), out_weight, sems.at[0])
    up_copies = piece_copies(core, (u_own, u_sib), up_weight, sems.at[1])
    down_copies = piece_copies(core, (d_own, d_sib), down_weight, sems.at[2])

    @pl.when(first)
    def _():
        start_all(out_copies)
        start_all(up_copies)
        start_all(down_copies)
        sums[...] = jnp.zeros_like(sums)
        up_sums[...] = jnp.zeros_like(up_sums)
        wait_all(out_copies)

    width = ctx.shape[1]
    chunks = [slice(c * width, (c + 1) * width) for c in range(up_weight.shape[0] // width)]
    for part in range(ctx.shape[0] // SUB):
        rows = slice(part * SUB, (part + 1) * SUB)
        hidden = normalize(resid[rows, :])[0] * vecs[G2 : G2 + 1, :] + vecs[S2 : S2 + 1, :]
        mixed = hidden + dot_nt(ctx[rows, :], out_weight[...]) + vecs[OB : OB + 1, :]
        first_unit, first_rstd = normalize(mixed)
        combined = first_unit * vecs[G1 : G1 + 1, :] + vecs[S1 : S1 + 1, :]
        low = combined.astype(bf16)
        low_out[rows, :] = low

        @pl.when(first)
        def _():
            wait_all(up_copies)
            wait_all(down_copies)

        for cols in chunks:
            act, slope = gelu_both(dot_nt(low, up_weight[cols, :]) + up_bias[0:1, cols])
            act = act.astype(bf16)
            act_out[rows, cols] = act
            slopes[rows, cols] = slope.astype(bf16)
            combined = combined + dot_nt(act, down_weight[:, cols])
        unit, rstd = normalize(combined + vecs[DB : DB + 1, :])
        gain = vecs[G2 : G2 + 1, :]
        alive = alive_col[rows, 0:1].astype(f32)
        outputs[rows, :] = ((unit * gain + vecs[S2 : S2 + 1, :]) * alive).astype(bf16)
        grad = cot[rows, :].astype(f32) * alive
        sums[0] += partial_sum(grad * unit)
        sums[1] += partial_sum(grad)
        grad = normalize_back(grad, gain, unit, rstd)
        feed_back_rows(
            rows, chunks, grad, slopes, first_unit, first_rstd, vecs, down_weight, up_weight, out_weight,
            gb_out, gu_out, ga_out, gm_out, gctx_out, sums, up_sums,
        )


def feed_back_rows(
    rows, chunks, grad, slopes, unit, rstd, vecs, down_weight, up_weight, out_weight,
    gb_out, gu_out, ga_out, gm_out, gctx_out, sums, up_sums,
):
    branch = grad.astype(bf16)
    gb_out[rows, :] = branch
    sums[2] += partial_sum(branch.astype(f32))
    for cols in chunks:
        grad_up = (dot_nn(branch, down_weight[:, cols]) * slopes[rows, cols].astype(f32)).astype(bf16)
        gu_out[rows, cols] = grad_up
        up_sums[:, cols] += partial_sum(grad_up.astype(f32))
        grad = grad + dot_nn(grad_up, up_weight[cols, :])
    sums[3] += partial_sum(grad * unit)
    sums[4] += partial_sum(grad)
    grad = normalize_back(grad, vecs[G1 : G1 + 1, :], unit, rstd)
    gm_out[rows, :] = grad
    attn = grad.astype(bf16)
    ga_out[rows, :] = attn
    sums[5] += partial_sum(attn.astype(f32))
    gctx_out[rows, :] = dot_nn(attn, out_weight[...]).astype(bf16)


def top(core, ctx, resid, cot, alive_col, vecs, up_bias, out_weight, up_weight, down_weight):
    count, width = ctx.shape
    wide = up_bias.shape[1]
    tile = pl.BlockSpec((TILE, width), lambda i: (i, 0))
    broad = pl.BlockSpec((TILE, wide), lambda i: (i, 0))
    low = jax.ShapeDtypeStruct((count, width), bf16)
    low_wide = jax.ShapeDtypeStruct((count, wide), bf16)
    return pl.pallas_call(
        top_kernel,
        grid=(count // TILE,),
        in_specs=[SMEM, tile, tile, tile, pl.BlockSpec((TILE, 128), lambda i: (i, 0)), whole((8, width)),
                  whole((8, wide))] + [ANY] * 6,
        out_specs=[tile, tile, broad, tile, broad, tile, tile, tile, whole((6, 8, width)), whole((8, wide))],
        out_shape=[low, low, low_wide, low, low_wide, low, jax.ShapeDtypeStruct((count, width), f32), low,
                   jax.ShapeDtypeStruct((6, 8, width), f32), jax.ShapeDtypeStruct((8, wide), f32)],
        scratch_shapes=[
            pltpu.VMEM((width, width), bf16),
            pltpu.VMEM((wide, width), bf16),
            pltpu.VMEM((width, wide), bf16),
            pltpu.VMEM((TILE, wide), bf16),
            pltpu.SemaphoreType.DMA((3, 8)),
        ],
        compiler_params=params(),
        cost_estimate=pl.CostEstimate(
            flops=4 * count * width * (width + 2 * wide),
            bytes_accessed=count * (width * 22 + wide * 4), transcendentals=0),
        name="top",
    )(core, ctx, resid, cot, alive_col, vecs, up_bias, *out_weight, *up_weight, *down_weight)


def lower_kernel(
    core_ref, grads, gm, combined, slope, mixed, vecs, d_own, d_sib, u_own, u_sib,
    o_own, o_sib, q_own, q_sib,
    gb_out, gu_out, ga_out, gm_out, gctx_out, sums, up_sums, down_weight, up_weight, out_weight, weights, sems,
):
    core = core_ref[0]
    first = pl.program_id(0) == 0
    down_copies = piece_copies(core, (d_own, d_sib), down_weight, sems.at[0])
    up_copies = piece_copies(core, (u_own, u_sib), up_weight, sems.at[1])
    out_copies = piece_copies(core, (o_own, o_sib), out_weight, sems.at[2])
    copies = [
        piece_copies(core, (q_own, q_sib), weights.at[w], sems.at[3 + w], w) for w in range(3)
    ]

    @pl.when(first)
    def _():
        for group in copies:
            start_all(group)
        start_all(down_copies)
        start_all(up_copies)
        start_all(out_copies)
        sums[...] = jnp.zeros_like(sums)
        up_sums[...] = jnp.zeros_like(up_sums)
        for group in copies:
            wait_all(group)

    width = gm.shape[1]
    chunks = [slice(c * width, (c + 1) * width) for c in range(up_weight.shape[0] // width)]
    for part in range(gm.shape[0] // SUB):
        rows = slice(part * SUB, (part + 1) * SUB)
        grad = gm[rows, :]
        for w in range(3):
            grad = grad + dot_nn(grads[w, rows, :], weights[w])
        unit, rstd = normalize(combined[rows, :])
        sums[0] += partial_sum(grad * unit)
        sums[1] += partial_sum(grad)
        grad = normalize_back(grad, vecs[G2 : G2 + 1, :], unit, rstd)
        first_unit, first_rstd = normalize(mixed[rows, :])

        @pl.when(first)
        def _():
            wait_all(down_copies)
            wait_all(up_copies)
            wait_all(out_copies)

        feed_back_rows(
            rows, chunks, grad, slope, first_unit, first_rstd, vecs, down_weight, up_weight, out_weight,
            gb_out, gu_out, ga_out, gm_out, gctx_out, sums, up_sums,
        )


def lower(core, grads, gm, combined, slope, mixed, vecs, down_weight, up_weight, out_weight, qkv):
    count, width = mixed.shape
    wide = slope.shape[1]
    tile = pl.BlockSpec((TILE, width), lambda i: (i, 0))
    broad = pl.BlockSpec((TILE, wide), lambda i: (i, 0))
    low = jax.ShapeDtypeStruct((count, width), bf16)
    return pl.pallas_call(
        lower_kernel,
        grid=(count // TILE,),
        in_specs=[SMEM, pl.BlockSpec((3, TILE, width), lambda i: (0, i, 0)), tile, tile, broad, tile,
                  whole((8, width))] + [ANY] * 8,
        out_specs=[tile, broad, tile, tile, tile, whole((6, 8, width)), whole((8, wide))],
        out_shape=[low, jax.ShapeDtypeStruct((count, wide), bf16), low, jax.ShapeDtypeStruct((count, width), f32), low,
                   jax.ShapeDtypeStruct((6, 8, width), f32), jax.ShapeDtypeStruct((8, wide), f32)],
        scratch_shapes=[
            pltpu.VMEM((width, wide), bf16),
            pltpu.VMEM((wide, width), bf16),
            pltpu.VMEM((width, width), bf16),
            pltpu.VMEM((3, width, width), bf16),
            pltpu.SemaphoreType.DMA((6, 8)),
        ],
        compiler_params=params(),
        cost_estimate=pl.CostEstimate(
            flops=2 * count * width * (4 * width + 2 * wide),
            bytes_accessed=count * (width * 30 + wide * 4), transcendentals=0),
        name="lower",
    )(core, grads, gm, combined, slope, mixed, vecs, *down_weight, *up_weight, *out_weight, *qkv)


def attend_back_kernel(
    q, k, v, gctx, lse, seg_col, alive_col, seg_row, *rest
):
    grads, sums, mask = rest[-3:]

    @pl.when(pl.program_id(1) == 0)
    def _():
        mask_into(mask, seg_col, alive_col, seg_row)

    length = q.shape[0]
    lane = lax.broadcasted_iota(jnp.int32, (length, 2 * HEAD), 1)
    scaling = HEAD**-0.5
    for pair in range(2):
        cols = slice(pair * 2 * HEAD, (pair + 1) * 2 * HEAD)
        kp, vp, go = k[:, cols], v[:, cols], gctx[:, cols]
        qp = q[:, cols] * bf16(scaling)
        kt = kp.T
        dq_parts = []
        dk = dv = None
        for h in range(2):
            here = (lane >= HEAD) if h else (lane < HEAD)
            zero = bf16(0)
            qm, gm = jnp.where(here, qp, zero), jnp.where(here, go, zero)
            scores = dot_nt(kp, qm) + mask[...]
            probs = jnp.exp(scores - lse[0, 0, pl.ds(2 * pair + h, 1), :])
            weighted = probs * dot_nt(vp, gm)
            inner = jnp.sum(weighted, axis=0, keepdims=True)
            grad_scores = (weighted - probs * inner).astype(bf16)
            dv_h = dot_nn(probs.astype(bf16), gm)
            dk_h = dot_nn(grad_scores, qm)
            dv = dv_h if dv is None else dv + dv_h
            dk = dk_h if dk is None else dk + dk_h
            dq_parts.append(dot_nn(kt[h * HEAD : (h + 1) * HEAD], grad_scores))
        dq = (jnp.concatenate(dq_parts, axis=0).T * scaling).astype(bf16)
        dv = dv.astype(bf16)
        grads[0, :, cols] = dq
        grads[1, :, cols] = dk.astype(bf16)
        grads[2, :, cols] = dv
        sums[0, 0, :, cols] = partial_sum(dq.astype(f32))
        sums[0, 1, :, cols] = partial_sum(dv.astype(f32))


def attend_back(q, k, v, gctx, lse, seg_col, alive_col, seg_row, start=0, stop=None, before=()):
    count, width = q.shape
    rows, _, length = seg_row.shape
    stop = rows if stop is None else stop
    col = pl.BlockSpec((length, 128), lambda r, j: (r + start, 0))
    block = pl.BlockSpec((length, QUAD), lambda r, j: (r + start, j))
    share = (stop - start) / rows
    return pl.pallas_call(
        attend_back_kernel,
        grid=(stop - start, width // QUAD),
        in_specs=[block] * 4 + [pl.BlockSpec((1, 1, 8, length), lambda r, j: (r + start, j, 0, 0)), col, col,
                                pl.BlockSpec((1, 1, length), lambda r, j: (r + start, 0, 0))] + [ANY] * len(before),
        out_specs=[pl.BlockSpec((3, length, QUAD), lambda r, j: (0, r + start, j)),
                   pl.BlockSpec((1, 2, 8, QUAD), lambda r, j: (r + start, 0, 0, j))],
        out_shape=[jax.ShapeDtypeStruct((3, count, width), bf16), jax.ShapeDtypeStruct((rows, 2, 8, width), f32)],
        scratch_shapes=[pltpu.VMEM((length, length), f32)],
        input_output_aliases={8 + i: i for i in range(len(before))},
        compiler_params=params(),
        cost_estimate=pl.CostEstimate(
            flops=int(share * 4 * 10 * count * length * width),
            bytes_accessed=int(share * count * width * 16), transcendentals=0),
        name="attend_back",
    )(q, k, v, gctx, lse, seg_col, alive_col, seg_row, *before)


def input_back_kernel(core_ref, grads, gm, own, sib, grad_out, weights, sems):
    core = core_ref[0]
    copies = [
        piece_copies(core, (own, sib), weights.at[w], sems.at[w], w)
        for w in range(3)
    ]

    @pl.when(pl.program_id(0) == 0)
    def _():
        for group in copies:
            start_all(group)
        for group in copies:
            wait_all(group)

    grad = gm[...]
    for w in range(3):
        grad = grad + dot_nn(grads[w], weights[w])
    grad_out[...] = grad


def input_back(core, grads, gm, qkv):
    count, width = gm.shape
    tile = pl.BlockSpec((TILE, width), lambda i: (i, 0))
    return pl.pallas_call(
        input_back_kernel,
        grid=(count // TILE,),
        in_specs=[SMEM, pl.BlockSpec((3, TILE, width), lambda i: (0, i, 0)), tile] + [ANY] * 2,
        out_specs=tile,
        out_shape=jax.ShapeDtypeStruct((count, width), f32),
        scratch_shapes=[pltpu.VMEM((3, width, width), bf16), pltpu.SemaphoreType.DMA((3, 8))],
        compiler_params=params(),
        cost_estimate=pl.CostEstimate(
            flops=2 * count * width * width * 3, bytes_accessed=count * width * 14, transcendentals=0),
        name="input_back",
    )(core, grads, gm, *qkv)


def store_blocks(core, flip, total, put):
    rows = total.shape[0] // 4
    for block in range(4):
        x, c = block // 2, block % 2
        part = total[block * rows : (block + 1) * rows]
        for side in range(2):
            @pl.when(core == (c + side) % 2)
            def _():
                put(side, (x + flip) % 2, part)


def weight_grad_kernel(layers, place_ref, *refs):
    grads, inputs = refs[:layers], refs[layers : 2 * layers]
    outs = refs[2 * layers :]
    total = None
    for layer in range(layers):
        term = dot_tn(grads[layer][0], inputs[layer][...])
        total = term if total is None else total + term
    halves, wide = outs[0].shape[1], outs[0].shape[-1]

    def put(side, x, part):
        for half in range(halves):
            outs[side][0, half, x] = part[:, half * wide : (half + 1) * wide]

    store_blocks(place_ref[0], place_ref[1], total.astype(bf16), put)


def weight_grad(place, grads, inputs):
    layers = len(grads)
    count_w, span, n = grads[0].shape
    depth = inputs[0].shape[1]
    chunk = min(depth, n)
    chunks = depth // chunk
    halves = 2 if chunks == 1 else 1
    wide = chunk // halves
    per_half = depth // 2 // wide
    rows = n // 4
    if chunks == 1:
        out_spec = pl.BlockSpec((1, 2, 2, rows, wide), lambda w, j: (w, 0, 0, 0, 0))
    else:
        out_spec = pl.BlockSpec((1, 1, 2, rows, wide), lambda w, j: (w, j // per_half, 0, 0, j % per_half))
    out = jax.ShapeDtypeStruct((count_w, 2, 2, rows, depth // 2), bf16)
    return pl.pallas_call(
        partial(weight_grad_kernel, layers),
        grid=(count_w, chunks),
        in_specs=[SMEM] + [pl.BlockSpec((1, span, n), lambda w, j: (w, 0, 0))] * layers
        + [pl.BlockSpec((span, chunk), lambda w, j: (0, j))] * layers,
        out_specs=[out_spec, out_spec],
        out_shape=[out, out],
        compiler_params=params(),
        cost_estimate=pl.CostEstimate(
            flops=2 * layers * span * n * depth * count_w,
            bytes_accessed=2 * layers * span * (n * count_w + depth) + 2 * n * depth * count_w, transcendentals=0),
        name="weight_grad",
    )(place, *grads, *inputs)


def joint_grad_kernel(layers, small, tall, place_ref, *refs):
    grads, inputs = refs[:layers], refs[layers : 2 * layers]
    bias_sums, norm_sums, up_sums = (refs[(2 + i) * layers : (3 + i) * layers] for i in range(3))
    keep, send, totals, short = refs[5 * layers :]
    core, flip = place_ref[0], place_ref[1]
    which = pl.program_id(0)
    sides, _, blocks, _, half = keep.shape
    width = totals.shape[1]
    rows = width // 4

    def slot(block):
        return 2 * ((block // 2 + flip) % 2) + (block % 2 + core) % 2

    total = None
    for layer in range(layers):
        term = dot_tn(grads[layer][0], inputs[layer][...])
        total = term if total is None else total + term
    for block in range(4):
        totals[which, pl.ds(pl.multiple_of(slot(block) * rows, rows), rows), :] = total[block * rows : (block + 1) * rows]

    @pl.when(which == 0)
    def _():
        bias = sum(jnp.sum(ref[...], axis=(0, 2)) for ref in bias_sums)
        norm = sum(jnp.sum(ref[...], axis=1) for ref in norm_sums)
        up = sum(jnp.sum(ref[...], axis=0, keepdims=True) for ref in up_sums)
        rest = [norm[n : n + 1] for n in (5, 3, 4, 2, 0, 1)]
        lines = jnp.concatenate([bias[0:1], bias[1:2], *rest], axis=0)
        short[...] = jnp.zeros_like(short)
        quarter = up.shape[1] // 4
        for block in range(4):
            place = slot(block)
            here = pltpu.roll(lines, lax.rem(width - place * rows, width), 1)
            above = jnp.where(place == 0, up[:, :quarter], 0.0)
            for index in range(1, 4):
                above = above + jnp.where(place == index, up[:, index * quarter : (index + 1) * quarter], 0.0)
            above = jnp.broadcast_to(above, (8, quarter))
            for zy in range(blocks):
                first = pltpu.roll(here, (width - zy * small) % width, 1)[:, :128]
                second = pltpu.roll(above, (quarter - zy * tall) % quarter, 1)[:, :128]
                short[block, zy, :, 0:128] = first
                short[block, zy, :, 128:256] = second

    @pl.when(which == pl.num_programs(0) - 1)
    def _():
        for block in range(4):
            out = (keep, send)[block % 2]
            for zy in range(blocks):
                start = block * rows + zy * small
                for side in range(sides):
                    cols = slice(side * half, (side + 1) * half)
                    parts = [totals[w, start : start + small, cols] for w in range(totals.shape[0])]
                    out[side, block // 2, zy] = jnp.concatenate([*parts, short[block, zy, :, cols]], axis=0).astype(bf16)


def joint_grad(place, grads, inputs, bias_sums, norm_sums, up_sums, small, tall):
    layers = len(grads)
    count, span, n = grads[0].shape
    depth = inputs[0].shape[1]
    blocks = n // 4 // small
    lines = count * small + 8
    out = jax.ShapeDtypeStruct((2, 2, blocks, lines, depth // 2), bf16)
    sums = [*bias_sums, *norm_sums, *up_sums]
    return pl.pallas_call(
        partial(joint_grad_kernel, layers, small, tall),
        grid=(count,),
        in_specs=[SMEM] + [pl.BlockSpec((1, span, n), lambda w: (w, 0, 0))] * layers + [whole((span, depth))] * layers
        + [whole(v.shape) for v in sums],
        out_specs=[whole(out.shape)] * 2,
        out_shape=[out, out],
        scratch_shapes=[
            pltpu.VMEM((count, n, depth), f32),
            pltpu.VMEM((4, blocks, 8, depth), f32),
        ],
        compiler_params=params(),
        cost_estimate=pl.CostEstimate(
            flops=2 * layers * span * n * depth * count,
            bytes_accessed=2 * layers * span * (n * count + depth) + 2 * n * depth * count, transcendentals=0),
        name="joint_grad",
    )(place, *grads, *inputs, *sums)


def tall_grad_kernel(layers, place_ref, *refs):
    tall, tall_in, flat, flat_in = (refs[i * layers : (i + 1) * layers] for i in range(4))
    keep, send, turned, flat_total = refs[4 * layers :]
    step = pl.program_id(0)
    core, flip = place_ref[0], place_ref[1]
    sides, _, blocks, rows, half = keep.shape
    flat_rows = flat_total.shape[0] // 4
    small = flat_rows // blocks
    large = rows - small

    def product(left, right):
        total = None
        for layer in range(layers):
            term = dot_tn(left[layer][...], right[layer][...])
            total = term if total is None else total + term
        return total

    @pl.when(step == 0)
    def _():
        total = product(flat, flat_in)
        for block in range(4):
            slot = 2 * ((block // 2 + flip) % 2) + (block % 2 + core) % 2
            flat_total[pl.ds(pl.multiple_of(slot * flat_rows, flat_rows), flat_rows), :] = (
                total[block * flat_rows : (block + 1) * flat_rows]
            )

    @pl.when(step > 0)
    def _():
        turned[...] = product(tall, tall_in).astype(bf16)
        slot = step - 1
        for c, out in ((0, keep), (1, send)):
            @pl.when(slot % 2 == c)
            def _():
                for side in range(sides):
                    cols = slice(side * half, (side + 1) * half)
                    for block in range(blocks):
                        out[side, 0, block, :large, :] = turned[block * large : (block + 1) * large, cols]
                        start = pl.multiple_of(slot * flat_rows + block * small, 8)
                        out[side, 0, block, large:, :] = flat_total[pl.ds(start, small), cols].astype(bf16)


def tall_grad(place, tall, tall_in, flat, flat_in):
    layers = len(tall)
    span, n = tall[0].shape
    depth = tall_in[0].shape[1]
    flat_n = flat[0].shape[1]
    rows = n // 4

    def column(s, place):
        slot = jnp.maximum(s - 1, 0)
        return 0, 2 * ((slot // 2 + place[1]) % 2) + (slot % 2 + place[0]) % 2

    def fixed(shape):
        return pl.BlockSpec(shape, lambda s, place: (0, 0))

    blocks = 8
    share = (n + flat_n) // 4 // blocks
    out_spec = pl.BlockSpec(
        (2, 1, blocks, share, depth // 2), lambda s, place: (0, jnp.maximum(s - 1, 0) // 2, 0, 0, 0)
    )
    out = jax.ShapeDtypeStruct((2, 2, blocks, share, depth // 2), bf16)
    return pl.pallas_call(
        partial(tall_grad_kernel, layers),
        grid_spec=pltpu.PrefetchScalarGridSpec(
            num_scalar_prefetch=1,
            grid=(5,),
            in_specs=[pl.BlockSpec((span, rows), column)] * layers + [fixed((span, depth))] * layers
            + [fixed((span, flat_n))] * layers + [fixed((span, depth))] * layers,
            out_specs=[out_spec, out_spec],
            scratch_shapes=[pltpu.VMEM((rows, depth), bf16), pltpu.VMEM((flat_n, depth), f32)],
        ),
        out_shape=[out, out],
        compiler_params=params(),
        cost_estimate=pl.CostEstimate(
            flops=2 * layers * span * (n + flat_n) * depth,
            bytes_accessed=2 * layers * span * (n + flat_n + 2 * depth) + 2 * (n + flat_n) * depth, transcendentals=0),
        name="tall_grad",
    )(place, *tall, *tall_in, *flat, *flat_in)


def pack_kernel(weights, *refs):
    parts, out, rows = refs[:-2], refs[-2], refs[-1]
    rows[...] = jnp.zeros_like(rows)
    start = 0
    for part in parts[:weights]:
        rows[start : start + part.shape[0], :] = part[...].astype(f32)
        start += part.shape[0]
    for index, part in enumerate(parts[weights:-1]):
        rows[start + index : start + index + 1, : part.shape[1]] = part[...].astype(f32)
    rows[start : start + 1, 128 : 128 + parts[-1].shape[1]] = parts[-1][...].astype(f32)
    out[...] = rows[...].astype(bf16)


def pack(vectors, weights=()):
    parts = [*weights, *(vector[None] for vector in vectors)]
    shape = (sum(weight.shape[0] for weight in weights) + 8, weights[0].shape[1] if weights else 256)
    return pl.pallas_call(
        partial(pack_kernel, len(weights)),
        in_specs=[whole(part.shape) for part in parts],
        out_specs=whole(shape),
        out_shape=jax.ShapeDtypeStruct(shape, bf16),
        scratch_shapes=[pltpu.VMEM(shape, f32)],
        name="pack",
    )(*parts)


AXES = ("dp", "fsdp")


def halves(v):
    middle = v.shape[-1] // 2
    return v[..., :middle], v[..., middle:]


def tie(value, after):
    return value if after is None else lax.optimization_barrier((value, after))[0]


class Chain:
    def __init__(self, stages):
        self.stages, self.result, self.landed = stages, None, None
        self.step()

    def step(self, after=None):
        if self.stages is None:
            return self.landed
        try:
            self.landed = self.stages.send(after) if self.landed is not None else next(self.stages)
        except StopIteration as end:
            self.result = end.value
            self.stages = None
        return self.landed

    def finish(self, after=None):
        while self.stages is not None:
            self.step(after)
        return self.result


class Plain:
    def __init__(self, mesh):
        self.devices = math.prod(mesh.shape.values())

    def place(self):
        return jnp.zeros((2,), jnp.int32)

    def spread(self, shards, vectors=None):
        def pieces(full):
            blocks = full.reshape(full.shape[:-2] + (2, 2, full.shape[-2] // 4, full.shape[-1]))
            return tuple(jnp.stack(halves(blocks[..., core, :, :]), axis=-4) for core in range(2))

        full = [lax.all_gather(shard, AXES, axis=0, tiled=True) for shard in shards]
        yield full[0]
        if vectors is None:
            return [pieces(weight) for weight in full]
        return pieces(jnp.stack(full)), lax.all_gather(pack(vectors), AXES, axis=0, tiled=False)

    def reduce(self, keep, send):
        count, sides, xs, rows, half = keep.shape
        both = jnp.stack([keep, send], axis=3).astype(f32)
        full = jnp.moveaxis(both, 1, 4).reshape(count, xs * 2 * rows, sides * half)
        full = lax.psum_scatter(full, AXES, scatter_dimension=1, tiled=True)
        yield full
        return full

    def reduce_joined(self, keep, send, tall, flat):
        large = keep.shape[3] * tall // (tall + flat)
        results = []
        for rows in (slice(0, large), slice(large, None)):
            sides, xs, half = keep.shape[0], keep.shape[1], keep.shape[-1]
            parts = [v[:, :, :, rows].reshape(1, sides, xs, -1, half) for v in (keep, send)]
            results.append(Chain(self.reduce(*parts)).finish())
        yield results[0]
        return jnp.concatenate(results, axis=1)

    def joint_grad(self, place, grads, inputs, bias_sums, norm_sums, up_sums, small, tall):
        bias = sum(jnp.sum(v, axis=(0, 2)) for v in bias_sums)
        norm = sum(jnp.sum(v, axis=1) for v in norm_sums)
        up = sum(jnp.sum(v, axis=0) for v in up_sums)
        lines = jnp.stack([bias[0], bias[1], norm[5], norm[3], norm[4], norm[2], norm[0], norm[1]])
        lines = lines.reshape(8, self.devices, small).transpose(1, 0, 2)
        return (*weight_grad(place, grads, inputs), lines, up.reshape(self.devices, tall))

    def reduce_joint(self, keep, send, lines, up):
        full = Chain(self.reduce(keep, send)).finish()
        lines = lax.psum_scatter(lines, AXES, scatter_dimension=0, tiled=True)[0]
        up = lax.psum_scatter(up, AXES, scatter_dimension=0, tiled=True)
        rows = full.reshape(-1, full.shape[-1])
        yield rows
        short = jnp.zeros((8, full.shape[-1]), f32).at[:, : lines.shape[1]].set(lines).at[:1, 128 : 128 + up.shape[1]].set(up)
        return jnp.concatenate([rows, short], axis=0)


class Grid:
    def __init__(self, mesh):
        pass

    def where(self):
        dp, fsdp = lax.axis_index("dp"), lax.axis_index("fsdp")
        return dp // 2, dp % 2, fsdp // 2, fsdp % 2

    def place(self):
        x, core, _, _ = self.where()
        return jnp.stack([core, x]).astype(jnp.int32)

    def swap(self, value, x=0, core=0, z=0, y=0):
        flip = ((x * 2 + core) * 4 + z) * 2 + y
        return lax.ppermute(value, AXES, [(i, i ^ flip) for i in range(32)])

    def ordered(self, mine, other, side, axis=0):
        return jnp.stack([jnp.where(side == 0, mine, other), jnp.where(side == 0, other, mine)], axis=axis)

    def ordered_z(self, parts, z):
        odd, high = z % 2, z // 2
        parts = [jnp.where(odd == 0, parts[k], parts[k ^ 1]) for k in range(4)]
        return jnp.stack([jnp.where(high == 0, parts[k], parts[k ^ 2]) for k in range(4)])

    def spread(self, shards, vectors=None):
        x, core, z, y = self.where()
        if vectors is not None:
            payload = pack(vectors, shards)
        else:
            payload = jnp.concatenate(shards, axis=0) if len(shards) > 1 else shards[0]
        parts = [payload] + [self.swap(payload, z=k) for k in range(1, 4)]
        parts = tie(parts, (yield parts[1:]))
        left, right = halves(self.ordered_z(parts, z))
        got = self.swap(left, x=1), self.swap(right, y=1)
        got = tie(got, (yield got))
        left = self.ordered(left, got[0], x)
        right = self.ordered(right, got[1], y, axis=1)
        got = self.swap(left, y=1), self.swap(right, x=1)
        got = tie(got, (yield got))
        left = self.ordered(left, got[0], y, axis=2)
        right = self.ordered(right, got[1], x)
        own, start = [], 0
        for shard in shards:
            rows = shard.shape[0]
            own.append(jnp.stack([v[:, :, :, start : start + rows].reshape(2, 8 * rows, -1) for v in (left, right)]))
            start += rows
        if vectors is not None:
            own = [jnp.stack(own), left[:, :, :, start:, :256]]
        other = [self.swap(mine, core=1) for mine in own]
        other = tie(other, (yield other))
        if vectors is None:
            return list(zip(own, other))
        vectors = self.ordered(own[1], other[1], core, axis=1)
        return (own[0], other[0]), vectors.reshape(32, 8, 256)

    def reduce(self, keep, send):
        _, _, z, y = self.where()
        count, _, _, rows, half = keep.shape
        mine = rows // 8

        def add(a, b):
            return (a.astype(f32) + b.astype(f32)).astype(bf16)

        def pick(v, index, axis):
            return lax.dynamic_index_in_dim(v, index, axis, keepdims=False)

        got = self.swap(send, core=1)
        got = tie(got, (yield got))
        total = add(keep, got).reshape(count, 2, 2, 4, 2, mine, half)
        left, right = total[:, 0], total[:, 1]
        got = self.swap(left[:, 1], x=1), self.swap(pick(right, 1 - y, 3), y=1)
        got = tie(got, (yield got))
        left, right = add(left[:, 0], got[0]), add(pick(right, y, 3), got[1])
        got = self.swap(pick(left, 1 - y, 2), y=1), self.swap(right[:, 1], x=1)
        got = tie(got, (yield got))
        left, right = add(pick(left, y, 2), got[0]), add(right[:, 0], got[1])
        both = jnp.concatenate([left, right], axis=-1)
        got = [self.swap(pick(both, z ^ k, 1), z=k) for k in range(1, 4)]
        got = tie(got, (yield got))
        result = pick(both, z, 1).astype(f32)
        for part in got:
            result = result + part.astype(f32)
        return result

    def reduce_joined(self, keep, send, tall, flat):
        shape = (1, 2, 2, -1, keep.shape[-1])
        return self.reduce(keep.reshape(shape), send.reshape(shape))

    def joint_grad(self, *operands):
        return joint_grad(*operands)

    def reduce_joint(self, keep, send):
        shape = (1, 2, 2, -1, keep.shape[-1])
        result = yield from self.reduce(keep.reshape(shape), send.reshape(shape))
        return result[0]


def column_info(values, count):
    return jnp.broadcast_to(values.reshape(count, 1), (count, 128))


def body(
    exchange,
    tokens,
    cotangent,
    segment_ids,
    pad_mask,
    row_counts,
    query_weight,
    query_bias,
    key_weight,
    value_weight,
    value_bias,
    out_weight,
    out_bias,
    first_gain,
    first_shift,
    up_weight,
    up_bias,
    down_weight,
    down_bias,
    second_gain,
    second_shift,
):
    rows_here, row_len, width = tokens.shape
    count = rows_here * row_len
    small, tall = query_bias.shape[0], up_bias.shape[0]
    place = exchange.place()

    first = Chain(
        exchange.spread(
            [query_weight, key_weight, value_weight],
            [query_bias, value_bias, out_bias, first_gain, first_shift, down_bias, second_gain, second_shift, up_bias],
        )
    )
    z_landed = first.landed
    first.step()
    second = Chain(exchange.spread(tie([out_weight, up_weight], z_landed)))
    first.step()
    xy_landed = first.landed
    first.step()
    down_full = lax.all_gather(tie(down_weight, (xy_landed, second.landed)), AXES, axis=0, tiled=True)
    second.step(xy_landed)
    qkv, vectors = first.finish()
    vectors = vectors.astype(f32)
    devices = vectors.shape[0]
    wide = tall * devices
    vecs = vectors[:, :, :small].transpose(1, 0, 2).reshape(8, width)
    up_vec = jnp.broadcast_to(vectors[:, 0, 128 : 128 + tall].reshape(1, wide), (8, wide))

    present = (jnp.arange(rows_here, dtype=jnp.int32) < row_counts[0]).astype(jnp.int32)
    alive = pad_mask * present[:, None]
    alive_col = column_info(alive, count)
    seg_col = column_info(segment_ids, count)
    seg_row = segment_ids.reshape(rows_here, 1, row_len)
    info = (seg_col, alive_col, seg_row)
    flat = tokens.reshape(count, width)

    landed = second.landed
    lower_kept = attend_forward(place, flat, *info, vecs, qkv, 0, 1)
    second.step(lower_kept[3])
    lower_kept = attend_forward(place, tie(flat, landed), *info, vecs, qkv, 1, rows_here, lower_kept)
    second.step(lower_kept[3])
    out_w, up_w = second.finish()
    mixed, lower_low, lower_act, slope = widen(place, lower_kept[3], flat, vecs, up_vec, out_w, up_w)
    down_w = (down_full, down_full)
    combined, inputs = narrow(place, lower_act, mixed, vecs, down_w)

    upper_kept = attend_forward(place, inputs, *info, vecs, qkv)
    outputs, upper_low, upper_act, upper_gb, upper_gu, upper_ga, gm, gctx, sums, up_sums = top(
        place, upper_kept[3], combined, cotangent.reshape(count, width), alive_col, vecs, up_vec, out_w, up_w, down_w
    )
    upper_grads, bias_sums = attend_back(*upper_kept[:3], gctx, upper_kept[4], *info)
    lower_gb, lower_gu, lower_ga, gm, gctx, more_sums, more_up_sums = lower(
        place, upper_grads, gm, combined, slope, mixed, vecs, down_w, up_w, out_w, qkv
    )

    keep, send = weight_grad(place, [upper_gb[None], lower_gb[None]], [upper_act, lower_act])
    down_sum = Chain(exchange.reduce(keep, send))
    keep, send = tall_grad(
        place, [upper_gu, tie(lower_gu, keep)], [upper_low, lower_low], [upper_ga, lower_ga], [upper_kept[3], lower_kept[3]]
    )
    up_sum = Chain(exchange.reduce_joined(keep, send, tall, small))
    landed = down_sum.landed
    down_sum.step()
    lower_grads, more_bias_sums = attend_back(*lower_kept[:3], tie(gctx, (keep, landed)), lower_kept[4], *info)
    landed = (up_sum.landed, down_sum.landed)
    up_sum.step()
    down_sum.step()
    joint = exchange.joint_grad(
        place, [upper_grads, tie(lower_grads, landed)], [inputs, flat],
        [bias_sums, more_bias_sums], [sums, more_sums], [up_sums, more_up_sums], small, tall,
    )
    qkv_sum = Chain(exchange.reduce_joint(*joint))
    landed = (up_sum.landed, down_sum.landed)
    up_sum.step()
    down_sum.step()
    tokens_grad = input_back(place, tie(lower_grads, (joint[0], landed)), gm, qkv)
    up_sum.step(tokens_grad)
    qkv_sum.step(tokens_grad)
    up_out = up_sum.finish()[0]
    joint = qkv_sum.finish()
    query_grad, key_grad, value_grad = (joint[i * small : (i + 1) * small] for i in range(3))
    lines = joint[3 * small :]
    piece = [lines[i, :small] for i in range(8)]
    return (
        outputs.reshape(rows_here, row_len, width),
        tokens_grad.reshape(rows_here, row_len, width),
        query_grad,
        piece[QB],
        key_grad,
        value_grad,
        piece[VB],
        up_out[tall:],
        piece[OB],
        piece[G1],
        piece[S1],
        up_out[:tall],
        lines[0, 128 : 128 + tall],
        down_sum.finish()[0],
        piece[DB],
        piece[G2],
        piece[S2],
    )


def solution(mesh):
    rows = P(AXES, None, None)
    flat = P(AXES, None)
    line = P(AXES)
    matrices = (flat, line, flat, flat, line, flat, line, line, line, flat, line, flat, line, line, line)
    exchange = Grid(mesh) if dict(mesh.shape) == {"dp": 4, "fsdp": 8} else Plain(mesh)
    return jax.shard_map(
        partial(body, exchange),
        mesh=mesh,
        in_specs=(rows, rows, flat, flat, line) + matrices,
        out_specs=(rows, rows) + matrices,
        check_vma=False,
    )
```

```python
from functools import partial
import math

import jax
import jax.numpy as jnp
from jax import lax
from jax.experimental import pallas as pl
from jax.experimental.pallas import tpu as pltpu
from jax.sharding import PartitionSpec as P

HEAD = 64
LAYERS = 2
QUAD = 4 * HEAD
TILE = 256
SUB = 256
TOP_TILE = 512
norm_eps = 1e-06
masked_score = -1000000000.0
VMEM = 60 * 1024 * 1024
bf16 = jnp.bfloat16
f32 = jnp.float32

QB, VB, OB, G1, S1, DB, G2, S2 = range(8)


def dot_nt(left, right):
    return lax.dot_general(left, right, (((1,), (1,)), ((), ())), preferred_element_type=f32)


def dot_nn(left, right):
    return lax.dot_general(left, right, (((1,), (0,)), ((), ())), preferred_element_type=f32)


def dot_tn(left, right):
    return lax.dot_general(left, right, (((0,), (0,)), ((), ())), preferred_element_type=f32)


def normalize(v):
    mean = jnp.mean(v, axis=-1, keepdims=True)
    centered = v - mean
    rstd = lax.rsqrt(jnp.mean(centered * centered, axis=-1, keepdims=True) + norm_eps)
    return centered * rstd, rstd


def normalize_back(grad, gain, unit, rstd):
    scaled = grad * gain
    first = jnp.mean(scaled, axis=-1, keepdims=True)
    second = jnp.mean(scaled * unit, axis=-1, keepdims=True)
    return rstd * (scaled - first - unit * second)


def partial_sum(v):
    return jnp.sum(v.reshape(v.shape[0] // 8, 8, v.shape[1]), axis=0)


def piece_copies(core, pieces, place, sems, which=None):
    copies = []
    for sibling, piece in enumerate(pieces):
        source = piece if which is None else piece.at[which]
        if len(source.shape) == 2:
            rows = source.shape[0] // 2
            part = slice(sibling * rows, (sibling + 1) * rows)
            copies.append(pltpu.make_async_copy(source.at[part, :], place.at[part, :], sems.at[4 * sibling]))
            continue
        sides, _, rows, half = source.shape
        for side in range(sides):
            for x in range(2):
                slot = 2 * x + (1 - core if sibling else core)
                start = pl.multiple_of(slot * rows, rows)
                copies.append(
                    pltpu.make_async_copy(
                        source.at[side, x],
                        place.at[pl.ds(start, rows), pl.ds(side * half, half)],
                        sems.at[4 * sibling + 2 * side + x],
                    )
                )
    return copies


def start_all(copies):
    for copy in copies:
        copy.start()


def wait_all(copies):
    for copy in copies:
        copy.wait()


def params():
    return pltpu.CompilerParams(vmem_limit_bytes=VMEM)


ANY = pl.BlockSpec(memory_space=pl.ANY)
SMEM = pl.BlockSpec(memory_space=pltpu.SMEM)


def whole(shape):
    return pl.BlockSpec(shape, lambda *_: (0,) * len(shape))


def mask_into(mask, seg_col, alive_col, seg_row):
    length = mask.shape[0]
    key = lax.broadcasted_iota(jnp.int32, (length, length), 0)
    query = lax.broadcasted_iota(jnp.int32, (length, length), 1)
    same = seg_col[:, 0:1] == seg_row[0]
    allowed = same & ((alive_col[:, 0:1] > 0) | (key == query))
    mask[...] = jnp.where(allowed, 0.0, masked_score)


def attend_forward_kernel(
    start, core_ref, x, seg_col, alive_col, seg_row, vecs, own, sib, *rest
):
    q_out, k_out, v_out, ctx_out, lse_out, weights, mask, sems = rest[-8:]
    quad = (pl.program_id(0) + start) % (weights.shape[1] // QUAD)
    core = core_ref[0]
    first = pl.program_id(0) == 0
    copies = [
        piece_copies(core, (own, sib), weights.at[w], sems.at[w], w)
        for w in range(3)
    ]

    @pl.when(first)
    def _():
        for group in copies:
            start_all(group)

    @pl.when(first | (quad == 0))
    def _():
        mask_into(mask, seg_col, alive_col, seg_row)

    @pl.when(first)
    def _():
        for group in copies:
            wait_all(group)

    inputs = x[...]
    heads = pl.ds(pl.multiple_of(quad * QUAD, QUAD), QUAD)
    queries = (dot_nt(inputs, weights[0, heads, :]) + vecs[QB : QB + 1, :]).astype(bf16)
    keys = dot_nt(inputs, weights[1, heads, :]).astype(bf16)
    values = (dot_nt(inputs, weights[2, heads, :]) + vecs[VB : VB + 1, :]).astype(bf16)
    q_out[...] = queries
    k_out[...] = keys
    v_out[...] = values
    scaled = queries * bf16(HEAD**-0.5)
    length = inputs.shape[0]
    lane = lax.broadcasted_iota(jnp.int32, (length, 2 * HEAD), 1)
    for pair in range(2):
        cols = slice(pair * 2 * HEAD, (pair + 1) * 2 * HEAD)
        kp, qp = keys[:, cols], scaled[:, cols]
        vt = values[:, cols].T
        parts = []
        for h in range(2):
            km = jnp.where((lane >= HEAD) if h else (lane < HEAD), kp, bf16(0))
            scores = dot_nt(km, qp) + mask[...]
            highest = jnp.max(scores, axis=0, keepdims=True)
            weight = jnp.exp(scores - highest)
            total = jnp.sum(weight, axis=0, keepdims=True)
            parts.append(dot_nn(vt[h * HEAD : (h + 1) * HEAD], weight.astype(bf16)) / total)
            lse_out[0, 0, pl.ds(2 * pair + h, 1), :] = highest + jnp.log(total)
        ctx_out[:, cols] = jnp.concatenate(parts, axis=0).T.astype(bf16)


def attend_forward(core, x, seg_col, alive_col, seg_row, vecs, qkv, start=0, stop=None, before=()):
    count, width = x.shape
    rows, _, length = seg_row.shape
    quads = width // QUAD
    stop = rows * quads if stop is None else stop

    def row(s):
        return (s + start) // quads

    def quad(s):
        return (s + start) % quads

    full = pl.BlockSpec((length, width), lambda s: (row(s), 0))
    col = pl.BlockSpec((length, 128), lambda s: (row(s), 0))
    block = pl.BlockSpec((length, QUAD), lambda s: (row(s), quad(s)))
    low = jax.ShapeDtypeStruct((count, width), bf16)
    share = (stop - start) / (rows * quads)
    return pl.pallas_call(
        partial(attend_forward_kernel, start),
        grid=(stop - start,),
        in_specs=[SMEM, full, col, col, pl.BlockSpec((1, 1, length), lambda s: (row(s), 0, 0)),
                  pl.BlockSpec((8, QUAD), lambda s: (0, quad(s))), ANY, ANY] + [ANY] * len(before),
        out_specs=[block] * 4 + [pl.BlockSpec((1, 1, 8, length), lambda s: (row(s), quad(s), 0, 0))],
        out_shape=[low] * 4 + [jax.ShapeDtypeStruct((rows, quads, 8, length), f32)],
        scratch_shapes=[
            pltpu.VMEM((3, width, width), bf16),
            pltpu.VMEM((length, length), f32),
            pltpu.SemaphoreType.DMA((3, 8)),
        ],
        input_output_aliases={8 + i: i for i in range(len(before))},
        compiler_params=params(),
        cost_estimate=pl.CostEstimate(
            flops=int(share * (2 * count * width * width * 3 + 4 * 4 * count * length * width)),
            bytes_accessed=int(share * count * width * 10) + 3 * width * width * 2, transcendentals=0),
        name="attend_forward",
    )(core, x, seg_col, alive_col, seg_row, vecs, *qkv, *before)


GELU_A = math.sqrt(2.0 / math.pi)
GELU_B = 0.044715


def gelu_both(u):
    square = u * u
    t = jnp.tanh(u * (GELU_A + (GELU_A * GELU_B) * square))
    half = 0.5 + 0.5 * t
    slope = half + (u * (1.0 - t * t)) * (0.5 * GELU_A + (1.5 * GELU_A * GELU_B) * square)
    return u * half, slope


def widen_kernel(
    core_ref, ctx, resid, vecs, up_bias, o_own, o_sib, u_own, u_sib,
    mixed_out, low_out, act_out, slope_out, out_weight, up_weight, sems,
):
    core = core_ref[0]
    first = pl.program_id(0) == 0
    out_copies = piece_copies(core, (o_own, o_sib), out_weight, sems.at[0])
    up_copies = piece_copies(core, (u_own, u_sib), up_weight, sems.at[1])

    @pl.when(first)
    def _():
        start_all(out_copies)
        start_all(up_copies)
        wait_all(out_copies)

    mixed = resid[...].astype(f32) + dot_nt(ctx[...], out_weight[...]) + vecs[OB : OB + 1, :]
    mixed_out[...] = mixed
    normed = normalize(mixed)[0] * vecs[G1 : G1 + 1, :] + vecs[S1 : S1 + 1, :]
    low = normed.astype(bf16)
    low_out[...] = low

    @pl.when(first)
    def _():
        wait_all(up_copies)

    width = low.shape[1]
    for chunk in range(up_weight.shape[0] // width):
        cols = slice(chunk * width, (chunk + 1) * width)
        upward = dot_nt(low, up_weight[cols, :]) + up_bias[0:1, cols]
        act, slope = gelu_both(upward)
        act_out[:, cols] = act.astype(bf16)
        slope_out[:, cols] = slope.astype(bf16)


def widen(core, ctx, resid, vecs, up_bias, out_weight, up_weight):
    count, width = ctx.shape
    wide = up_bias.shape[1]
    tile = pl.BlockSpec((TILE, width), lambda i: (i, 0))
    broad = pl.BlockSpec((TILE, wide), lambda i: (i, 0))
    return pl.pallas_call(
        widen_kernel,
        grid=(count // TILE,),
        in_specs=[SMEM, tile, tile, whole((8, width)), whole((8, wide))] + [ANY] * 4,
        out_specs=[tile, tile, broad, broad],
        out_shape=[
            jax.ShapeDtypeStruct((count, width), f32),
            jax.ShapeDtypeStruct((count, width), bf16),
            jax.ShapeDtypeStruct((count, wide), bf16),
            jax.ShapeDtypeStruct((count, wide), bf16),
        ],
        scratch_shapes=[
            pltpu.VMEM((width, width), bf16),
            pltpu.VMEM((wide, width), bf16),
            pltpu.SemaphoreType.DMA((2, 8)),
        ],
        compiler_params=params(),
        cost_estimate=pl.CostEstimate(
            flops=2 * count * width * (width + wide),
            bytes_accessed=count * (width * 12 + wide * 4), transcendentals=0),
        name="widen",
    )(core, ctx, resid, vecs, up_bias, *out_weight, *up_weight)


def narrow_kernel(core_ref, act, mixed, vecs, d_own, d_sib, combined_out, low_out, down_weight, sems):
    core = core_ref[0]
    copies = piece_copies(core, (d_own, d_sib), down_weight, sems)

    @pl.when(pl.program_id(0) == 0)
    def _():
        start_all(copies)
        wait_all(copies)

    normed = normalize(mixed[...])[0] * vecs[G1 : G1 + 1, :] + vecs[S1 : S1 + 1, :]
    combined = normed + dot_nt(act[...], down_weight[...]) + vecs[DB : DB + 1, :]
    combined_out[...] = combined
    hidden = normalize(combined)[0] * vecs[G2 : G2 + 1, :] + vecs[S2 : S2 + 1, :]
    low_out[...] = hidden.astype(bf16)


def narrow(core, act, mixed, vecs, down_weight):
    count, width = mixed.shape
    wide = act.shape[1]
    tile = pl.BlockSpec((TILE, width), lambda i: (i, 0))
    broad = pl.BlockSpec((TILE, wide), lambda i: (i, 0))
    return pl.pallas_call(
        narrow_kernel,
        grid=(count // TILE,),
        in_specs=[SMEM, broad, tile, whole((8, width))] + [ANY] * 2,
        out_specs=[tile, tile],
        out_shape=[jax.ShapeDtypeStruct((count, width), f32), jax.ShapeDtypeStruct((count, width), bf16)],
        scratch_shapes=[pltpu.VMEM((width, wide), bf16), pltpu.SemaphoreType.DMA((8,))],
        compiler_params=params(),
        cost_estimate=pl.CostEstimate(
            flops=2 * count * width * wide, bytes_accessed=count * (width * 10 + wide * 2), transcendentals=0),
        name="narrow",
    )(core, act, mixed, vecs, *down_weight)


def add_rows(out, first, values):
    @pl.when(first)
    def _():
        out[...] = jnp.zeros_like(out)

    for index, value in enumerate(values):
        out[index] += partial_sum(value)


def in_turn(parts, first, landed):
    live = parts
    turn = 0
    while live:
        live = [part for part in live if next(part, live) is not live]
        if turn == 0:
            pl.when(first)(landed)
        turn += 1


def top_kernel(
    core_ref, ctx, resid, cot, alive_col, vecs, up_bias,
    o_own, o_sib, u_own, u_sib, d_own, d_sib,
    outputs, low_out, act_out, gb_out, gu_out, ga_out, gm_out, gctx_out, sums, up_sums,
    out_weight, up_weight, down_weight, slopes, sems,
):
    core = core_ref[0]
    first = pl.program_id(0) == 0
    out_copies = piece_copies(core, (o_own, o_sib), out_weight, sems.at[0])
    up_copies = piece_copies(core, (u_own, u_sib), up_weight, sems.at[1])
    down_copies = piece_copies(core, (d_own, d_sib), down_weight, sems.at[2])

    @pl.when(first)
    def _():
        start_all(out_copies)
        start_all(up_copies)
        start_all(down_copies)
        sums[...] = jnp.zeros_like(sums)
        up_sums[...] = jnp.zeros_like(up_sums)
        wait_all(out_copies)

    width = ctx.shape[1]
    chunks = [slice(c * width, (c + 1) * width) for c in range(up_weight.shape[0] // width)]
    def work(rows):
        hidden = normalize(resid[rows, :])[0] * vecs[G2 : G2 + 1, :] + vecs[S2 : S2 + 1, :]
        mixed = hidden + dot_nt(ctx[rows, :], out_weight[...]) + vecs[OB : OB + 1, :]
        first_unit, first_rstd = normalize(mixed)
        combined = first_unit * vecs[G1 : G1 + 1, :] + vecs[S1 : S1 + 1, :]
        low = combined.astype(bf16)
        low_out[rows, :] = low
        yield
        for cols in chunks:
            act, slope = gelu_both(dot_nt(low, up_weight[cols, :]) + up_bias[0:1, cols])
            act = act.astype(bf16)
            act_out[rows, cols] = act
            slopes[rows, cols] = slope.astype(bf16)
            combined = combined + dot_nt(act, down_weight[:, cols])
            yield
        unit, rstd = normalize(combined + vecs[DB : DB + 1, :])
        gain = vecs[G2 : G2 + 1, :]
        alive = alive_col[rows, 0:1].astype(f32)
        outputs[rows, :] = ((unit * gain + vecs[S2 : S2 + 1, :]) * alive).astype(bf16)
        grad = cot[rows, :].astype(f32) * alive
        sums[0] += partial_sum(grad * unit)
        sums[1] += partial_sum(grad)
        grad = normalize_back(grad, gain, unit, rstd)
        yield
        yield from feed_back_rows(
            rows, chunks, grad, slopes, first_unit, first_rstd, vecs, down_weight, up_weight, out_weight,
            gb_out, gu_out, ga_out, gm_out, gctx_out, sums, up_sums,
        )

    def landed():
        wait_all(up_copies)
        wait_all(down_copies)

    in_turn([work(slice(p * SUB, (p + 1) * SUB)) for p in range(ctx.shape[0] // SUB)], first, landed)


def feed_back_rows(
    rows, chunks, grad, slopes, unit, rstd, vecs, down_weight, up_weight, out_weight,
    gb_out, gu_out, ga_out, gm_out, gctx_out, sums, up_sums,
):
    branch = grad.astype(bf16)
    gb_out[rows, :] = branch
    sums[2] += partial_sum(branch.astype(f32))
    for cols in chunks:
        grad_up = (dot_nn(branch, down_weight[:, cols]) * slopes[rows, cols].astype(f32)).astype(bf16)
        gu_out[rows, cols] = grad_up
        up_sums[:, cols] += partial_sum(grad_up.astype(f32))
        grad = grad + dot_nn(grad_up, up_weight[cols, :])
        yield
    sums[3] += partial_sum(grad * unit)
    sums[4] += partial_sum(grad)
    grad = normalize_back(grad, vecs[G1 : G1 + 1, :], unit, rstd)
    gm_out[rows, :] = grad
    attn = grad.astype(bf16)
    ga_out[rows, :] = attn
    sums[5] += partial_sum(attn.astype(f32))
    yield
    gctx_out[rows, :] = dot_nn(attn, out_weight[...]).astype(bf16)


def top(core, ctx, resid, cot, alive_col, vecs, up_bias, out_weight, up_weight, down_weight):
    count, width = ctx.shape
    wide = up_bias.shape[1]
    tile = pl.BlockSpec((TOP_TILE, width), lambda i: (i, 0))
    broad = pl.BlockSpec((TOP_TILE, wide), lambda i: (i, 0))
    low = jax.ShapeDtypeStruct((count, width), bf16)
    low_wide = jax.ShapeDtypeStruct((count, wide), bf16)
    return pl.pallas_call(
        top_kernel,
        grid=(count // TOP_TILE,),
        in_specs=[SMEM, tile, tile, tile, pl.BlockSpec((TOP_TILE, 128), lambda i: (i, 0)), whole((8, width)),
                  whole((8, wide))] + [ANY] * 6,
        out_specs=[tile, tile, broad, tile, broad, tile, tile, tile, whole((6, 8, width)), whole((8, wide))],
        out_shape=[low, low, low_wide, low, low_wide, low, jax.ShapeDtypeStruct((count, width), f32), low,
                   jax.ShapeDtypeStruct((6, 8, width), f32), jax.ShapeDtypeStruct((8, wide), f32)],
        scratch_shapes=[
            pltpu.VMEM((width, width), bf16),
            pltpu.VMEM((wide, width), bf16),
            pltpu.VMEM((width, wide), bf16),
            pltpu.VMEM((TOP_TILE, wide), bf16),
            pltpu.SemaphoreType.DMA((3, 8)),
        ],
        compiler_params=params(),
        cost_estimate=pl.CostEstimate(
            flops=4 * count * width * (width + 2 * wide),
            bytes_accessed=count * (width * 22 + wide * 4), transcendentals=0),
        name="top",
    )(core, ctx, resid, cot, alive_col, vecs, up_bias, *out_weight, *up_weight, *down_weight)


def lower_kernel(
    core_ref, grads, gm, combined, slope, mixed, vecs, d_own, d_sib, u_own, u_sib,
    o_own, o_sib, q_own, q_sib,
    gb_out, gu_out, ga_out, gm_out, gctx_out, sums, up_sums, down_weight, up_weight, out_weight, weights, sems,
):
    core = core_ref[0]
    first = pl.program_id(0) == 0
    down_copies = piece_copies(core, (d_own, d_sib), down_weight, sems.at[0])
    up_copies = piece_copies(core, (u_own, u_sib), up_weight, sems.at[1])
    out_copies = piece_copies(core, (o_own, o_sib), out_weight, sems.at[2])
    copies = [
        piece_copies(core, (q_own, q_sib), weights.at[w], sems.at[3 + w], w) for w in range(3)
    ]

    @pl.when(first)
    def _():
        for group in copies:
            start_all(group)
        start_all(down_copies)
        start_all(up_copies)
        start_all(out_copies)
        sums[...] = jnp.zeros_like(sums)
        up_sums[...] = jnp.zeros_like(up_sums)
        for group in copies:
            wait_all(group)

    width = gm.shape[1]
    chunks = [slice(c * width, (c + 1) * width) for c in range(up_weight.shape[0] // width)]
    def work(rows):
        grad = gm[rows, :]
        for w in range(3):
            grad = grad + dot_nn(grads[w, rows, :], weights[w])
        unit, rstd = normalize(combined[rows, :])
        sums[0] += partial_sum(grad * unit)
        sums[1] += partial_sum(grad)
        grad = normalize_back(grad, vecs[G2 : G2 + 1, :], unit, rstd)
        first_unit, first_rstd = normalize(mixed[rows, :])
        yield
        yield from feed_back_rows(
            rows, chunks, grad, slope, first_unit, first_rstd, vecs, down_weight, up_weight, out_weight,
            gb_out, gu_out, ga_out, gm_out, gctx_out, sums, up_sums,
        )

    def landed():
        wait_all(down_copies)
        wait_all(up_copies)
        wait_all(out_copies)

    in_turn([work(slice(p * SUB, (p + 1) * SUB)) for p in range(gm.shape[0] // SUB)], first, landed)


def lower(core, grads, gm, combined, slope, mixed, vecs, down_weight, up_weight, out_weight, qkv):
    count, width = mixed.shape
    wide = slope.shape[1]
    tile = pl.BlockSpec((TILE, width), lambda i: (i, 0))
    broad = pl.BlockSpec((TILE, wide), lambda i: (i, 0))
    low = jax.ShapeDtypeStruct((count, width), bf16)
    return pl.pallas_call(
        lower_kernel,
        grid=(count // TILE,),
        in_specs=[SMEM, pl.BlockSpec((3, TILE, width), lambda i: (0, i, 0)), tile, tile, broad, tile,
                  whole((8, width))] + [ANY] * 8,
        out_specs=[tile, broad, tile, tile, tile, whole((6, 8, width)), whole((8, wide))],
        out_shape=[low, jax.ShapeDtypeStruct((count, wide), bf16), low, jax.ShapeDtypeStruct((count, width), f32), low,
                   jax.ShapeDtypeStruct((6, 8, width), f32), jax.ShapeDtypeStruct((8, wide), f32)],
        scratch_shapes=[
            pltpu.VMEM((width, wide), bf16),
            pltpu.VMEM((wide, width), bf16),
            pltpu.VMEM((width, width), bf16),
            pltpu.VMEM((3, width, width), bf16),
            pltpu.SemaphoreType.DMA((6, 8)),
        ],
        compiler_params=params(),
        cost_estimate=pl.CostEstimate(
            flops=2 * count * width * (4 * width + 2 * wide),
            bytes_accessed=count * (width * 30 + wide * 4), transcendentals=0),
        name="lower",
    )(core, grads, gm, combined, slope, mixed, vecs, *down_weight, *up_weight, *out_weight, *qkv)


def attend_back_kernel(
    q, k, v, gctx, lse, seg_col, alive_col, seg_row, *rest
):
    grads, sums, mask = rest[-3:]

    @pl.when(pl.program_id(1) == 0)
    def _():
        mask_into(mask, seg_col, alive_col, seg_row)

    length = q.shape[0]
    lane = lax.broadcasted_iota(jnp.int32, (length, 2 * HEAD), 1)
    scaling = HEAD**-0.5
    for pair in range(2):
        cols = slice(pair * 2 * HEAD, (pair + 1) * 2 * HEAD)
        kp, vp, go = k[:, cols], v[:, cols], gctx[:, cols]
        qp = q[:, cols] * bf16(scaling)
        kt = kp.T
        dq_parts = []
        dk = dv = None
        for h in range(2):
            here = (lane >= HEAD) if h else (lane < HEAD)
            zero = bf16(0)
            qm, gm = jnp.where(here, qp, zero), jnp.where(here, go, zero)
            scores = dot_nt(kp, qm) + mask[...]
            probs = jnp.exp(scores - lse[0, 0, pl.ds(2 * pair + h, 1), :])
            weighted = probs * dot_nt(vp, gm)
            inner = jnp.sum(weighted, axis=0, keepdims=True)
            grad_scores = (weighted - probs * inner).astype(bf16)
            dv_h = dot_nn(probs.astype(bf16), gm)
            dk_h = dot_nn(grad_scores, qm)
            dv = dv_h if dv is None else dv + dv_h
            dk = dk_h if dk is None else dk + dk_h
            dq_parts.append(dot_nn(kt[h * HEAD : (h + 1) * HEAD], grad_scores))
        dq = (jnp.concatenate(dq_parts, axis=0).T * scaling).astype(bf16)
        dv = dv.astype(bf16)
        grads[0, :, cols] = dq
        grads[1, :, cols] = dk.astype(bf16)
        grads[2, :, cols] = dv
        sums[0, 0, :, cols] = partial_sum(dq.astype(f32))
        sums[0, 1, :, cols] = partial_sum(dv.astype(f32))


def attend_back(q, k, v, gctx, lse, seg_col, alive_col, seg_row, start=0, stop=None, before=()):
    count, width = q.shape
    rows, _, length = seg_row.shape
    stop = rows if stop is None else stop
    col = pl.BlockSpec((length, 128), lambda r, j: (r + start, 0))
    block = pl.BlockSpec((length, QUAD), lambda r, j: (r + start, j))
    share = (stop - start) / rows
    return pl.pallas_call(
        attend_back_kernel,
        grid=(stop - start, width // QUAD),
        in_specs=[block] * 4 + [pl.BlockSpec((1, 1, 8, length), lambda r, j: (r + start, j, 0, 0)), col, col,
                                pl.BlockSpec((1, 1, length), lambda r, j: (r + start, 0, 0))] + [ANY] * len(before),
        out_specs=[pl.BlockSpec((3, length, QUAD), lambda r, j: (0, r + start, j)),
                   pl.BlockSpec((1, 2, 8, QUAD), lambda r, j: (r + start, 0, 0, j))],
        out_shape=[jax.ShapeDtypeStruct((3, count, width), bf16), jax.ShapeDtypeStruct((rows, 2, 8, width), f32)],
        scratch_shapes=[pltpu.VMEM((length, length), f32)],
        input_output_aliases={8 + i: i for i in range(len(before))},
        compiler_params=params(),
        cost_estimate=pl.CostEstimate(
            flops=int(share * 4 * 10 * count * length * width),
            bytes_accessed=int(share * count * width * 16), transcendentals=0),
        name="attend_back",
    )(q, k, v, gctx, lse, seg_col, alive_col, seg_row, *before)


def input_back_kernel(core_ref, grads, gm, own, sib, grad_out, weights, sems):
    core = core_ref[0]
    copies = [
        piece_copies(core, (own, sib), weights.at[w], sems.at[w], w)
        for w in range(3)
    ]

    @pl.when(pl.program_id(0) == 0)
    def _():
        for group in copies:
            start_all(group)
        for group in copies:
            wait_all(group)

    grad = gm[...]
    for w in range(3):
        grad = grad + dot_nn(grads[w], weights[w])
    grad_out[...] = grad


def input_back(core, grads, gm, qkv):
    count, width = gm.shape
    tile = pl.BlockSpec((TILE, width), lambda i: (i, 0))
    return pl.pallas_call(
        input_back_kernel,
        grid=(count // TILE,),
        in_specs=[SMEM, pl.BlockSpec((3, TILE, width), lambda i: (0, i, 0)), tile] + [ANY] * 2,
        out_specs=tile,
        out_shape=jax.ShapeDtypeStruct((count, width), f32),
        scratch_shapes=[pltpu.VMEM((3, width, width), bf16), pltpu.SemaphoreType.DMA((3, 8))],
        compiler_params=params(),
        cost_estimate=pl.CostEstimate(
            flops=2 * count * width * width * 3, bytes_accessed=count * width * 14, transcendentals=0),
        name="input_back",
    )(core, grads, gm, *qkv)


def store_blocks(core, flip, total, put):
    rows = total.shape[0] // 4
    for block in range(4):
        x, c = block // 2, block % 2
        part = total[block * rows : (block + 1) * rows]
        for side in range(2):
            @pl.when(core == (c + side) % 2)
            def _():
                put(side, (x + flip) % 2, part)


def weight_grad_kernel(layers, place_ref, *refs):
    grads, inputs = refs[:layers], refs[layers : 2 * layers]
    outs = refs[2 * layers :]
    total = None
    for layer in range(layers):
        term = dot_tn(grads[layer][0], inputs[layer][...])
        total = term if total is None else total + term
    halves, wide = outs[0].shape[1], outs[0].shape[-1]

    def put(side, x, part):
        for half in range(halves):
            outs[side][0, half, x] = part[:, half * wide : (half + 1) * wide]

    store_blocks(place_ref[0], place_ref[1], total.astype(bf16), put)


def weight_grad(place, grads, inputs):
    layers = len(grads)
    count_w, span, n = grads[0].shape
    depth = inputs[0].shape[1]
    chunk = depth if depth <= n else depth // 6
    chunks = depth // chunk
    halves = 2 if chunks == 1 else 1
    wide = chunk // halves
    per_half = depth // 2 // wide
    rows = n // 4
    if chunks == 1:
        out_spec = pl.BlockSpec((1, 2, 2, rows, wide), lambda w, j: (w, 0, 0, 0, 0))
    else:
        out_spec = pl.BlockSpec((1, 1, 2, rows, wide), lambda w, j: (w, j // per_half, 0, 0, j % per_half))
    out = jax.ShapeDtypeStruct((count_w, 2, 2, rows, depth // 2), bf16)
    return pl.pallas_call(
        partial(weight_grad_kernel, layers),
        grid=(count_w, chunks),
        in_specs=[SMEM] + [pl.BlockSpec((1, span, n), lambda w, j: (w, 0, 0))] * layers
        + [pl.BlockSpec((span, chunk), lambda w, j: (0, j))] * layers,
        out_specs=[out_spec, out_spec],
        out_shape=[out, out],
        compiler_params=params(),
        cost_estimate=pl.CostEstimate(
            flops=2 * layers * span * n * depth * count_w,
            bytes_accessed=2 * layers * span * (n * count_w + depth) + 2 * n * depth * count_w, transcendentals=0),
        name="weight_grad",
    )(place, *grads, *inputs)


def joint_grad_kernel(layers, small, tall, place_ref, *refs):
    grads, inputs = refs[:layers], refs[layers : 2 * layers]
    bias_sums, norm_sums, up_sums = (refs[(2 + i) * layers : (3 + i) * layers] for i in range(3))
    keep, send, totals, short = refs[5 * layers :]
    core, flip = place_ref[0], place_ref[1]
    which = pl.program_id(0)
    sides, _, blocks, _, half = keep.shape
    width = totals.shape[1]
    rows = width // 4

    def slot(block):
        return 2 * ((block // 2 + flip) % 2) + (block % 2 + core) % 2

    total = None
    for layer in range(layers):
        term = dot_tn(grads[layer][0], inputs[layer][...])
        total = term if total is None else total + term
    for block in range(4):
        totals[which, pl.ds(pl.multiple_of(slot(block) * rows, rows), rows), :] = total[block * rows : (block + 1) * rows]

    @pl.when(which == 0)
    def _():
        bias = sum(jnp.sum(ref[...], axis=(0, 2)) for ref in bias_sums)
        norm = sum(jnp.sum(ref[...], axis=1) for ref in norm_sums)
        up = sum(jnp.sum(ref[...], axis=0, keepdims=True) for ref in up_sums)
        rest = [norm[n : n + 1] for n in (5, 3, 4, 2, 0, 1)]
        lines = jnp.concatenate([bias[0:1], bias[1:2], *rest], axis=0)
        short[...] = jnp.zeros_like(short)
        quarter = up.shape[1] // 4
        for block in range(4):
            place = slot(block)
            here = pltpu.roll(lines, lax.rem(width - place * rows, width), 1)
            above = jnp.where(place == 0, up[:, :quarter], 0.0)
            for index in range(1, 4):
                above = above + jnp.where(place == index, up[:, index * quarter : (index + 1) * quarter], 0.0)
            above = jnp.broadcast_to(above, (8, quarter))
            for zy in range(blocks):
                first = pltpu.roll(here, (width - zy * small) % width, 1)[:, :128]
                second = pltpu.roll(above, (quarter - zy * tall) % quarter, 1)[:, :128]
                short[block, zy, :, 0:128] = first
                short[block, zy, :, 128:256] = second

    @pl.when(which == pl.num_programs(0) - 1)
    def _():
        for block in range(4):
            out = (keep, send)[block % 2]
            for zy in range(blocks):
                start = block * rows + zy * small
                for side in range(sides):
                    cols = slice(side * half, (side + 1) * half)
                    parts = [totals[w, start : start + small, cols] for w in range(totals.shape[0])]
                    out[side, block // 2, zy] = jnp.concatenate([*parts, short[block, zy, :, cols]], axis=0).astype(bf16)


def joint_grad(place, grads, inputs, bias_sums, norm_sums, up_sums, small, tall):
    layers = len(grads)
    count, span, n = grads[0].shape
    depth = inputs[0].shape[1]
    blocks = n // 4 // small
    lines = count * small + 8
    out = jax.ShapeDtypeStruct((2, 2, blocks, lines, depth // 2), bf16)
    sums = [*bias_sums, *norm_sums, *up_sums]
    return pl.pallas_call(
        partial(joint_grad_kernel, layers, small, tall),
        grid=(count,),
        in_specs=[SMEM] + [pl.BlockSpec((1, span, n), lambda w: (w, 0, 0))] * layers + [whole((span, depth))] * layers
        + [whole(v.shape) for v in sums],
        out_specs=[whole(out.shape)] * 2,
        out_shape=[out, out],
        scratch_shapes=[
            pltpu.VMEM((count, n, depth), f32),
            pltpu.VMEM((4, blocks, 8, depth), f32),
        ],
        compiler_params=params(),
        cost_estimate=pl.CostEstimate(
            flops=2 * layers * span * n * depth * count,
            bytes_accessed=2 * layers * span * (n * count + depth) + 2 * n * depth * count, transcendentals=0),
        name="joint_grad",
    )(place, *grads, *inputs, *sums)


def tall_grad_kernel(layers, place_ref, *refs):
    tall, tall_in, flat, flat_in = (refs[i * layers : (i + 1) * layers] for i in range(4))
    keep, send, turned, flat_total = refs[4 * layers :]
    step = pl.program_id(0)
    core, flip = place_ref[0], place_ref[1]
    sides, _, blocks, rows, half = keep.shape
    flat_rows = flat_total.shape[0] // 4
    small = flat_rows // blocks
    large = rows - small

    def product(left, right):
        total = None
        for layer in range(layers):
            term = dot_tn(left[layer][...], right[layer][...])
            total = term if total is None else total + term
        return total

    @pl.when(step == 0)
    def _():
        total = product(flat, flat_in)
        for block in range(4):
            slot = 2 * ((block // 2 + flip) % 2) + (block % 2 + core) % 2
            flat_total[pl.ds(pl.multiple_of(slot * flat_rows, flat_rows), flat_rows), :] = (
                total[block * flat_rows : (block + 1) * flat_rows]
            )

    @pl.when(step > 0)
    def _():
        turned[...] = product(tall, tall_in).astype(bf16)
        slot = step - 1
        for c, out in ((0, keep), (1, send)):
            @pl.when(slot % 2 == c)
            def _():
                for side in range(sides):
                    cols = slice(side * half, (side + 1) * half)
                    for block in range(blocks):
                        out[side, 0, block, :large, :] = turned[block * large : (block + 1) * large, cols]
                        start = pl.multiple_of(slot * flat_rows + block * small, 8)
                        out[side, 0, block, large:, :] = flat_total[pl.ds(start, small), cols].astype(bf16)


def tall_grad(place, tall, tall_in, flat, flat_in):
    layers = len(tall)
    span, n = tall[0].shape
    depth = tall_in[0].shape[1]
    flat_n = flat[0].shape[1]
    rows = n // 4

    def column(s, place):
        slot = jnp.maximum(s - 1, 0)
        return 0, 2 * ((slot // 2 + place[1]) % 2) + (slot % 2 + place[0]) % 2

    def fixed(shape):
        return pl.BlockSpec(shape, lambda s, place: (0, 0))

    blocks = 8
    share = (n + flat_n) // 4 // blocks
    out_spec = pl.BlockSpec(
        (2, 1, blocks, share, depth // 2), lambda s, place: (0, jnp.maximum(s - 1, 0) // 2, 0, 0, 0)
    )
    out = jax.ShapeDtypeStruct((2, 2, blocks, share, depth // 2), bf16)
    return pl.pallas_call(
        partial(tall_grad_kernel, layers),
        grid_spec=pltpu.PrefetchScalarGridSpec(
            num_scalar_prefetch=1,
            grid=(5,),
            in_specs=[pl.BlockSpec((span, rows), column)] * layers + [fixed((span, depth))] * layers
            + [fixed((span, flat_n))] * layers + [fixed((span, depth))] * layers,
            out_specs=[out_spec, out_spec],
            scratch_shapes=[pltpu.VMEM((rows, depth), bf16), pltpu.VMEM((flat_n, depth), f32)],
        ),
        out_shape=[out, out],
        compiler_params=params(),
        cost_estimate=pl.CostEstimate(
            flops=2 * layers * span * (n + flat_n) * depth,
            bytes_accessed=2 * layers * span * (n + flat_n + 2 * depth) + 2 * (n + flat_n) * depth, transcendentals=0),
        name="tall_grad",
    )(place, *tall, *tall_in, *flat, *flat_in)


def pack_kernel(weights, *refs):
    parts, out, rows = refs[:-2], refs[-2], refs[-1]
    rows[...] = jnp.zeros_like(rows)
    start = 0
    for part in parts[:weights]:
        rows[start : start + part.shape[0], :] = part[...].astype(f32)
        start += part.shape[0]
    for index, part in enumerate(parts[weights:-1]):
        rows[start + index : start + index + 1, : part.shape[1]] = part[...].astype(f32)
    rows[start : start + 1, 128 : 128 + parts[-1].shape[1]] = parts[-1][...].astype(f32)
    out[...] = rows[...].astype(bf16)


def pack(vectors, weights=()):
    parts = [*weights, *(vector[None] for vector in vectors)]
    shape = (sum(weight.shape[0] for weight in weights) + 8, weights[0].shape[1] if weights else 256)
    return pl.pallas_call(
        partial(pack_kernel, len(weights)),
        in_specs=[whole(part.shape) for part in parts],
        out_specs=whole(shape),
        out_shape=jax.ShapeDtypeStruct(shape, bf16),
        scratch_shapes=[pltpu.VMEM(shape, f32)],
        name="pack",
    )(*parts)


AXES = ("dp", "fsdp")


def halves(v):
    middle = v.shape[-1] // 2
    return v[..., :middle], v[..., middle:]


def tie(value, after):
    return value if after is None else lax.optimization_barrier((value, after))[0]


class Chain:
    def __init__(self, stages):
        self.stages, self.result, self.landed = stages, None, None
        self.step()

    def step(self, after=None):
        if self.stages is None:
            return self.landed
        try:
            self.landed = self.stages.send(after) if self.landed is not None else next(self.stages)
        except StopIteration as end:
            self.result = end.value
            self.stages = None
        return self.landed

    def finish(self, after=None):
        while self.stages is not None:
            self.step(after)
        return self.result


class Plain:
    def __init__(self, mesh):
        self.devices = math.prod(mesh.shape.values())
        self.sent = None

    def place(self):
        return jnp.zeros((2,), jnp.int32)

    def spread(self, shards, vectors=None):
        def pieces(full):
            blocks = full.reshape(full.shape[:-2] + (2, 2, full.shape[-2] // 4, full.shape[-1]))
            return tuple(jnp.stack(halves(blocks[..., core, :, :]), axis=-4) for core in range(2))

        full = [lax.all_gather(shard, AXES, axis=0, tiled=True) for shard in shards]
        yield full[0]
        if vectors is None:
            return [pieces(weight) for weight in full]
        return pieces(jnp.stack(full)), lax.all_gather(pack(vectors), AXES, axis=0, tiled=False)

    def reduce(self, keep, send):
        count, sides, xs, rows, half = keep.shape
        both = jnp.stack([keep, send], axis=3).astype(f32)
        full = jnp.moveaxis(both, 1, 4).reshape(count, xs * 2 * rows, sides * half)
        full = lax.psum_scatter(full, AXES, scatter_dimension=1, tiled=True)
        yield full
        return full

    def reduce_joined(self, keep, send, tall, flat):
        large = keep.shape[3] * tall // (tall + flat)
        results = []
        for rows in (slice(0, large), slice(large, None)):
            sides, xs, half = keep.shape[0], keep.shape[1], keep.shape[-1]
            parts = [v[:, :, :, rows].reshape(1, sides, xs, -1, half) for v in (keep, send)]
            results.append(Chain(self.reduce(*parts)).finish())
        yield results[0]
        return jnp.concatenate(results, axis=1)

    def joint_grad(self, place, grads, inputs, bias_sums, norm_sums, up_sums, small, tall):
        bias = sum(jnp.sum(v, axis=(0, 2)) for v in bias_sums)
        norm = sum(jnp.sum(v, axis=1) for v in norm_sums)
        up = sum(jnp.sum(v, axis=0) for v in up_sums)
        lines = jnp.stack([bias[0], bias[1], norm[5], norm[3], norm[4], norm[2], norm[0], norm[1]])
        lines = lines.reshape(8, self.devices, small).transpose(1, 0, 2)
        return (*weight_grad(place, grads, inputs), lines, up.reshape(self.devices, tall))

    def reduce_joint(self, keep, send, lines, up):
        full = Chain(self.reduce(keep, send)).finish()
        lines = lax.psum_scatter(lines, AXES, scatter_dimension=0, tiled=True)[0]
        up = lax.psum_scatter(up, AXES, scatter_dimension=0, tiled=True)
        rows = full.reshape(-1, full.shape[-1])
        yield rows
        short = jnp.zeros((8, full.shape[-1]), f32).at[:, : lines.shape[1]].set(lines).at[:1, 128 : 128 + up.shape[1]].set(up)
        return jnp.concatenate([rows, short], axis=0)


class Grid:
    def __init__(self, mesh):
        self.sent = None

    def where(self):
        dp, fsdp = lax.axis_index("dp"), lax.axis_index("fsdp")
        return dp // 2, dp % 2, fsdp // 2, fsdp % 2

    def place(self):
        x, core, _, _ = self.where()
        return jnp.stack([core, x]).astype(jnp.int32)

    def swap(self, value, x=0, core=0, z=0, y=0):
        flip = ((x * 2 + core) * 4 + z) * 2 + y
        return lax.ppermute(value, AXES, [(i, i ^ flip) for i in range(32)])

    def ordered(self, mine, other, side, axis=0):
        return jnp.stack([jnp.where(side == 0, mine, other), jnp.where(side == 0, other, mine)], axis=axis)

    def ordered_z(self, parts, z):
        odd, high = z % 2, z // 2
        parts = [jnp.where(odd == 0, parts[k], parts[k ^ 1]) for k in range(4)]
        return jnp.stack([jnp.where(high == 0, parts[k], parts[k ^ 2]) for k in range(4)])

    def spread(self, shards, vectors=None):
        x, core, z, y = self.where()
        if vectors is not None:
            payload = pack(vectors, shards)
        else:
            payload = jnp.concatenate(shards, axis=0) if len(shards) > 1 else shards[0]
        parts = [payload] + [self.swap(payload, z=k) for k in range(1, 4)]
        parts = tie(parts, (yield parts[1:]))
        left, right = halves(self.ordered_z(parts, z))
        got = self.swap(left, x=1), self.swap(right, y=1)
        got = tie(got, (yield got))
        left = self.ordered(left, got[0], x)
        right = self.ordered(right, got[1], y, axis=1)
        got = self.swap(left, y=1), self.swap(right, x=1)
        got = tie(got, (yield got))
        left = self.ordered(left, got[0], y, axis=2)
        right = self.ordered(right, got[1], x)
        own, start = [], 0
        for shard in shards:
            rows = shard.shape[0]
            own.append(jnp.stack([v[:, :, :, start : start + rows].reshape(2, 8 * rows, -1) for v in (left, right)]))
            start += rows
        if vectors is not None:
            own = [jnp.stack(own), left[:, :, :, start:, :256]]
        other = [self.swap(mine, core=1) for mine in own]
        other = tie(other, (yield other))
        if vectors is None:
            return list(zip(own, other))
        vectors = self.ordered(own[1], other[1], core, axis=1)
        return (own[0], other[0]), vectors.reshape(32, 8, 256)

    def reduce(self, keep, send):
        _, _, z, y = self.where()
        count, _, _, rows, half = keep.shape
        mine = rows // 8

        def add(a, b):
            return (a.astype(f32) + b.astype(f32)).astype(bf16)

        def pick(v, index, axis):
            return lax.dynamic_index_in_dim(v, index, axis, keepdims=False)

        got = self.swap(send, core=1)
        got = tie(got, (yield got))
        total = add(keep, got).reshape(count, 2, 2, 4, 2, mine, half)
        left, right = total[:, 0], total[:, 1]
        self.sent = left[:, 1], pick(right, 1 - y, 3)
        got = self.swap(self.sent[0], x=1), self.swap(self.sent[1], y=1)
        got = tie(got, (yield got))
        left, right = add(left[:, 0], got[0]), add(pick(right, y, 3), got[1])
        self.sent = pick(left, 1 - y, 2), right[:, 1]
        got = self.swap(self.sent[0], y=1), self.swap(self.sent[1], x=1)
        got = tie(got, (yield got))
        left, right = add(pick(left, y, 2), got[0]), add(right[:, 0], got[1])
        both = jnp.concatenate([left, right], axis=-1)
        got = [self.swap(pick(both, z ^ k, 1), z=k) for k in range(1, 4)]
        got = tie(got, (yield got))
        result = pick(both, z, 1).astype(f32)
        for part in got:
            result = result + part.astype(f32)
        return result

    def reduce_joined(self, keep, send, tall, flat):
        shape = (1, 2, 2, -1, keep.shape[-1])
        return self.reduce(keep.reshape(shape), send.reshape(shape))

    def joint_grad(self, *operands):
        return joint_grad(*operands)

    def reduce_joint(self, keep, send):
        shape = (1, 2, 2, -1, keep.shape[-1])
        result = yield from self.reduce(keep.reshape(shape), send.reshape(shape))
        return result[0]


def column_info(values, count):
    return jnp.broadcast_to(values.reshape(count, 1), (count, 128))


def body(
    exchange,
    tokens,
    cotangent,
    segment_ids,
    pad_mask,
    row_counts,
    query_weight,
    query_bias,
    key_weight,
    value_weight,
    value_bias,
    out_weight,
    out_bias,
    first_gain,
    first_shift,
    up_weight,
    up_bias,
    down_weight,
    down_bias,
    second_gain,
    second_shift,
):
    rows_here, row_len, width = tokens.shape
    count = rows_here * row_len
    small, tall = query_bias.shape[0], up_bias.shape[0]
    place = exchange.place()

    first = Chain(
        exchange.spread(
            [query_weight, key_weight, value_weight],
            [query_bias, value_bias, out_bias, first_gain, first_shift, down_bias, second_gain, second_shift, up_bias],
        )
    )
    z_landed = first.landed
    first.step()
    second = Chain(exchange.spread(tie([out_weight, up_weight], z_landed)))
    first.step()
    xy_landed = first.landed
    first.step()
    down_full = lax.all_gather(tie(down_weight, (xy_landed, second.landed)), AXES, axis=0, tiled=True)
    second.step(xy_landed)
    qkv, vectors = first.finish()
    vectors = vectors.astype(f32)
    devices = vectors.shape[0]
    wide = tall * devices
    vecs = vectors[:, :, :small].transpose(1, 0, 2).reshape(8, width)
    up_vec = jnp.broadcast_to(vectors[:, 0, 128 : 128 + tall].reshape(1, wide), (8, wide))

    present = (jnp.arange(rows_here, dtype=jnp.int32) < row_counts[0]).astype(jnp.int32)
    alive = pad_mask * present[:, None]
    alive_col = column_info(alive, count)
    seg_col = column_info(segment_ids, count)
    seg_row = segment_ids.reshape(rows_here, 1, row_len)
    info = (seg_col, alive_col, seg_row)
    flat = tokens.reshape(count, width)

    landed = second.landed
    lower_kept = attend_forward(place, flat, *info, vecs, qkv, 0, 2)
    second.step(lower_kept[3])
    lower_kept = attend_forward(place, tie(flat, landed), *info, vecs, qkv, 2, None, lower_kept)
    second.step(lower_kept[3])
    out_w, up_w = second.finish()
    mixed, lower_low, lower_act, slope = widen(place, lower_kept[3], flat, vecs, up_vec, out_w, up_w)
    down_w = (down_full, down_full)
    combined, inputs = narrow(place, lower_act, mixed, vecs, down_w)

    upper_kept = attend_forward(place, inputs, *info, vecs, qkv)
    outputs, upper_low, upper_act, upper_gb, upper_gu, upper_ga, gm, gctx, sums, up_sums = top(
        place, upper_kept[3], combined, cotangent.reshape(count, width), alive_col, vecs, up_vec, out_w, up_w, down_w
    )
    upper_grads, bias_sums = attend_back(*upper_kept[:3], gctx, upper_kept[4], *info)
    lower_gb, lower_gu, lower_ga, gm, gctx, more_sums, more_up_sums = lower(
        place, upper_grads, gm, combined, slope, mixed, vecs, down_w, up_w, out_w, qkv
    )

    keep, send = weight_grad(place, [upper_gb[None], lower_gb[None]], [upper_act, lower_act])
    down_sum = Chain(exchange.reduce(keep, send))
    keep, send = tall_grad(
        place, [upper_gu, tie(lower_gu, keep)], [upper_low, lower_low], [upper_ga, lower_ga], [upper_kept[3], lower_kept[3]]
    )
    up_sum = Chain(exchange.reduce_joined(keep, send, tall, small))
    landed = down_sum.landed
    down_sum.step()
    lower_grads, more_bias_sums = attend_back(*lower_kept[:3], tie(gctx, (keep, landed)), lower_kept[4], *info)
    landed = (up_sum.landed, down_sum.landed)
    up_sum.step()
    down_sum.step()
    joint = exchange.joint_grad(
        place, [upper_grads, tie(lower_grads, landed)], [inputs, flat],
        [bias_sums, more_bias_sums], [sums, more_sums], [up_sums, more_up_sums], small, tall,
    )
    qkv_sum = Chain(exchange.reduce_joint(*joint))
    landed = (up_sum.landed, down_sum.landed)
    up_sum.step()
    ready = exchange.sent
    down_sum.step()
    tokens_grad = input_back(place, tie(lower_grads, (joint[0], landed, ready) if ready is not None else joint[0]), gm, qkv)
    qkv_sum.step(tokens_grad)
    up_sum.step(tokens_grad if exchange.sent is None else (tokens_grad, exchange.sent))
    down_grad = down_sum.finish(tokens_grad)[0]
    up_out = up_sum.finish()[0]
    joint = qkv_sum.finish()
    query_grad, key_grad, value_grad = (joint[i * small : (i + 1) * small] for i in range(3))
    lines = joint[3 * small :]
    piece = [lines[i, :small] for i in range(8)]
    return (
        outputs.reshape(rows_here, row_len, width),
        tokens_grad.reshape(rows_here, row_len, width),
        query_grad,
        piece[QB],
        key_grad,
        value_grad,
        piece[VB],
        up_out[tall:],
        piece[OB],
        piece[G1],
        piece[S1],
        up_out[:tall],
        lines[0, 128 : 128 + tall],
        down_grad,
        piece[DB],
        piece[G2],
        piece[S2],
    )


def solution(mesh):
    rows = P(AXES, None, None)
    flat = P(AXES, None)
    line = P(AXES)
    matrices = (flat, line, flat, flat, line, flat, line, line, line, flat, line, flat, line, line, line)
    exchange = Grid(mesh) if dict(mesh.shape) == {"dp": 4, "fsdp": 8} else Plain(mesh)
    return jax.shard_map(
        partial(body, exchange),
        mesh=mesh,
        in_specs=(rows, rows, flat, flat, line) + matrices,
        out_specs=(rows, rows) + matrices,
        check_vma=False,
    )
```

```python
from functools import partial
import math

import jax
import jax.numpy as jnp
from jax import lax
from jax.experimental import pallas as pl
from jax.experimental.pallas import tpu as pltpu
from jax.sharding import PartitionSpec as P

HEAD = 64
LAYERS = 2
QUAD = 4 * HEAD
TILE = 256
SUB = 256
TOP_TILE = 512
norm_eps = 1e-06
masked_score = -1000000000.0
VMEM = 60 * 1024 * 1024
bf16 = jnp.bfloat16
f32 = jnp.float32

QB, VB, OB, G1, S1, DB, G2, S2 = range(8)


def dot_nt(left, right):
    return lax.dot_general(left, right, (((1,), (1,)), ((), ())), preferred_element_type=f32)


def dot_nn(left, right):
    return lax.dot_general(left, right, (((1,), (0,)), ((), ())), preferred_element_type=f32)


def dot_tn(left, right):
    return lax.dot_general(left, right, (((0,), (0,)), ((), ())), preferred_element_type=f32)


def normalize(v):
    mean = jnp.mean(v, axis=-1, keepdims=True)
    centered = v - mean
    rstd = lax.rsqrt(jnp.mean(centered * centered, axis=-1, keepdims=True) + norm_eps)
    return centered * rstd, rstd


def normalize_back(grad, gain, unit, rstd):
    scaled = grad * gain
    first = jnp.mean(scaled, axis=-1, keepdims=True)
    second = jnp.mean(scaled * unit, axis=-1, keepdims=True)
    return rstd * (scaled - first - unit * second)


def partial_sum(v):
    return jnp.sum(v.reshape(v.shape[0] // 8, 8, v.shape[1]), axis=0)


def piece_copies(core, pieces, place, sems, which=None):
    copies = []
    for sibling, piece in enumerate(pieces):
        source = piece if which is None else piece.at[which]
        if len(source.shape) == 2:
            rows = source.shape[0] // 2
            part = slice(sibling * rows, (sibling + 1) * rows)
            copies.append(pltpu.make_async_copy(source.at[part, :], place.at[part, :], sems.at[4 * sibling]))
            continue
        sides, _, rows, half = source.shape
        for side in range(sides):
            for x in range(2):
                slot = 2 * x + (1 - core if sibling else core)
                start = pl.multiple_of(slot * rows, rows)
                copies.append(
                    pltpu.make_async_copy(
                        source.at[side, x],
                        place.at[pl.ds(start, rows), pl.ds(side * half, half)],
                        sems.at[4 * sibling + 2 * side + x],
                    )
                )
    return copies


def start_all(copies):
    for copy in copies:
        copy.start()


def wait_all(copies):
    for copy in copies:
        copy.wait()


def params():
    return pltpu.CompilerParams(vmem_limit_bytes=VMEM)


ANY = pl.BlockSpec(memory_space=pl.ANY)
SMEM = pl.BlockSpec(memory_space=pltpu.SMEM)


def whole(shape):
    return pl.BlockSpec(shape, lambda *_: (0,) * len(shape))


def mask_into(mask, seg_col, alive_col, seg_row):
    length = mask.shape[0]
    key = lax.broadcasted_iota(jnp.int32, (length, length), 0)
    query = lax.broadcasted_iota(jnp.int32, (length, length), 1)
    same = seg_col[:, 0:1] == seg_row[0]
    allowed = same & ((alive_col[:, 0:1] > 0) | (key == query))
    mask[...] = jnp.where(allowed, 0.0, masked_score)


def attend_forward_kernel(
    start, core_ref, x, seg_col, alive_col, seg_row, vecs, own, sib, *rest
):
    q_out, k_out, v_out, ctx_out, lse_out, weights, mask, sems = rest[-8:]
    quad = (pl.program_id(0) + start) % (weights.shape[1] // QUAD)
    core = core_ref[0]
    first = pl.program_id(0) == 0
    copies = [
        piece_copies(core, (own, sib), weights.at[w], sems.at[w], w)
        for w in range(3)
    ]

    @pl.when(first)
    def _():
        for group in copies:
            start_all(group)

    @pl.when(first | (quad == 0))
    def _():
        mask_into(mask, seg_col, alive_col, seg_row)

    @pl.when(first)
    def _():
        for group in copies:
            wait_all(group)

    inputs = x[...]
    heads = pl.ds(pl.multiple_of(quad * QUAD, QUAD), QUAD)
    queries = (dot_nt(inputs, weights[0, heads, :]) + vecs[QB : QB + 1, :]).astype(bf16)
    keys = dot_nt(inputs, weights[1, heads, :]).astype(bf16)
    values = (dot_nt(inputs, weights[2, heads, :]) + vecs[VB : VB + 1, :]).astype(bf16)
    q_out[...] = queries
    k_out[...] = keys
    v_out[...] = values
    scaled = queries * bf16(HEAD**-0.5)
    length = inputs.shape[0]
    lane = lax.broadcasted_iota(jnp.int32, (length, 2 * HEAD), 1)
    for pair in range(2):
        cols = slice(pair * 2 * HEAD, (pair + 1) * 2 * HEAD)
        kp, qp = keys[:, cols], scaled[:, cols]
        vt = values[:, cols].T
        parts = []
        for h in range(2):
            km = jnp.where((lane >= HEAD) if h else (lane < HEAD), kp, bf16(0))
            scores = dot_nt(km, qp) + mask[...]
            highest = jnp.max(scores, axis=0, keepdims=True)
            weight = jnp.exp(scores - highest)
            total = jnp.sum(weight, axis=0, keepdims=True)
            parts.append(dot_nn(vt[h * HEAD : (h + 1) * HEAD], weight.astype(bf16)) / total)
            lse_out[0, 0, pl.ds(2 * pair + h, 1), :] = highest + jnp.log(total)
        ctx_out[:, cols] = jnp.concatenate(parts, axis=0).T.astype(bf16)


def attend_forward(core, x, seg_col, alive_col, seg_row, vecs, qkv, start=0, stop=None, before=()):
    count, width = x.shape
    rows, _, length = seg_row.shape
    quads = width // QUAD
    stop = rows * quads if stop is None else stop

    def row(s):
        return (s + start) // quads

    def quad(s):
        return (s + start) % quads

    full = pl.BlockSpec((length, width), lambda s: (row(s), 0))
    col = pl.BlockSpec((length, 128), lambda s: (row(s), 0))
    block = pl.BlockSpec((length, QUAD), lambda s: (row(s), quad(s)))
    low = jax.ShapeDtypeStruct((count, width), bf16)
    share = (stop - start) / (rows * quads)
    return pl.pallas_call(
        partial(attend_forward_kernel, start),
        grid=(stop - start,),
        in_specs=[SMEM, full, col, col, pl.BlockSpec((1, 1, length), lambda s: (row(s), 0, 0)),
                  pl.BlockSpec((8, QUAD), lambda s: (0, quad(s))), ANY, ANY] + [ANY] * len(before),
        out_specs=[block] * 4 + [pl.BlockSpec((1, 1, 8, length), lambda s: (row(s), quad(s), 0, 0))],
        out_shape=[low] * 4 + [jax.ShapeDtypeStruct((rows, quads, 8, length), f32)],
        scratch_shapes=[
            pltpu.VMEM((3, width, width), bf16),
            pltpu.VMEM((length, length), f32),
            pltpu.SemaphoreType.DMA((3, 8)),
        ],
        input_output_aliases={8 + i: i for i in range(len(before))},
        compiler_params=params(),
        cost_estimate=pl.CostEstimate(
            flops=int(share * (2 * count * width * width * 3 + 4 * 4 * count * length * width)),
            bytes_accessed=int(share * count * width * 10) + 3 * width * width * 2, transcendentals=0),
        name="attend_forward",
    )(core, x, seg_col, alive_col, seg_row, vecs, *qkv, *before)


GELU_A = math.sqrt(2.0 / math.pi)
GELU_B = 0.044715


def gelu_both(u):
    square = u * u
    t = jnp.tanh(u * (GELU_A + (GELU_A * GELU_B) * square))
    half = 0.5 + 0.5 * t
    slope = half + (u * (1.0 - t * t)) * (0.5 * GELU_A + (1.5 * GELU_A * GELU_B) * square)
    return u * half, slope


def widen_kernel(
    core_ref, ctx, resid, vecs, up_bias, o_own, o_sib, u_own, u_sib,
    mixed_out, low_out, act_out, slope_out, out_weight, up_weight, sems,
):
    core = core_ref[0]
    first = pl.program_id(0) == 0
    out_copies = piece_copies(core, (o_own, o_sib), out_weight, sems.at[0])
    up_copies = piece_copies(core, (u_own, u_sib), up_weight, sems.at[1])

    @pl.when(first)
    def _():
        start_all(out_copies)
        start_all(up_copies)
        wait_all(out_copies)

    mixed = resid[...].astype(f32) + dot_nt(ctx[...], out_weight[...]) + vecs[OB : OB + 1, :]
    mixed_out[...] = mixed
    normed = normalize(mixed)[0] * vecs[G1 : G1 + 1, :] + vecs[S1 : S1 + 1, :]
    low = normed.astype(bf16)
    low_out[...] = low

    @pl.when(first)
    def _():
        wait_all(up_copies)

    width = low.shape[1]
    for chunk in range(up_weight.shape[0] // width):
        cols = slice(chunk * width, (chunk + 1) * width)
        upward = dot_nt(low, up_weight[cols, :]) + up_bias[0:1, cols]
        act, slope = gelu_both(upward)
        act_out[:, cols] = act.astype(bf16)
        slope_out[:, cols] = slope.astype(bf16)


def widen(core, ctx, resid, vecs, up_bias, out_weight, up_weight):
    count, width = ctx.shape
    wide = up_bias.shape[1]
    tile = pl.BlockSpec((TILE, width), lambda i: (i, 0))
    broad = pl.BlockSpec((TILE, wide), lambda i: (i, 0))
    return pl.pallas_call(
        widen_kernel,
        grid=(count // TILE,),
        in_specs=[SMEM, tile, tile, whole((8, width)), whole((8, wide))] + [ANY] * 4,
        out_specs=[tile, tile, broad, broad],
        out_shape=[
            jax.ShapeDtypeStruct((count, width), f32),
            jax.ShapeDtypeStruct((count, width), bf16),
            jax.ShapeDtypeStruct((count, wide), bf16),
            jax.ShapeDtypeStruct((count, wide), bf16),
        ],
        scratch_shapes=[
            pltpu.VMEM((width, width), bf16),
            pltpu.VMEM((wide, width), bf16),
            pltpu.SemaphoreType.DMA((2, 8)),
        ],
        compiler_params=params(),
        cost_estimate=pl.CostEstimate(
            flops=2 * count * width * (width + wide),
            bytes_accessed=count * (width * 12 + wide * 4), transcendentals=0),
        name="widen",
    )(core, ctx, resid, vecs, up_bias, *out_weight, *up_weight)


def narrow_kernel(core_ref, act, mixed, vecs, d_own, d_sib, combined_out, low_out, down_weight, sems):
    core = core_ref[0]
    copies = piece_copies(core, (d_own, d_sib), down_weight, sems)

    @pl.when(pl.program_id(0) == 0)
    def _():
        start_all(copies)
        wait_all(copies)

    normed = normalize(mixed[...])[0] * vecs[G1 : G1 + 1, :] + vecs[S1 : S1 + 1, :]
    combined = normed + dot_nt(act[...], down_weight[...]) + vecs[DB : DB + 1, :]
    combined_out[...] = combined
    hidden = normalize(combined)[0] * vecs[G2 : G2 + 1, :] + vecs[S2 : S2 + 1, :]
    low_out[...] = hidden.astype(bf16)


def narrow(core, act, mixed, vecs, down_weight):
    count, width = mixed.shape
    wide = act.shape[1]
    tile = pl.BlockSpec((TILE, width), lambda i: (i, 0))
    broad = pl.BlockSpec((TILE, wide), lambda i: (i, 0))
    return pl.pallas_call(
        narrow_kernel,
        grid=(count // TILE,),
        in_specs=[SMEM, broad, tile, whole((8, width))] + [ANY] * 2,
        out_specs=[tile, tile],
        out_shape=[jax.ShapeDtypeStruct((count, width), f32), jax.ShapeDtypeStruct((count, width), bf16)],
        scratch_shapes=[pltpu.VMEM((width, wide), bf16), pltpu.SemaphoreType.DMA((8,))],
        compiler_params=params(),
        cost_estimate=pl.CostEstimate(
            flops=2 * count * width * wide, bytes_accessed=count * (width * 10 + wide * 2), transcendentals=0),
        name="narrow",
    )(core, act, mixed, vecs, *down_weight)


def add_rows(out, first, values):
    @pl.when(first)
    def _():
        out[...] = jnp.zeros_like(out)

    for index, value in enumerate(values):
        out[index] += partial_sum(value)


def in_turn(parts, first, landed):
    live = parts
    turn = 0
    while live:
        live = [part for part in live if next(part, live) is not live]
        if turn == 0:
            pl.when(first)(landed)
        turn += 1


def top_kernel(
    core_ref, ctx, resid, cot, alive_col, vecs, up_bias,
    o_own, o_sib, u_own, u_sib, d_own, d_sib,
    outputs, low_out, act_out, gb_out, gu_out, ga_out, gm_out, gctx_out, sums, up_sums,
    out_weight, up_weight, down_weight, slopes, sems,
):
    core = core_ref[0]
    first = pl.program_id(0) == 0
    out_copies = piece_copies(core, (o_own, o_sib), out_weight, sems.at[0])
    up_copies = piece_copies(core, (u_own, u_sib), up_weight, sems.at[1])
    down_copies = piece_copies(core, (d_own, d_sib), down_weight, sems.at[2])

    @pl.when(first)
    def _():
        start_all(out_copies)
        start_all(up_copies)
        start_all(down_copies)
        sums[...] = jnp.zeros_like(sums)
        up_sums[...] = jnp.zeros_like(up_sums)
        wait_all(out_copies)

    width = ctx.shape[1]
    chunks = [slice(c * width, (c + 1) * width) for c in range(up_weight.shape[0] // width)]
    def work(rows):
        hidden = normalize(resid[rows, :])[0] * vecs[G2 : G2 + 1, :] + vecs[S2 : S2 + 1, :]
        mixed = hidden + dot_nt(ctx[rows, :], out_weight[...]) + vecs[OB : OB + 1, :]
        first_unit, first_rstd = normalize(mixed)
        combined = first_unit * vecs[G1 : G1 + 1, :] + vecs[S1 : S1 + 1, :]
        low = combined.astype(bf16)
        low_out[rows, :] = low
        yield
        for cols in chunks:
            act, slope = gelu_both(dot_nt(low, up_weight[cols, :]) + up_bias[0:1, cols])
            act = act.astype(bf16)
            act_out[rows, cols] = act
            slopes[rows, cols] = slope.astype(bf16)
            combined = combined + dot_nt(act, down_weight[:, cols])
            yield
        unit, rstd = normalize(combined + vecs[DB : DB + 1, :])
        gain = vecs[G2 : G2 + 1, :]
        alive = alive_col[rows, 0:1].astype(f32)
        outputs[rows, :] = ((unit * gain + vecs[S2 : S2 + 1, :]) * alive).astype(bf16)
        grad = cot[rows, :].astype(f32) * alive
        sums[0] += partial_sum(grad * unit)
        sums[1] += partial_sum(grad)
        grad = normalize_back(grad, gain, unit, rstd)
        yield
        yield from feed_back_rows(
            rows, chunks, grad, slopes, first_unit, first_rstd, vecs, down_weight, up_weight, out_weight,
            gb_out, gu_out, ga_out, gm_out, gctx_out, sums, up_sums,
        )

    def landed():
        wait_all(up_copies)
        wait_all(down_copies)

    in_turn([work(slice(p * SUB, (p + 1) * SUB)) for p in range(ctx.shape[0] // SUB)], first, landed)


def feed_back_rows(
    rows, chunks, grad, slopes, unit, rstd, vecs, down_weight, up_weight, out_weight,
    gb_out, gu_out, ga_out, gm_out, gctx_out, sums, up_sums,
):
    branch = grad.astype(bf16)
    gb_out[rows, :] = branch
    sums[2] += partial_sum(branch.astype(f32))
    for cols in chunks:
        grad_up = (dot_nn(branch, down_weight[:, cols]) * slopes[rows, cols].astype(f32)).astype(bf16)
        gu_out[rows, cols] = grad_up
        up_sums[:, cols] += partial_sum(grad_up.astype(f32))
        grad = grad + dot_nn(grad_up, up_weight[cols, :])
        yield
    sums[3] += partial_sum(grad * unit)
    sums[4] += partial_sum(grad)
    grad = normalize_back(grad, vecs[G1 : G1 + 1, :], unit, rstd)
    gm_out[rows, :] = grad
    attn = grad.astype(bf16)
    ga_out[rows, :] = attn
    sums[5] += partial_sum(attn.astype(f32))
    yield
    gctx_out[rows, :] = dot_nn(attn, out_weight[...]).astype(bf16)


def top(core, ctx, resid, cot, alive_col, vecs, up_bias, out_weight, up_weight, down_weight):
    count, width = ctx.shape
    wide = up_bias.shape[1]
    tile = pl.BlockSpec((TOP_TILE, width), lambda i: (i, 0))
    broad = pl.BlockSpec((TOP_TILE, wide), lambda i: (i, 0))
    low = jax.ShapeDtypeStruct((count, width), bf16)
    low_wide = jax.ShapeDtypeStruct((count, wide), bf16)
    return pl.pallas_call(
        top_kernel,
        grid=(count // TOP_TILE,),
        in_specs=[SMEM, tile, tile, tile, pl.BlockSpec((TOP_TILE, 128), lambda i: (i, 0)), whole((8, width)),
                  whole((8, wide))] + [ANY] * 6,
        out_specs=[tile, tile, broad, tile, broad, tile, tile, tile, whole((6, 8, width)), whole((8, wide))],
        out_shape=[low, low, low_wide, low, low_wide, low, jax.ShapeDtypeStruct((count, width), f32), low,
                   jax.ShapeDtypeStruct((6, 8, width), f32), jax.ShapeDtypeStruct((8, wide), f32)],
        scratch_shapes=[
            pltpu.VMEM((width, width), bf16),
            pltpu.VMEM((wide, width), bf16),
            pltpu.VMEM((width, wide), bf16),
            pltpu.VMEM((TOP_TILE, wide), bf16),
            pltpu.SemaphoreType.DMA((3, 8)),
        ],
        compiler_params=params(),
        cost_estimate=pl.CostEstimate(
            flops=4 * count * width * (width + 2 * wide),
            bytes_accessed=count * (width * 22 + wide * 4), transcendentals=0),
        name="top",
    )(core, ctx, resid, cot, alive_col, vecs, up_bias, *out_weight, *up_weight, *down_weight)


def lower_kernel(
    core_ref, grads, gm, combined, slope, mixed, vecs, d_own, d_sib, u_own, u_sib,
    o_own, o_sib, q_own, q_sib,
    gb_out, gu_out, ga_out, gm_out, gctx_out, sums, up_sums, down_weight, up_weight, out_weight, weights, sems,
):
    core = core_ref[0]
    first = pl.program_id(0) == 0
    down_copies = piece_copies(core, (d_own, d_sib), down_weight, sems.at[0])
    up_copies = piece_copies(core, (u_own, u_sib), up_weight, sems.at[1])
    out_copies = piece_copies(core, (o_own, o_sib), out_weight, sems.at[2])
    copies = [
        piece_copies(core, (q_own, q_sib), weights.at[w], sems.at[3 + w], w) for w in range(3)
    ]

    @pl.when(first)
    def _():
        for group in copies:
            start_all(group)
        start_all(down_copies)
        start_all(up_copies)
        start_all(out_copies)
        sums[...] = jnp.zeros_like(sums)
        up_sums[...] = jnp.zeros_like(up_sums)
        for group in copies:
            wait_all(group)

    width = gm.shape[1]
    chunks = [slice(c * width, (c + 1) * width) for c in range(up_weight.shape[0] // width)]
    def work(rows):
        grad = gm[rows, :]
        for w in range(3):
            grad = grad + dot_nn(grads[w, rows, :], weights[w])
        unit, rstd = normalize(combined[rows, :])
        sums[0] += partial_sum(grad * unit)
        sums[1] += partial_sum(grad)
        grad = normalize_back(grad, vecs[G2 : G2 + 1, :], unit, rstd)
        first_unit, first_rstd = normalize(mixed[rows, :])
        yield
        yield from feed_back_rows(
            rows, chunks, grad, slope, first_unit, first_rstd, vecs, down_weight, up_weight, out_weight,
            gb_out, gu_out, ga_out, gm_out, gctx_out, sums, up_sums,
        )

    def landed():
        wait_all(down_copies)
        wait_all(up_copies)
        wait_all(out_copies)

    in_turn([work(slice(p * SUB, (p + 1) * SUB)) for p in range(gm.shape[0] // SUB)], first, landed)


def lower(core, grads, gm, combined, slope, mixed, vecs, down_weight, up_weight, out_weight, qkv):
    count, width = mixed.shape
    wide = slope.shape[1]
    tile = pl.BlockSpec((TILE, width), lambda i: (i, 0))
    broad = pl.BlockSpec((TILE, wide), lambda i: (i, 0))
    low = jax.ShapeDtypeStruct((count, width), bf16)
    return pl.pallas_call(
        lower_kernel,
        grid=(count // TILE,),
        in_specs=[SMEM, pl.BlockSpec((3, TILE, width), lambda i: (0, i, 0)), tile, tile, broad, tile,
                  whole((8, width))] + [ANY] * 8,
        out_specs=[tile, broad, tile, tile, tile, whole((6, 8, width)), whole((8, wide))],
        out_shape=[low, jax.ShapeDtypeStruct((count, wide), bf16), low, jax.ShapeDtypeStruct((count, width), f32), low,
                   jax.ShapeDtypeStruct((6, 8, width), f32), jax.ShapeDtypeStruct((8, wide), f32)],
        scratch_shapes=[
            pltpu.VMEM((width, wide), bf16),
            pltpu.VMEM((wide, width), bf16),
            pltpu.VMEM((width, width), bf16),
            pltpu.VMEM((3, width, width), bf16),
            pltpu.SemaphoreType.DMA((6, 8)),
        ],
        compiler_params=params(),
        cost_estimate=pl.CostEstimate(
            flops=2 * count * width * (4 * width + 2 * wide),
            bytes_accessed=count * (width * 30 + wide * 4), transcendentals=0),
        name="lower",
    )(core, grads, gm, combined, slope, mixed, vecs, *down_weight, *up_weight, *out_weight, *qkv)


def attend_back_kernel(
    q, k, v, gctx, lse, seg_col, alive_col, seg_row, *rest
):
    grads, sums, mask = rest[-3:]

    @pl.when(pl.program_id(1) == 0)
    def _():
        mask_into(mask, seg_col, alive_col, seg_row)

    length = q.shape[0]
    lane = lax.broadcasted_iota(jnp.int32, (length, 2 * HEAD), 1)
    scaling = HEAD**-0.5
    for pair in range(2):
        cols = slice(pair * 2 * HEAD, (pair + 1) * 2 * HEAD)
        kp, vp, go = k[:, cols], v[:, cols], gctx[:, cols]
        qp = q[:, cols] * bf16(scaling)
        kt = kp.T
        dq_parts = []
        dk = dv = None
        for h in range(2):
            here = (lane >= HEAD) if h else (lane < HEAD)
            zero = bf16(0)
            qm, gm = jnp.where(here, qp, zero), jnp.where(here, go, zero)
            scores = dot_nt(kp, qm) + mask[...]
            probs = jnp.exp(scores - lse[0, 0, pl.ds(2 * pair + h, 1), :])
            weighted = probs * dot_nt(vp, gm)
            inner = jnp.sum(weighted, axis=0, keepdims=True)
            grad_scores = (weighted - probs * inner).astype(bf16)
            dv_h = dot_nn(probs.astype(bf16), gm)
            dk_h = dot_nn(grad_scores, qm)
            dv = dv_h if dv is None else dv + dv_h
            dk = dk_h if dk is None else dk + dk_h
            dq_parts.append(dot_nn(kt[h * HEAD : (h + 1) * HEAD], grad_scores))
        dq = (jnp.concatenate(dq_parts, axis=0).T * scaling).astype(bf16)
        dv = dv.astype(bf16)
        grads[0, :, cols] = dq
        grads[1, :, cols] = dk.astype(bf16)
        grads[2, :, cols] = dv
        sums[0, 0, :, cols] = partial_sum(dq.astype(f32))
        sums[0, 1, :, cols] = partial_sum(dv.astype(f32))


def attend_back(q, k, v, gctx, lse, seg_col, alive_col, seg_row, start=0, stop=None, before=()):
    count, width = q.shape
    rows, _, length = seg_row.shape
    stop = rows if stop is None else stop
    col = pl.BlockSpec((length, 128), lambda r, j: (r + start, 0))
    block = pl.BlockSpec((length, QUAD), lambda r, j: (r + start, j))
    share = (stop - start) / rows
    return pl.pallas_call(
        attend_back_kernel,
        grid=(stop - start, width // QUAD),
        in_specs=[block] * 4 + [pl.BlockSpec((1, 1, 8, length), lambda r, j: (r + start, j, 0, 0)), col, col,
                                pl.BlockSpec((1, 1, length), lambda r, j: (r + start, 0, 0))] + [ANY] * len(before),
        out_specs=[pl.BlockSpec((3, length, QUAD), lambda r, j: (0, r + start, j)),
                   pl.BlockSpec((1, 2, 8, QUAD), lambda r, j: (r + start, 0, 0, j))],
        out_shape=[jax.ShapeDtypeStruct((3, count, width), bf16), jax.ShapeDtypeStruct((rows, 2, 8, width), f32)],
        scratch_shapes=[pltpu.VMEM((length, length), f32)],
        input_output_aliases={8 + i: i for i in range(len(before))},
        compiler_params=params(),
        cost_estimate=pl.CostEstimate(
            flops=int(share * 4 * 10 * count * length * width),
            bytes_accessed=int(share * count * width * 16), transcendentals=0),
        name="attend_back",
    )(q, k, v, gctx, lse, seg_col, alive_col, seg_row, *before)


def input_back_kernel(core_ref, grads, gm, own, sib, grad_out, weights, sems):
    core = core_ref[0]
    copies = [
        piece_copies(core, (own, sib), weights.at[w], sems.at[w], w)
        for w in range(3)
    ]

    @pl.when(pl.program_id(0) == 0)
    def _():
        for group in copies:
            start_all(group)
        for group in copies:
            wait_all(group)

    grad = gm[...]
    for w in range(3):
        grad = grad + dot_nn(grads[w], weights[w])
    grad_out[...] = grad


def input_back(core, grads, gm, qkv):
    count, width = gm.shape
    tile = pl.BlockSpec((TILE, width), lambda i: (i, 0))
    return pl.pallas_call(
        input_back_kernel,
        grid=(count // TILE,),
        in_specs=[SMEM, pl.BlockSpec((3, TILE, width), lambda i: (0, i, 0)), tile] + [ANY] * 2,
        out_specs=tile,
        out_shape=jax.ShapeDtypeStruct((count, width), f32),
        scratch_shapes=[pltpu.VMEM((3, width, width), bf16), pltpu.SemaphoreType.DMA((3, 8))],
        compiler_params=params(),
        cost_estimate=pl.CostEstimate(
            flops=2 * count * width * width * 3, bytes_accessed=count * width * 14, transcendentals=0),
        name="input_back",
    )(core, grads, gm, *qkv)


def store_blocks(core, flip, total, put):
    rows = total.shape[0] // 4
    for block in range(4):
        x, c = block // 2, block % 2
        part = total[block * rows : (block + 1) * rows]
        for side in range(2):
            @pl.when(core == (c + side) % 2)
            def _():
                put(side, (x + flip) % 2, part)


def weight_grad_kernel(layers, place_ref, *refs):
    grads, inputs = refs[:layers], refs[layers : 2 * layers]
    outs = refs[2 * layers :]
    total = None
    for layer in range(layers):
        term = dot_tn(grads[layer][0], inputs[layer][...])
        total = term if total is None else total + term
    halves, wide = outs[0].shape[1], outs[0].shape[-1]

    def put(side, x, part):
        for half in range(halves):
            outs[side][0, half, x] = part[:, half * wide : (half + 1) * wide]

    store_blocks(place_ref[0], place_ref[1], total.astype(bf16), put)


def weight_grad(place, grads, inputs):
    layers = len(grads)
    count_w, span, n = grads[0].shape
    depth = inputs[0].shape[1]
    chunk = depth if depth <= n else depth // 6
    chunks = depth // chunk
    halves = 2 if chunks == 1 else 1
    wide = chunk // halves
    per_half = depth // 2 // wide
    rows = n // 4
    if chunks == 1:
        out_spec = pl.BlockSpec((1, 2, 2, rows, wide), lambda w, j: (w, 0, 0, 0, 0))
    else:
        out_spec = pl.BlockSpec((1, 1, 2, rows, wide), lambda w, j: (w, j // per_half, 0, 0, j % per_half))
    out = jax.ShapeDtypeStruct((count_w, 2, 2, rows, depth // 2), bf16)
    return pl.pallas_call(
        partial(weight_grad_kernel, layers),
        grid=(count_w, chunks),
        in_specs=[SMEM] + [pl.BlockSpec((1, span, n), lambda w, j: (w, 0, 0))] * layers
        + [pl.BlockSpec((span, chunk), lambda w, j: (0, j))] * layers,
        out_specs=[out_spec, out_spec],
        out_shape=[out, out],
        compiler_params=params(),
        cost_estimate=pl.CostEstimate(
            flops=2 * layers * span * n * depth * count_w,
            bytes_accessed=2 * layers * span * (n * count_w + depth) + 2 * n * depth * count_w, transcendentals=0),
        name="weight_grad",
    )(place, *grads, *inputs)


def joint_grad_kernel(layers, small, tall, place_ref, *refs):
    grads, inputs = refs[:layers], refs[layers : 2 * layers]
    bias_sums, norm_sums, up_sums = (refs[(2 + i) * layers : (3 + i) * layers] for i in range(3))
    keep, send, totals, short = refs[5 * layers :]
    core, flip = place_ref[0], place_ref[1]
    which = pl.program_id(0)
    sides, _, blocks, _, half = keep.shape
    width = totals.shape[1]
    rows = width // 4

    def slot(block):
        return 2 * ((block // 2 + flip) % 2) + (block % 2 + core) % 2

    total = None
    for layer in range(layers):
        term = dot_tn(grads[layer][0], inputs[layer][...])
        total = term if total is None else total + term
    for block in range(4):
        totals[which, pl.ds(pl.multiple_of(slot(block) * rows, rows), rows), :] = total[block * rows : (block + 1) * rows]

    @pl.when(which == 0)
    def _():
        bias = sum(jnp.sum(ref[...], axis=(0, 2)) for ref in bias_sums)
        norm = sum(jnp.sum(ref[...], axis=1) for ref in norm_sums)
        up = sum(jnp.sum(ref[...], axis=0, keepdims=True) for ref in up_sums)
        rest = [norm[n : n + 1] for n in (5, 3, 4, 2, 0, 1)]
        lines = jnp.concatenate([bias[0:1], bias[1:2], *rest], axis=0)
        short[...] = jnp.zeros_like(short)
        quarter = up.shape[1] // 4
        for block in range(4):
            place = slot(block)
            here = pltpu.roll(lines, lax.rem(width - place * rows, width), 1)
            above = jnp.where(place == 0, up[:, :quarter], 0.0)
            for index in range(1, 4):
                above = above + jnp.where(place == index, up[:, index * quarter : (index + 1) * quarter], 0.0)
            above = jnp.broadcast_to(above, (8, quarter))
            for zy in range(blocks):
                first = pltpu.roll(here, (width - zy * small) % width, 1)[:, :128]
                second = pltpu.roll(above, (quarter - zy * tall) % quarter, 1)[:, :128]
                short[block, zy, :, 0:128] = first
                short[block, zy, :, 128:256] = second

    @pl.when(which == pl.num_programs(0) - 1)
    def _():
        for block in range(4):
            out = (keep, send)[block % 2]
            for zy in range(blocks):
                start = block * rows + zy * small
                for side in range(sides):
                    cols = slice(side * half, (side + 1) * half)
                    parts = [totals[w, start : start + small, cols] for w in range(totals.shape[0])]
                    out[side, block // 2, zy] = jnp.concatenate([*parts, short[block, zy, :, cols]], axis=0).astype(bf16)


def joint_grad(place, grads, inputs, bias_sums, norm_sums, up_sums, small, tall):
    layers = len(grads)
    count, span, n = grads[0].shape
    depth = inputs[0].shape[1]
    blocks = n // 4 // small
    lines = count * small + 8
    out = jax.ShapeDtypeStruct((2, 2, blocks, lines, depth // 2), bf16)
    sums = [*bias_sums, *norm_sums, *up_sums]
    return pl.pallas_call(
        partial(joint_grad_kernel, layers, small, tall),
        grid=(count,),
        in_specs=[SMEM] + [pl.BlockSpec((1, span, n), lambda w: (w, 0, 0))] * layers + [whole((span, depth))] * layers
        + [whole(v.shape) for v in sums],
        out_specs=[whole(out.shape)] * 2,
        out_shape=[out, out],
        scratch_shapes=[
            pltpu.VMEM((count, n, depth), f32),
            pltpu.VMEM((4, blocks, 8, depth), f32),
        ],
        compiler_params=params(),
        cost_estimate=pl.CostEstimate(
            flops=2 * layers * span * n * depth * count,
            bytes_accessed=2 * layers * span * (n * count + depth) + 2 * n * depth * count, transcendentals=0),
        name="joint_grad",
    )(place, *grads, *inputs, *sums)


def tall_grad_kernel(layers, place_ref, *refs):
    tall, tall_in, flat, flat_in = (refs[i * layers : (i + 1) * layers] for i in range(4))
    keep, send, turned, flat_total = refs[4 * layers :]
    step = pl.program_id(0)
    core, flip = place_ref[0], place_ref[1]
    sides, _, blocks, rows, half = keep.shape
    flat_rows = flat_total.shape[0] // 4
    small = flat_rows // blocks
    large = rows - small

    def product(left, right):
        total = None
        for layer in range(layers):
            term = dot_tn(left[layer][...], right[layer][...])
            total = term if total is None else total + term
        return total

    @pl.when(step == 0)
    def _():
        total = product(flat, flat_in)
        for block in range(4):
            slot = 2 * ((block // 2 + flip) % 2) + (block % 2 + core) % 2
            flat_total[pl.ds(pl.multiple_of(slot * flat_rows, flat_rows), flat_rows), :] = (
                total[block * flat_rows : (block + 1) * flat_rows]
            )

    @pl.when(step > 0)
    def _():
        turned[...] = product(tall, tall_in).astype(bf16)
        slot = step - 1
        for c, out in ((0, keep), (1, send)):
            @pl.when(slot % 2 == c)
            def _():
                for side in range(sides):
                    cols = slice(side * half, (side + 1) * half)
                    for block in range(blocks):
                        out[side, 0, block, :large, :] = turned[block * large : (block + 1) * large, cols]
                        start = pl.multiple_of(slot * flat_rows + block * small, 8)
                        out[side, 0, block, large:, :] = flat_total[pl.ds(start, small), cols].astype(bf16)


def tall_grad(place, tall, tall_in, flat, flat_in):
    layers = len(tall)
    span, n = tall[0].shape
    depth = tall_in[0].shape[1]
    flat_n = flat[0].shape[1]
    rows = n // 4

    def column(s, place):
        slot = jnp.maximum(s - 1, 0)
        return 0, 2 * ((slot // 2 + place[1]) % 2) + (slot % 2 + place[0]) % 2

    def fixed(shape):
        return pl.BlockSpec(shape, lambda s, place: (0, 0))

    blocks = 8
    share = (n + flat_n) // 4 // blocks
    out_spec = pl.BlockSpec(
        (2, 1, blocks, share, depth // 2), lambda s, place: (0, jnp.maximum(s - 1, 0) // 2, 0, 0, 0)
    )
    out = jax.ShapeDtypeStruct((2, 2, blocks, share, depth // 2), bf16)
    return pl.pallas_call(
        partial(tall_grad_kernel, layers),
        grid_spec=pltpu.PrefetchScalarGridSpec(
            num_scalar_prefetch=1,
            grid=(5,),
            in_specs=[pl.BlockSpec((span, rows), column)] * layers + [fixed((span, depth))] * layers
            + [fixed((span, flat_n))] * layers + [fixed((span, depth))] * layers,
            out_specs=[out_spec, out_spec],
            scratch_shapes=[pltpu.VMEM((rows, depth), bf16), pltpu.VMEM((flat_n, depth), f32)],
        ),
        out_shape=[out, out],
        compiler_params=params(),
        cost_estimate=pl.CostEstimate(
            flops=2 * layers * span * (n + flat_n) * depth,
            bytes_accessed=2 * layers * span * (n + flat_n + 2 * depth) + 2 * (n + flat_n) * depth, transcendentals=0),
        name="tall_grad",
    )(place, *tall, *tall_in, *flat, *flat_in)


def pack_kernel(weights, *refs):
    parts, out, rows = refs[:-2], refs[-2], refs[-1]
    rows[...] = jnp.zeros_like(rows)
    start = 0
    for part in parts[:weights]:
        rows[start : start + part.shape[0], :] = part[...].astype(f32)
        start += part.shape[0]
    for index, part in enumerate(parts[weights:-1]):
        rows[start + index : start + index + 1, : part.shape[1]] = part[...].astype(f32)
    rows[start : start + 1, 128 : 128 + parts[-1].shape[1]] = parts[-1][...].astype(f32)
    out[...] = rows[...].astype(bf16)


def pack(vectors, weights=()):
    parts = [*weights, *(vector[None] for vector in vectors)]
    shape = (sum(weight.shape[0] for weight in weights) + 8, weights[0].shape[1] if weights else 256)
    return pl.pallas_call(
        partial(pack_kernel, len(weights)),
        in_specs=[whole(part.shape) for part in parts],
        out_specs=whole(shape),
        out_shape=jax.ShapeDtypeStruct(shape, bf16),
        scratch_shapes=[pltpu.VMEM(shape, f32)],
        name="pack",
    )(*parts)


AXES = ("dp", "fsdp")


def halves(v):
    middle = v.shape[-1] // 2
    return v[..., :middle], v[..., middle:]


def tie(value, after):
    return value if after is None else lax.optimization_barrier((value, after))[0]


class Chain:
    def __init__(self, stages):
        self.stages, self.result, self.landed = stages, None, None
        self.step()

    def step(self, after=None):
        if self.stages is None:
            return self.landed
        try:
            self.landed = self.stages.send(after) if self.landed is not None else next(self.stages)
        except StopIteration as end:
            self.result = end.value
            self.stages = None
        return self.landed

    def finish(self, after=None):
        while self.stages is not None:
            self.step(after)
        return self.result


class Plain:
    def __init__(self, mesh):
        self.devices = math.prod(mesh.shape.values())
        self.sent = None

    def place(self):
        return jnp.zeros((2,), jnp.int32)

    def spread(self, shards, vectors=None):
        def pieces(full):
            blocks = full.reshape(full.shape[:-2] + (2, 2, full.shape[-2] // 4, full.shape[-1]))
            return tuple(jnp.stack(halves(blocks[..., core, :, :]), axis=-4) for core in range(2))

        full = [lax.all_gather(shard, AXES, axis=0, tiled=True) for shard in shards]
        yield full[0]
        if vectors is None:
            return [pieces(weight) for weight in full]
        return pieces(jnp.stack(full)), lax.all_gather(pack(vectors), AXES, axis=0, tiled=False)

    def reduce(self, keep, send):
        count, sides, xs, rows, half = keep.shape
        both = jnp.stack([keep, send], axis=3).astype(f32)
        full = jnp.moveaxis(both, 1, 4).reshape(count, xs * 2 * rows, sides * half)
        full = lax.psum_scatter(full, AXES, scatter_dimension=1, tiled=True)
        yield full
        return full

    def reduce_joined(self, keep, send, tall, flat):
        large = keep.shape[3] * tall // (tall + flat)
        results = []
        for rows in (slice(0, large), slice(large, None)):
            sides, xs, half = keep.shape[0], keep.shape[1], keep.shape[-1]
            parts = [v[:, :, :, rows].reshape(1, sides, xs, -1, half) for v in (keep, send)]
            results.append(Chain(self.reduce(*parts)).finish())
        yield results[0]
        return jnp.concatenate(results, axis=1)

    def joint_grad(self, place, grads, inputs, bias_sums, norm_sums, up_sums, small, tall):
        bias = sum(jnp.sum(v, axis=(0, 2)) for v in bias_sums)
        norm = sum(jnp.sum(v, axis=1) for v in norm_sums)
        up = sum(jnp.sum(v, axis=0) for v in up_sums)
        lines = jnp.stack([bias[0], bias[1], norm[5], norm[3], norm[4], norm[2], norm[0], norm[1]])
        lines = lines.reshape(8, self.devices, small).transpose(1, 0, 2)
        return (*weight_grad(place, grads, inputs), lines, up.reshape(self.devices, tall))

    def reduce_joint(self, keep, send, lines, up):
        full = Chain(self.reduce(keep, send)).finish()
        lines = lax.psum_scatter(lines, AXES, scatter_dimension=0, tiled=True)[0]
        up = lax.psum_scatter(up, AXES, scatter_dimension=0, tiled=True)
        rows = full.reshape(-1, full.shape[-1])
        yield rows
        short = jnp.zeros((8, full.shape[-1]), f32).at[:, : lines.shape[1]].set(lines).at[:1, 128 : 128 + up.shape[1]].set(up)
        return jnp.concatenate([rows, short], axis=0)


class Grid:
    def __init__(self, mesh):
        self.sent = None

    def where(self):
        dp, fsdp = lax.axis_index("dp"), lax.axis_index("fsdp")
        return dp // 2, dp % 2, fsdp // 2, fsdp % 2

    def place(self):
        x, core, _, _ = self.where()
        return jnp.stack([core, x]).astype(jnp.int32)

    def swap(self, value, x=0, core=0, z=0, y=0):
        flip = ((x * 2 + core) * 4 + z) * 2 + y
        return lax.ppermute(value, AXES, [(i, i ^ flip) for i in range(32)])

    def ordered(self, mine, other, side, axis=0):
        return jnp.stack([jnp.where(side == 0, mine, other), jnp.where(side == 0, other, mine)], axis=axis)

    def ordered_z(self, parts, z):
        odd, high = z % 2, z // 2
        parts = [jnp.where(odd == 0, parts[k], parts[k ^ 1]) for k in range(4)]
        return jnp.stack([jnp.where(high == 0, parts[k], parts[k ^ 2]) for k in range(4)])

    def spread(self, shards, vectors=None):
        x, core, z, y = self.where()
        if vectors is not None:
            payload = pack(vectors, shards)
        else:
            payload = jnp.concatenate(shards, axis=0) if len(shards) > 1 else shards[0]
        parts = [payload] + [self.swap(payload, z=k) for k in range(1, 4)]
        parts = tie(parts, (yield parts[1:]))
        left, right = halves(self.ordered_z(parts, z))
        got = self.swap(left, x=1), self.swap(right, y=1)
        got = tie(got, (yield got))
        left = self.ordered(left, got[0], x)
        right = self.ordered(right, got[1], y, axis=1)
        got = self.swap(left, y=1), self.swap(right, x=1)
        got = tie(got, (yield got))
        left = self.ordered(left, got[0], y, axis=2)
        right = self.ordered(right, got[1], x)
        own, start = [], 0
        for shard in shards:
            rows = shard.shape[0]
            own.append(jnp.stack([v[:, :, :, start : start + rows].reshape(2, 8 * rows, -1) for v in (left, right)]))
            start += rows
        if vectors is not None:
            own = [jnp.stack(own), left[:, :, :, start:, :256]]
        other = [self.swap(mine, core=1) for mine in own]
        other = tie(other, (yield other))
        if vectors is None:
            return list(zip(own, other))
        vectors = self.ordered(own[1], other[1], core, axis=1)
        return (own[0], other[0]), vectors.reshape(32, 8, 256)

    def reduce(self, keep, send):
        _, _, z, y = self.where()
        count, _, _, rows, half = keep.shape
        mine = rows // 8

        def add(a, b):
            return (a.astype(f32) + b.astype(f32)).astype(bf16)

        def pick(v, index, axis):
            return lax.dynamic_index_in_dim(v, index, axis, keepdims=False)

        got = self.swap(send, core=1)
        got = tie(got, (yield got))
        total = add(keep, got).reshape(count, 2, 2, 4, 2, mine, half)
        left, right = total[:, 0], total[:, 1]
        self.sent = left[:, 1], pick(right, 1 - y, 3)
        got = self.swap(self.sent[0], x=1), self.swap(self.sent[1], y=1)
        got = tie(got, (yield got))
        left, right = add(left[:, 0], got[0]), add(pick(right, y, 3), got[1])
        self.sent = pick(left, 1 - y, 2), right[:, 1]
        got = self.swap(self.sent[0], y=1), self.swap(self.sent[1], x=1)
        got = tie(got, (yield got))
        left, right = add(pick(left, y, 2), got[0]), add(right[:, 0], got[1])
        both = jnp.concatenate([left, right], axis=-1)
        got = [self.swap(pick(both, z ^ k, 1), z=k) for k in range(1, 4)]
        got = tie(got, (yield got))
        result = pick(both, z, 1).astype(f32)
        for part in got:
            result = result + part.astype(f32)
        return result

    def reduce_joined(self, keep, send, tall, flat):
        shape = (1, 2, 2, -1, keep.shape[-1])
        return self.reduce(keep.reshape(shape), send.reshape(shape))

    def joint_grad(self, *operands):
        return joint_grad(*operands)

    def reduce_joint(self, keep, send):
        shape = (1, 2, 2, -1, keep.shape[-1])
        result = yield from self.reduce(keep.reshape(shape), send.reshape(shape))
        return result[0]


def column_info(values, count):
    return jnp.broadcast_to(values.reshape(count, 1), (count, 128))


def body(
    exchange,
    tokens,
    cotangent,
    segment_ids,
    pad_mask,
    row_counts,
    query_weight,
    query_bias,
    key_weight,
    value_weight,
    value_bias,
    out_weight,
    out_bias,
    first_gain,
    first_shift,
    up_weight,
    up_bias,
    down_weight,
    down_bias,
    second_gain,
    second_shift,
):
    rows_here, row_len, width = tokens.shape
    count = rows_here * row_len
    small, tall = query_bias.shape[0], up_bias.shape[0]
    place = exchange.place()

    present = (jnp.arange(rows_here, dtype=jnp.int32) < row_counts[0]).astype(jnp.int32)
    alive = pad_mask * present[:, None]
    alive_col = column_info(alive, count)
    seg_col = column_info(segment_ids, count)

    first = Chain(
        exchange.spread(
            [query_weight, key_weight, value_weight],
            [query_bias, value_bias, out_bias, first_gain, first_shift, down_bias, second_gain, second_shift, up_bias],
        )
    )
    z_landed = first.landed
    first.step()
    second = Chain(exchange.spread(tie([out_weight, up_weight], z_landed)))
    first.step()
    xy_landed = first.landed
    first.step((seg_col, alive_col))
    down_full = lax.all_gather(tie(down_weight, (xy_landed, second.landed)), AXES, axis=0, tiled=True)
    second.step(xy_landed)
    qkv, vectors = first.finish()
    vectors = vectors.astype(f32)
    devices = vectors.shape[0]
    wide = tall * devices
    vecs = vectors[:, :, :small].transpose(1, 0, 2).reshape(8, width)
    up_vec = jnp.broadcast_to(vectors[:, 0, 128 : 128 + tall].reshape(1, wide), (8, wide))

    seg_row = segment_ids.reshape(rows_here, 1, row_len)
    info = (seg_col, alive_col, seg_row)
    flat = tokens.reshape(count, width)

    landed = second.landed
    lower_kept = attend_forward(place, flat, *info, vecs, qkv, 0, 2)
    second.step(lower_kept[3])
    lower_kept = attend_forward(place, tie(flat, landed), *info, vecs, qkv, 2, None, lower_kept)
    second.step(lower_kept[3])
    out_w, up_w = second.finish()
    mixed, lower_low, lower_act, slope = widen(place, lower_kept[3], flat, vecs, up_vec, out_w, up_w)
    down_w = (down_full, down_full)
    combined, inputs = narrow(place, lower_act, mixed, vecs, down_w)

    upper_kept = attend_forward(place, inputs, *info, vecs, qkv)
    outputs, upper_low, upper_act, upper_gb, upper_gu, upper_ga, gm, gctx, sums, up_sums = top(
        place, upper_kept[3], combined, cotangent.reshape(count, width), alive_col, vecs, up_vec, out_w, up_w, down_w
    )
    upper_grads, bias_sums = attend_back(*upper_kept[:3], gctx, upper_kept[4], *info)
    lower_gb, lower_gu, lower_ga, gm, gctx, more_sums, more_up_sums = lower(
        place, upper_grads, gm, combined, slope, mixed, vecs, down_w, up_w, out_w, qkv
    )

    keep, send = weight_grad(place, [upper_gb[None], lower_gb[None]], [upper_act, lower_act])
    down_sum = Chain(exchange.reduce(keep, send))
    keep, send = tall_grad(
        place, [upper_gu, tie(lower_gu, keep)], [upper_low, lower_low], [upper_ga, lower_ga], [upper_kept[3], lower_kept[3]]
    )
    up_sum = Chain(exchange.reduce_joined(keep, send, tall, small))
    landed = down_sum.landed
    down_sum.step()
    lower_grads, more_bias_sums = attend_back(*lower_kept[:3], tie(gctx, (keep, landed)), lower_kept[4], *info)
    landed = (up_sum.landed, down_sum.landed)
    up_sum.step()
    down_sum.step()
    joint = exchange.joint_grad(
        place, [upper_grads, tie(lower_grads, landed)], [inputs, flat],
        [bias_sums, more_bias_sums], [sums, more_sums], [up_sums, more_up_sums], small, tall,
    )
    qkv_sum = Chain(exchange.reduce_joint(*joint))
    landed = (up_sum.landed, down_sum.landed)
    up_sum.step()
    ready = exchange.sent
    down_sum.step()
    tokens_grad = input_back(place, tie(lower_grads, (joint[0], landed, ready) if ready is not None else joint[0]), gm, qkv)
    qkv_sum.step(tokens_grad)
    up_sum.step(tokens_grad if exchange.sent is None else (tokens_grad, exchange.sent))
    down_grad = down_sum.finish(tokens_grad)[0]
    up_out = up_sum.finish()[0]
    joint = qkv_sum.finish()
    query_grad, key_grad, value_grad = (joint[i * small : (i + 1) * small] for i in range(3))
    lines = joint[3 * small :]
    piece = [lines[i, :small] for i in range(8)]
    return (
        outputs.reshape(rows_here, row_len, width),
        tokens_grad.reshape(rows_here, row_len, width),
        query_grad,
        piece[QB],
        key_grad,
        value_grad,
        piece[VB],
        up_out[tall:],
        piece[OB],
        piece[G1],
        piece[S1],
        up_out[:tall],
        lines[0, 128 : 128 + tall],
        down_grad,
        piece[DB],
        piece[G2],
        piece[S2],
    )


def solution(mesh):
    rows = P(AXES, None, None)
    flat = P(AXES, None)
    line = P(AXES)
    matrices = (flat, line, flat, flat, line, flat, line, line, line, flat, line, flat, line, line, line)
    exchange = Grid(mesh) if dict(mesh.shape) == {"dp": 4, "fsdp": 8} else Plain(mesh)
    return jax.shard_map(
        partial(body, exchange),
        mesh=mesh,
        in_specs=(rows, rows, flat, flat, line) + matrices,
        out_specs=(rows, rows) + matrices,
        check_vma=False,
    )
```
